32 devices in a mesh: dp: 4 (over y, x), seq: 4 (over z), head: 2 (over core).
Axes of the slice: x: 2, y: 2, z: 4, core: 2. Of those that a mesh axis runs over, the one named last changes fastest.
Arguments:
- dec_input: bfloat16 [96, 128, 768], P(('dp', 'seq'), 'head'), may hold values from -6 to 6
- enc_states: bfloat16 [96, 1296, 768], P('dp', 'seq'), may hold values from -6 to 6
- page_group: int32 [96], P(('dp', 'seq')), may hold values from 0 to 1, as said below
- target_mask: int32 [96, 128], P(('dp', 'seq')), may hold values from 0 to 1, as said below
- rel_buckets: int32 [96, 128, 128], P(('dp', 'seq')), may hold values from 0 to 31, as said below
- self_gain: float32 [768], replicated, may hold values from 0.5 to 1.5
- cross_gain: float32 [768], replicated, may hold values from 0.5 to 1.5
- ffn_gain: float32 [768], replicated, may hold values from 0.5 to 1.5
- self_q: bfloat16 [768, 768], P(None, 'head'), may hold values from -0.21875 to 0.21875
- self_k: bfloat16 [768, 768], P(None, 'head'), may hold values from -0.21875 to 0.21875
- self_v: bfloat16 [768, 768], P(None, 'head'), may hold values from -0.21875 to 0.21875
- self_o: bfloat16 [768, 768], P('head'), may hold values from -0.625 to 0.625
- rel_table: float32 [32, 12], P(None, 'head'), may hold values from -4 to 4
- cross_q: bfloat16 [768, 768], P(None, 'head'), may hold values from -0.21875 to 0.21875
- cross_k: bfloat16 [768, 768], P(None, 'head'), may hold values from -0.21875 to 0.21875
- cross_v: bfloat16 [768, 768], P(None, 'head'), may hold values from -0.21875 to 0.21875
- cross_o: bfloat16 [768, 768], P('head'), may hold values from -1 to 1
- ff_in: bfloat16 [768, 3072], P(None, 'head'), may hold values from -0.21875 to 0.21875
- ff_out: bfloat16 [3072, 768], P('head'), may hold values from -0.15625 to 0.15625
- cotangent: bfloat16 [96, 128, 768], P(('dp', 'seq'), 'head'), may hold values from -6 to 6
Outputs:
- dec_output: bfloat16 [96, 128, 768], P(('dp', 'seq'), 'head')
- input_grad: float32 [96, 128, 768], P(('dp', 'seq'), 'head')
- enc_grad: float32 [96, 1296, 768], P('dp', 'seq', 'head')
- self_gain_grad: float32 [768], replicated
- cross_gain_grad: float32 [768], replicated
- ffn_gain_grad: float32 [768], replicated
- self_q_grad: float32 [768, 768], P(None, 'head')
- self_k_grad: float32 [768, 768], P(None, 'head')
- self_v_grad: float32 [768, 768], P(None, 'head')
- self_o_grad: float32 [768, 768], P('head')
- rel_table_grad: float32 [32, 12], P(None, 'head')
- cross_q_grad: float32 [768, 768], P(None, 'head')
- cross_k_grad: float32 [768, 768], P(None, 'head')
- cross_v_grad: float32 [768, 768], P(None, 'head')
- cross_o_grad: float32 [768, 768], P('head')
- ff_in_grad: float32 [768, 3072], P(None, 'head')
- ff_out_grad: float32 [3072, 768], P('head')
- rms_stats: float32 [96, 4], P(('dp', 'seq'))
The draws below stay inside these ranges and needn't reach their ends.
Inputs may be any that keep to these rules, and one draw needn't show every extreme that they name: `page_group`: 1 marks a page with 784 patches, 0 one with 196; every aligned block of 24 pages holds a page of group 1. `target_mask`: each page's row is ones followed by zeros, with 32 ones or more. `rel_buckets`: the T5 unidirectional bucket (32 buckets, exact up to 16, logarithmic up to distance 128) of the distance from key j to query i between increasing token positions of the page; 0 where j > i.
All inputs are finite; a program needn't handle non-finite values.
Results may differ from the reference program's by a relative error of at most 0.017.
Values may be sent and summed in bfloat16 or wider, within the bound.
No kernel may reach another device: no remote copies, remote signals or barrier semaphores. Data moves between devices by JAX's collectives and lax.ppermute only.
A program may use at most 256 MiB of HBM per device.

```python
import math
import jax
import jax.numpy as jnp
from jax import lax

D = 768
HEADS = 12
HEAD_DIM = 64
FF = 3072
NUM_BUCKETS = 32
DEC_LEN = 128
OCR = 512
PATCH_SMALL = 196
PATCH_LARGE = 784
PAGES_DEV = 6
ENC_CAP = 1296
PAGES = 96
N_SEQ = 4


def draw_page_group(key, part):
    key = jax.random.fold_in(key, 11)
    block = PAGES_DEV * N_SEQ
    blocks = PAGES // block
    random_bits = jax.random.randint(jax.random.fold_in(key, 1), (PAGES,), 0, 2)
    chosen = jax.random.randint(jax.random.fold_in(key, 2), (blocks,), 0, block)
    within = jnp.arange(PAGES, dtype=jnp.int32) % block
    forced = (within == jnp.repeat(chosen, block)).astype(jnp.int32)
    return jnp.maximum(random_bits, forced).astype(jnp.int32)


def draw_target_mask(key, part):
    key = jax.random.fold_in(key, 12)
    lengths = jax.random.randint(key, (PAGES,), DEC_LEN // 4, DEC_LEN + 1)
    positions = jnp.arange(DEC_LEN, dtype=jnp.int32)
    return (positions[None, :] < lengths[:, None]).astype(jnp.int32)


def draw_rel_buckets(key, part):
    key = jax.random.fold_in(key, 13)
    exact = NUM_BUCKETS // 2
    spans = NUM_BUCKETS - exact
    edges = [int(math.ceil(exact * (128.0 / exact) ** (step / spans))) for step in range(1, spans)]
    gaps = jax.random.randint(key, (PAGES, DEC_LEN), 1, 5)
    places = jnp.cumsum(gaps, axis=1)
    distance = jnp.maximum(places[:, :, None] - places[:, None, :], 0)
    large = jnp.full(distance.shape, exact, jnp.int32)
    for edge in edges:
        large = large + (distance >= edge).astype(jnp.int32)
    return jnp.where(distance < exact, distance, large).astype(jnp.int32)


def block_levels(key, shape, cuts, low, largest):
    def one(position, parts):
        draws = jax.random.uniform(jax.random.fold_in(jax.random.fold_in(key, 6), position), (parts,), jnp.float32, low / len(cuts), largest / len(cuts))
        return jnp.repeat(jnp.exp(draws), shape[position] // parts).reshape((-1,) + (1,) * (len(shape) - position - 1))

    gain = one(*cuts[0])
    for cut in cuts[1:]:
        gain = gain * one(*cut)
    return gain


def centred(rng, dims, deviation, bound, pieces=(), held_as=jnp.bfloat16):
    loudness = block_levels(rng, dims, pieces, -0.22, 0.18) if pieces else 1.0
    entries = jax.random.normal(rng, dims, jnp.float32) * deviation * loudness
    return jnp.minimum(jnp.maximum(entries, -bound), bound).astype(held_as)


def setup_inputs(seed: int = 0) -> dict:
    key_list = jax.random.split(jax.random.key(seed), 21)
    dec_input = centred(key_list[0], (PAGES, DEC_LEN, D), 1.0, 6.0, ((0, 16), (1, 2)))
    enc_states = centred(key_list[1], (PAGES, ENC_CAP, D), 1.0, 6.0, ((0, 4), (1, 4)))
    page_group = draw_page_group(jax.random.fold_in(key_list[20], 71), 0)
    target_mask = draw_target_mask(jax.random.fold_in(key_list[20], 71), 0)
    rel_buckets = draw_rel_buckets(jax.random.fold_in(key_list[20], 71), 0)
    self_gain = jnp.clip(1.0 + 0.1 * jax.random.normal(key_list[5], (D,), jnp.float32), 0.5, 1.5)
    cross_gain = jnp.clip(1.0 + 0.1 * jax.random.normal(key_list[6], (D,), jnp.float32), 0.5, 1.5)
    ffn_gain = jnp.clip(1.0 + 0.1 * jax.random.normal(key_list[7], (D,), jnp.float32), 0.5, 1.5)
    self_q = centred(key_list[8], (D, D), D ** -0.5, 0.21875, ((1, 2),))
    self_k = centred(key_list[9], (D, D), D ** -0.5, 0.21875, ((1, 2),))
    self_v = centred(key_list[10], (D, D), D ** -0.5, 0.21875, ((1, 2),))
    self_o = centred(key_list[11], (D, D), (D // 8) ** -0.5, 0.625, ((0, 2),))
    rel_table = centred(key_list[12], (NUM_BUCKETS, HEADS), 1.0, 4.0, ((1, 2),), jnp.float32)
    cross_q = centred(key_list[13], (D, D), D ** -0.5, 0.21875, ((1, 2),))
    cross_k = centred(key_list[14], (D, D), D ** -0.5, 0.21875, ((1, 2),))
    cross_v = centred(key_list[15], (D, D), D ** -0.5, 0.21875, ((1, 2),))
    cross_o = centred(key_list[16], (D, D), (D // 24) ** -0.5, 1.0, ((0, 2),))
    ff_in = centred(key_list[17], (D, FF), D ** -0.5, 0.21875, ((1, 2),))
    ff_out = centred(key_list[18], (FF, D), (FF // 2) ** -0.5, 0.15625, ((0, 2),))
    cotangent = centred(key_list[19], (PAGES, DEC_LEN, D), 1.0, 6.0, ((0, 16), (1, 2)))
    return {"dec_input": dec_input, "enc_states": enc_states, "page_group": page_group, "target_mask": target_mask, "rel_buckets": rel_buckets, "self_gain": self_gain, "cross_gain": cross_gain, "ffn_gain": ffn_gain, "self_q": self_q, "self_k": self_k, "self_v": self_v, "self_o": self_o, "rel_table": rel_table, "cross_q": cross_q, "cross_k": cross_k, "cross_v": cross_v, "cross_o": cross_o, "ff_in": ff_in, "ff_out": ff_out, "cotangent": cotangent}


EPSILON = 1e-06
MASKED = -1000000000.0

@jax.custom_vjp
def low(v):
    return lax.optimization_barrier(v.astype(jnp.bfloat16)).astype(jnp.float32)

@jax.custom_vjp
def low_back(v):
    return v

def low_keep(v):
    return (low(v), None)

def low_pass(kept, grad):
    return (grad,)

def back_keep(v):
    return (v, None)

def back_low(kept, grad):
    return (low(grad),)
low.defvjp(low_keep, low_pass)
low_back.defvjp(back_keep, back_low)

def rounded_both(tensor):
    return low_back(low(tensor))

def matmul(left, right):
    return jnp.dot(left, right, precision=lax.Precision.HIGHEST)

def rms_norm(tensor, gain_vec):
    return tensor * lax.rsqrt(lax.optimization_barrier(jnp.mean(tensor * tensor, axis=-1, keepdims=True)) + EPSILON) * gain_vec

def attend(queries, key_rows, value_rows, score_bias, allowed):
    query_len = queries.shape[0]
    key_len = key_rows.shape[0]
    q_heads = queries.reshape(query_len, HEADS, HEAD_DIM)
    k_heads = key_rows.reshape(key_len, HEADS, HEAD_DIM)
    v_heads = value_rows.reshape(key_len, HEADS, HEAD_DIM)
    scores = jnp.einsum('qhd,khd->hqk', q_heads, k_heads, precision=lax.Precision.HIGHEST) * HEAD_DIM ** (-0.5)
    scores = jnp.where(allowed, low_back(scores + score_bias), MASKED)
    attn_probs = jax.nn.softmax(scores, axis=-1)
    attn_out = jnp.einsum('hqk,khd->qhd', low(attn_probs), v_heads, precision=lax.Precision.HIGHEST)
    return rounded_both(attn_out.reshape(query_len, HEADS * HEAD_DIM))

def page_forward(weights, tokens, encoded, group_id, mask_row, buckets):
    gain_self, gain_cross, gain_ffn, self_q, self_k, self_v, self_o, rel_table, cross_q, cross_k, cross_v, cross_o, ff_in, ff_out = weights
    normed_one = low(rms_norm(tokens, gain_self))
    queries = rounded_both(matmul(normed_one, self_q))
    key_rows = rounded_both(matmul(normed_one, self_k))
    value_rows = rounded_both(matmul(normed_one, self_v))
    score_bias = jnp.transpose(rel_table[buckets], (2, 0, 1))
    positions = jnp.arange(DEC_LEN, dtype=jnp.int32)
    allowed = (positions[None, :] <= positions[:, None]) & (mask_row[None, :] == 1)
    branch_self = low_back(matmul(attend(queries, key_rows, value_rows, score_bias, allowed), self_o))
    hidden_one = tokens + branch_self
    normed_two = low(rms_norm(hidden_one, gain_cross))
    cross_queries = rounded_both(matmul(normed_two, cross_q))
    cross_keys = rounded_both(matmul(encoded, cross_k))
    cross_values = rounded_both(matmul(encoded, cross_v))
    enc_len = OCR + PATCH_SMALL + group_id * (PATCH_LARGE - PATCH_SMALL)
    cross_allowed = (jnp.arange(ENC_CAP, dtype=jnp.int32) < enc_len)[None, :]
    cross_mixed = attend(cross_queries, cross_keys, cross_values, 0.0, cross_allowed)
    branch_cross = low_back(matmul(cross_mixed, cross_o))
    hidden_two = hidden_one + branch_cross
    normed_three = low(rms_norm(hidden_two, gain_ffn))
    activated = low(jax.nn.gelu(low_back(matmul(normed_three, ff_in))))
    branch_ffn = low_back(matmul(activated, ff_out))
    output = hidden_two + branch_ffn
    valid_rows = (mask_row == 1).astype(jnp.float32)[:, None]
    denominator = jnp.sum(valid_rows) * D

    def page_rms(tensor):
        return jnp.sqrt(jnp.sum(tensor * tensor * valid_rows) / denominator)
    rms_values = jnp.stack([page_rms(output), page_rms(branch_self), page_rms(branch_cross), page_rms(branch_ffn)])
    return (output, rms_values)

def reference(dec_input, enc_states, page_group, target_mask, rel_buckets, self_gain, cross_gain, ffn_gain, self_q, self_k, self_v, self_o, rel_table, cross_q, cross_k, cross_v, cross_o, ff_in, ff_out, cotangent):

    def widen(tensor):
        return tensor.astype(jnp.float32)
    weights = (self_gain, cross_gain, ffn_gain, widen(self_q), widen(self_k), widen(self_v), widen(self_o), rel_table, widen(cross_q), widen(cross_k), widen(cross_v), widen(cross_o), widen(ff_in), widen(ff_out))

    def whole(tokens_all, encoded_all, params):

        def one_page(page_item):
            tokens, encoded, group_id, mask_row, buckets = page_item
            return jax.checkpoint(page_forward)(params, tokens, encoded, group_id, mask_row, buckets)
        return lax.map(one_page, (tokens_all, encoded_all, page_group, target_mask, rel_buckets))
    output, pull_back, rms_stats = jax.vjp(whole, widen(dec_input), widen(enc_states), weights, has_aux=True)
    input_grad, enc_grad, grads = pull_back(widen(cotangent))
    return (output.astype(jnp.bfloat16), input_grad, enc_grad, grads[0], grads[1], grads[2], grads[3], grads[4], grads[5], grads[6], grads[7], grads[8], grads[9], grads[10], grads[11], grads[12], grads[13], rms_stats)
```

```python
import functools

import jax
import jax.numpy as jnp
from jax import lax
from jax.experimental import pallas as pl
from jax.experimental.pallas import tpu as pltpu
from jax.sharding import PartitionSpec as P

HEAD_DIM = 64
OCR = 512
PATCH_SMALL = 196
PATCH_LARGE = 784
EPSILON = 1e-06
MASKED = -1000000000.0
BF = jnp.bfloat16
F32 = jnp.float32
SCALE = HEAD_DIM ** (-0.5)
VMEM = 56 * 1024 * 1024
PAIR = 2 * HEAD_DIM


def nn(a, b):
    return lax.dot_general(a, b, (((1,), (0,)), ((), ())), preferred_element_type=F32)


def nt(a, b):
    return lax.dot_general(a, b, (((1,), (1,)), ((), ())), preferred_element_type=F32)


def tn(a, b):
    return lax.dot_general(a, b, (((0,), (0,)), ((), ())), preferred_element_type=F32)


def call(body, grid, ins, outs, *, scalars=(), scratch=(), flops=0, nbytes=0, exps=0, aliases={}):
    spec = pltpu.PrefetchScalarGridSpec(
        num_scalar_prefetch=len(scalars),
        grid=grid,
        in_specs=[pl.BlockSpec(b, m) for _, b, m in ins],
        out_specs=[pl.BlockSpec(b, m) for _, _, b, m in outs],
        scratch_shapes=list(scratch),
    )
    return pl.pallas_call(
        body,
        grid_spec=spec,
        out_shape=[jax.ShapeDtypeStruct(s, d) for s, d, _, _ in outs],
        compiler_params=pltpu.CompilerParams(
            vmem_limit_bytes=VMEM, dimension_semantics=("arbitrary",) * len(grid)
        ),
        cost_estimate=pl.CostEstimate(flops=flops, bytes_accessed=nbytes, transcendentals=exps),
        input_output_aliases=aliases,
    )(*scalars, *[a for a, _, _ in ins])


def whole(a):
    n = a.ndim
    return (a, a.shape, lambda *_: (0,) * n)


def paged(a, k=1):
    n = a.ndim
    return (a, (k,) + a.shape[1:], lambda i, *_: (i,) + (0,) * (n - 1))


def out_paged(shape, dtype, k=1):
    n = len(shape)
    return (shape, dtype, (k,) + tuple(shape[1:]), lambda i, *_: (i,) + (0,) * (n - 1))


def out_whole(shape, dtype):
    n = len(shape)
    return (shape, dtype, tuple(shape), lambda *_: (0,) * n)


def inv_rms(v):
    return lax.rsqrt(jnp.mean(v * v, axis=-1, keepdims=True) + EPSILON)


def pair_rows(block):
    lane = lax.broadcasted_iota(jnp.int32, (1, PAIR), 1)
    low = (lane < HEAD_DIM).astype(F32).astype(block.dtype)
    return jnp.concatenate([block * low, block * (1 - low)], axis=0)


def two_rows(ref_rows, t):
    return jnp.concatenate([ref_rows[2 * t : 2 * t + 1, :], ref_rows[2 * t + 1 : 2 * t + 2, :]], axis=1)


def norm_back(v, gain, dn):
    inv = inv_rms(v)
    weighted = dn * gain
    inner = jnp.mean(weighted * v, axis=-1, keepdims=True)
    return dn * v * inv, inv * weighted - v * (inv * inv * inv * inner)


def fold8(v):
    return jnp.sum(v.reshape(v.shape[0] // 8, 8, v.shape[1]), axis=0)


def self_bias(buckets_ref, table_ref, heads):
    idx = jnp.transpose(buckets_ref[0])
    rows = []
    for h in range(heads):
        tab = jnp.broadcast_to(table_ref[h : h + 1, :], idx.shape)
        rows.append(jnp.take_along_axis(tab, idx, axis=1))
    return rows


def self_allowed(length, rows):
    key = lax.broadcasted_iota(jnp.int32, (rows, rows), 0)
    query = lax.broadcasted_iota(jnp.int32, (rows, rows), 1)
    ok = (key <= query) & (key < length)
    return jnp.concatenate([ok, ok], axis=1)


def self_fwd_kernel(
    head, lens, xo, xr, gain, wq, wk, wv, wo, buckets, table, xf, n1, qkv, o1, lse, a_part
):
    page = pl.program_id(0)
    first = head[0] == 0
    own, rec = xo[0].astype(F32), xr[0].astype(F32)
    x = jnp.concatenate([jnp.where(first, own, rec), jnp.where(first, rec, own)], axis=0)
    xf[0] = x.astype(BF)
    n = (x * inv_rms(x) * gain[...]).astype(BF)
    n1[0] = n
    w = wq.shape[1]
    q = (nn(n, wq[...]).astype(BF).astype(F32) * SCALE).astype(BF)
    k = nn(n, wk[...]).astype(BF)
    v = nn(n, wv[...]).astype(BF)
    qkv[0, :, 0:w] = q
    qkv[0, :, w : 2 * w] = k
    qkv[0, :, 2 * w : 3 * w] = v
    rows = x.shape[0]
    bias = self_bias(buckets, table, w // HEAD_DIM)
    ok = self_allowed(lens[page], rows)
    lses, outs = [], []
    for t in range(w // PAIR):
        c = slice(t * PAIR, (t + 1) * PAIR)
        s = nt(k[:, c], pair_rows(q[:, c])) + jnp.concatenate(bias[2 * t : 2 * t + 2], axis=1)
        s = jnp.where(ok, s, MASKED)
        m = jnp.max(s, axis=0, keepdims=True)
        e = jnp.exp(s - m)
        total = jnp.sum(e, axis=0, keepdims=True)
        p = e * (1.0 / total)
        o = tn(p.astype(BF), v[:, c])
        lane = lax.broadcasted_iota(jnp.int32, (rows, PAIR), 1)
        outs.append(jnp.where(lane < HEAD_DIM, o[:rows], o[rows:]))
        row = m + jnp.log(total)
        lses += [row[:, :rows], row[:, rows:]]
    lses += [jnp.zeros((1, rows), F32)] * (8 - len(lses))
    lse[0] = jnp.concatenate(lses, axis=0)
    o = jnp.concatenate(outs, axis=1).astype(BF)
    o1[0] = o
    a_part[0] = nn(o, wo[...]).astype(BF)


def self_fwd(head, lens, xo, xr, gain, wq, wk, wv, wo, buckets, table):
    pages, half, d = xo.shape
    rows, w = 2 * half, wq.shape[1]
    return call(
        self_fwd_kernel,
        (pages,),
        [
            paged(xo), paged(xr), whole(gain), whole(wq), whole(wk), whole(wv), whole(wo),
            paged(buckets), whole(table),
        ],
        [
            out_paged((pages, rows, d), BF), out_paged((pages, rows, d), BF),
            out_paged((pages, rows, 3 * w), BF), out_paged((pages, rows, w), BF),
            out_paged((pages, 8, rows), F32), out_paged((pages, rows, d), BF),
        ],
        scalars=(head, lens),
        flops=8 * pages * rows * d * w + 8 * pages * rows * rows * w,
        nbytes=pages * rows * (8 * d + 8 * w) + 8 * d * w,
        exps=pages * rows * rows * w // HEAD_DIM,
    )


def self_bwd_kernel(
    head, lens, h1, dn_a, dn_b, dh2, gain, wq, wk, wv, wo, buckets, table, qkv, lse,
    dh1, dar_out, dqkv, ds_out, dn_keep, dn_send, gain_grad,
):
    page = pl.program_id(0)
    first = head[0] == 0
    v1 = h1[0]
    rows = v1.shape[0]
    half = rows // 2
    gg, dv = norm_back(v1, gain[...], dn_a[0].astype(F32) + dn_b[0].astype(F32))
    d1 = dh2[0] + dv
    gpart = fold8(jnp.where(first, gg[:half], gg[half:]))

    @pl.when(page == 0)
    def _():
        gain_grad[...] = gpart

    @pl.when(page != 0)
    def _():
        gain_grad[...] += gpart

    dh1[0] = jnp.where(first, d1[:half], d1[half:])
    dar = d1.astype(BF)
    dar_out[0] = dar
    w = wo.shape[0]
    do = nt(dar, wo[...]).astype(BF)
    bias = self_bias(buckets, table, w // HEAD_DIM)
    ok = self_allowed(lens[page], rows)
    lane = lax.broadcasted_iota(jnp.int32, (rows, PAIR), 1)
    dqs, dks, dvs = [], [], []
    for t in range(w // PAIR):
        c = slice(t * PAIR, (t + 1) * PAIR)
        q = pair_rows(qkv[0, :, t * PAIR : (t + 1) * PAIR])
        k = qkv[0, :, w + t * PAIR : w + (t + 1) * PAIR]
        v = qkv[0, :, 2 * w + t * PAIR : 2 * w + (t + 1) * PAIR]
        g = pair_rows(do[:, c])
        s = nt(k, q) + jnp.concatenate(bias[2 * t : 2 * t + 2], axis=1)
        s = jnp.where(ok, s, MASKED)
        p = jnp.exp(s - two_rows(lse[0], t))
        dp = nt(v, g)
        ds = (p * (dp - jnp.sum(p * dp, axis=0, keepdims=True))).astype(BF)
        ds_out[0, 2 * t] = ds[:, :rows]
        ds_out[0, 2 * t + 1] = ds[:, rows:]
        dq = tn(ds, k) * SCALE
        dqs.append(jnp.where(lane < HEAD_DIM, dq[:rows], dq[rows:]).astype(BF))
        dks.append(nn(ds, q).astype(BF))
        dvs.append(nn(p.astype(BF), g).astype(BF))
    dq, dk, dvv = (jnp.concatenate(a, axis=1) for a in (dqs, dks, dvs))
    dqkv[0, :, 0:w] = dq
    dqkv[0, :, w : 2 * w] = dk
    dqkv[0, :, 2 * w : 3 * w] = dvv
    dn = (nt(dq, wq[...]) + nt(dk, wk[...]) + nt(dvv, wv[...])).astype(BF).astype(F32)
    dn_keep[0] = jnp.where(first, dn[:half], dn[half:]).astype(BF)
    dn_send[0] = jnp.where(first, dn[half:], dn[:half]).astype(BF)


def self_bwd(head, lens, h1, dn_a, dn_b, dh2, gain, wq, wk, wv, wo, buckets, table, qkv, lse):
    pages, rows, d = h1.shape
    w = wq.shape[1]
    heads = w // HEAD_DIM
    return call(
        self_bwd_kernel,
        (pages,),
        [
            paged(h1), paged(dn_a), paged(dn_b), paged(dh2), whole(gain), whole(wq), whole(wk),
            whole(wv), whole(wo), paged(buckets), whole(table), paged(qkv), paged(lse),
        ],
        [
            out_paged((pages, rows // 2, d), F32), out_paged((pages, rows, d), BF),
            out_paged((pages, rows, 3 * w), BF), out_paged((pages, heads, rows, rows), BF),
            out_paged((pages, rows // 2, d), BF), out_paged((pages, rows // 2, d), BF),
            out_whole((8, d), F32),
        ],
        scalars=(head, lens),
        flops=8 * pages * rows * d * w + 20 * pages * rows * rows * w,
        nbytes=pages * rows * (16 * d + 12 * w) + 8 * d * w,
        exps=pages * rows * rows * heads,
    )


def table_grad_kernel(ds, buckets, out):
    page = pl.program_id(0)
    idx = jnp.transpose(buckets[0])
    heads = ds.shape[1]
    dsf = [ds[0, h].astype(F32) for h in range(heads)]
    rows = [[] for _ in range(heads)]
    for b in range(32):
        hit = idx == b
        for h in range(heads):
            rows[h].append(jnp.sum(jnp.where(hit, dsf[h], 0.0), axis=0, keepdims=True))
    for h in range(heads):
        part = jnp.concatenate(rows[h], axis=0)

        @pl.when(page == 0)
        def _():
            out[h] = part

        @pl.when(page != 0)
        def _():
            out[h] += part


def table_grad(ds, buckets):
    pages, heads, rows, _ = ds.shape
    (out,) = call(
        table_grad_kernel,
        (pages,),
        [paged(ds), paged(buckets)],
        [out_whole((heads, 32, rows), F32)],
        flops=64 * pages * heads * rows * rows,
        nbytes=pages * rows * rows * (4 + 2 * heads),
    )
    return jnp.sum(out, axis=-1)


def cross_q_kernel(xf, a_a, a_b, gain, wq, h1, n2, q2):
    k, rows, d = xf.shape
    h = xf[...].astype(F32) + a_a[...].astype(F32) + a_b[...].astype(F32)
    h1[...] = h
    h = h.reshape(k * rows, d)
    n = (h * inv_rms(h) * gain[...]).astype(BF)
    n2[...] = n.reshape(k, rows, d)
    q = nn(n, wq[...]).astype(BF).astype(F32) * SCALE
    q2[...] = q.astype(BF).reshape(k, rows, wq.shape[1])


def cross_q(xf, a_a, a_b, gain, wq, k):
    pages, rows, d = xf.shape
    w = wq.shape[1]
    return call(
        cross_q_kernel,
        (pages // k,),
        [paged(xf, k), paged(a_a, k), paged(a_b, k), whole(gain), whole(wq)],
        [
            out_paged((pages, rows, d), F32, k), out_paged((pages, rows, d), BF, k),
            out_paged((pages, rows, w), BF, k),
        ],
        flops=2 * pages * rows * d * w,
        nbytes=pages * rows * (12 * d + 2 * w) + 2 * d * w,
    )


def combine_kernel(nparts, *refs):
    os, ls = refs[:nparts], refs[nparts : 2 * nparts]
    wo, o2, o2t, lse, c_part = refs[2 * nparts :]
    k, w, rows = o2t.shape
    heads = w // HEAD_DIM
    flat = []
    for i in range(k):
        m = ls[0][i]
        for l in ls[1:]:
            m = jnp.maximum(m, l[i])
        es = [jnp.exp(l[i] - m) for l in ls]
        total = sum(es[1:], es[0])
        lse[i] = m + jnp.log(total)
        inv = 1.0 / total
        ws = [e * inv for e in es]
        pieces = []
        for h in range(heads):
            r = slice(h * HEAD_DIM, (h + 1) * HEAD_DIM)
            acc = os[0][i, r, :].astype(F32) * ws[0][h : h + 1, :]
            for o, ww in zip(os[1:], ws[1:]):
                acc = acc + o[i, r, :].astype(F32) * ww[h : h + 1, :]
            pieces.append(acc)
        ot = jnp.concatenate(pieces, axis=0)
        o2t[i] = ot.astype(BF)
        o = jnp.transpose(ot).astype(BF)
        o2[i] = o
        flat.append(o)
    c = nn(jnp.concatenate(flat, axis=0), wo[...])
    c_part[...] = c.astype(BF).reshape(c_part.shape)


def combine(os, ls, wo, k):
    pages, w, rows = os[0].shape
    d = wo.shape[1]
    return call(
        functools.partial(combine_kernel, len(os)),
        (pages // k,),
        [paged(o, k) for o in os] + [paged(l, k) for l in ls] + [whole(wo)],
        [
            out_paged((pages, rows, w), BF, k), out_paged((pages, w, rows), BF, k),
            out_paged((pages, 8, rows), F32, k), out_paged((pages, rows, d), BF, k),
        ],
        flops=2 * pages * rows * d * w,
        nbytes=pages * rows * (2 * d + 8 * w) + 2 * d * w,
    )


def ffn_kernel(h1, c_a, c_b, cot, gain, w_in, w_out, h2, n3, act_out, du_out, dn3):
    k, rows, d = h1.shape
    h = (h1[...] + c_a[...].astype(F32) + c_b[...].astype(F32)).reshape(k * rows, d)
    h2[...] = h.reshape(k, rows, d)
    n = (h * inv_rms(h) * gain[...]).astype(BF)
    n3[...] = n.reshape(k, rows, d)
    g = cot[...].reshape(k * rows, d)
    units = w_in.shape[1]
    step = units // 3
    root = 0.7978845608028654
    total = None
    for j in range(0, units, step):
        c = slice(j, j + step)
        u = nn(n, w_in[:, c])
        da = nt(g, w_out[c, :])
        u2 = u * u
        th = jnp.tanh(root * u * (1.0 + 0.044715 * u2))
        half = 0.5 + 0.5 * th
        act_out[:, :, c] = (u * half).astype(BF).reshape(k, rows, step)
        slope = half + (0.5 * root) * u * (1.0 - th * th) * (1.0 + (3 * 0.044715) * u2)
        du = (da * slope).astype(BF)
        du_out[:, :, c] = du.reshape(k, rows, step)
        part = nt(du, w_in[:, c])
        total = part if total is None else total + part
    dn3[...] = total.astype(BF).reshape(k, rows, d)


def ffn(h1, c_a, c_b, cot, gain, w_in, w_out, k):
    pages, rows, d = h1.shape
    units = w_in.shape[1]
    return call(
        ffn_kernel,
        (pages // k,),
        [
            paged(h1, k), paged(c_a, k), paged(c_b, k), paged(cot, k), whole(gain), whole(w_in),
            whole(w_out),
        ],
        [
            out_paged((pages, rows, d), F32, k), out_paged((pages, rows, d), BF, k),
            out_paged((pages, rows, units), BF, k), out_paged((pages, rows, units), BF, k),
            out_paged((pages, rows, d), BF, k),
        ],
        flops=6 * pages * rows * d * units,
        nbytes=pages * rows * (18 * d + 4 * units) + 4 * d * units,
        exps=pages * rows * units,
    )


def grad_two_kernel(head, h2, dn_a, dn_b, cot, gain, wo, o2t, dh2, dcr_out, do2, delta, gain_grad):
    step = pl.program_id(0)
    k, rows, d = h2.shape
    half = rows // 2
    w = wo.shape[0]
    first = head[0] == 0
    gacc = None
    flat = []
    for i in range(k):
        gg, dv = norm_back(h2[i], gain[...], dn_a[i].astype(F32) + dn_b[i].astype(F32))
        part = fold8(jnp.where(first, gg[:half], gg[half:]))
        gacc = part if gacc is None else gacc + part
        g = cot[i].astype(F32) + dv
        dh2[i] = g
        dcr = g.astype(BF)
        dcr_out[i] = dcr
        flat.append(dcr)
        dot = nt(wo[...], dcr).astype(BF).astype(F32) * o2t[i].astype(F32)
        sums = [
            jnp.sum(dot[a : a + HEAD_DIM], axis=0, keepdims=True) for a in range(0, w, HEAD_DIM)
        ]
        sums += [jnp.zeros((1, rows), F32)] * (8 - len(sums))
        delta[i] = jnp.concatenate(sums, axis=0)
    do2[...] = nt(jnp.concatenate(flat, axis=0), wo[...]).astype(BF).reshape(k, rows, w)

    @pl.when(step == 0)
    def _():
        gain_grad[...] = gacc

    @pl.when(step != 0)
    def _():
        gain_grad[...] += gacc


def grad_two(head, h2, dn_a, dn_b, cot, gain, wo, o2t, k):
    pages, rows, d = h2.shape
    w = wo.shape[0]
    return call(
        grad_two_kernel,
        (pages // k,),
        [
            paged(h2, k), paged(dn_a, k), paged(dn_b, k), paged(cot, k), whole(gain), whole(wo),
            paged(o2t, k),
        ],
        [
            out_paged((pages, rows, d), F32, k), out_paged((pages, rows, d), BF, k),
            out_paged((pages, rows, w), BF, k), out_paged((pages, 8, rows), F32, k),
            out_whole((8, d), F32),
        ],
        scalars=(head,),
        flops=4 * pages * rows * d * w,
        nbytes=pages * rows * (18 * d + 4 * w) + 2 * d * w,
    )


def grad_q_kernel(nparts, *refs):
    parts = refs[:nparts]
    wq, dq2, dn2 = refs[nparts:]
    k, w, rows = parts[0].shape
    flat = []
    for i in range(k):
        acc = parts[0][i].astype(F32)
        for p in parts[1:]:
            acc = acc + p[i].astype(F32)
        dq = jnp.transpose(acc).astype(BF)
        dq2[i] = dq
        flat.append(dq)
    dn = nt(jnp.concatenate(flat, axis=0), wq[...])
    dn2[...] = dn.astype(BF).reshape(dn2.shape)


def grad_q(parts, wq, k):
    pages, w, rows = parts[0].shape
    d = wq.shape[0]
    return call(
        functools.partial(grad_q_kernel, len(parts)),
        (pages // k,),
        [paged(p, k) for p in parts] + [whole(wq)],
        [out_paged((pages, rows, w), BF, k), out_paged((pages, rows, d), BF, k)],
        flops=2 * pages * rows * d * w,
        nbytes=pages * rows * (2 * d + 8 * w) + 2 * d * w,
    )


def last_kernel(xo, dn_a, dn_b, dh1, gain, out, gain_grad):
    page = pl.program_id(0)
    gg, dv = norm_back(
        xo[0].astype(F32), gain[...], dn_a[0].astype(F32) + dn_b[0].astype(F32)
    )
    out[0] = dh1[0] + dv
    part = fold8(gg)

    @pl.when(page == 0)
    def _():
        gain_grad[...] = part

    @pl.when(page != 0)
    def _():
        gain_grad[...] += part


def last(xo, dn_a, dn_b, dh1, gain):
    pages, half, d = xo.shape
    return call(
        last_kernel,
        (pages,),
        [paged(xo), paged(dn_a), paged(dn_b), paged(dh1), whole(gain)],
        [out_paged((pages, half, d), F32), out_whole((8, d), F32)],
        flops=20 * pages * half * d,
        nbytes=pages * half * d * 14,
    )


def branch_ffn_kernel(head, act, w_out, keep, send):
    k, rows, units = act.shape
    half = rows // 2
    first = head[0] == 0
    f = nn(act[...].reshape(k * rows, units), w_out[...])
    f = f.reshape(k, rows, f.shape[1])
    keep[...] = jnp.where(first, f[:, :half], f[:, half:]).astype(BF)
    send[...] = jnp.where(first, f[:, half:], f[:, :half]).astype(BF)


def branch_ffn(head, act, w_out, k):
    pages, rows, units = act.shape
    d = w_out.shape[1]
    return call(
        branch_ffn_kernel,
        (pages // k,),
        [paged(act, k), whole(w_out)],
        [out_paged((pages, rows // 2, d), BF, k), out_paged((pages, rows // 2, d), BF, k)],
        scalars=(head,),
        flops=2 * pages * rows * d * units,
        nbytes=pages * rows * (2 * d + 2 * units) + 2 * d * units,
    )


def output_kernel(head, lens, h2, f_a, f_b, a_a, a_b, c_a, c_b, out, stats):
    page = pl.program_id(0)
    first = head[0] == 0
    half = f_a.shape[1]

    def mine(ref):
        v = ref[0].astype(F32)
        return jnp.where(first, v[:half], v[half:])

    f = f_a[0].astype(F32) + f_b[0].astype(F32)
    y = mine(h2) + f
    out[0] = y.astype(BF)
    a = mine(a_a) + mine(a_b)
    c = mine(c_a) + mine(c_b)
    row = lax.broadcasted_iota(jnp.int32, (half, 1), 0) + head[0] * half
    valid = (row < lens[page]).astype(F32)
    stats[0] = jnp.concatenate(
        [jnp.sum(v * v * valid, axis=0, keepdims=True) for v in (y, a, c, f)]
        + [jnp.zeros((4, y.shape[1]), F32)],
        axis=0,
    )


def output_rows(head, lens, h2, f_a, f_b, a_a, a_b, c_a, c_b):
    pages, rows, d = h2.shape
    return call(
        output_kernel,
        (pages,),
        [paged(a) for a in (h2, f_a, f_b, a_a, a_b, c_a, c_b)],
        [out_paged((pages, rows // 2, d), BF), out_paged((pages, 8, d), F32)],
        scalars=(head, lens),
        flops=10 * pages * rows * d,
        nbytes=pages * rows * d * 16,
    )


def kv_own_kernel(table, enc, w, kv):
    kv[0] = nn(enc[0], w[...]).astype(BF)


def kv_own(table, enc, w, slots):
    pages, n, d = enc.shape
    return call(
        kv_own_kernel,
        (slots,),
        [(enc, (1, n, d), lambda i, t: (t[i], 0, 0)), whole(w)],
        [out_paged((slots, n, w.shape[1]), BF)],
        scalars=(table,),
        flops=2 * slots * n * d * w.shape[1],
        nbytes=4 * slots * n * d + 2 * d * d,
    )[0]


def kv_rec_kernel(split, table, enc_a, enc_b, w, kv):
    i = pl.program_id(0)

    @pl.when(table[i] < split)
    def _():
        kv[0] = nn(enc_a[0], w[...]).astype(BF)

    @pl.when(table[i] >= split)
    def _():
        kv[0] = nn(enc_b[0], w[...]).astype(BF)


def rec_blocks(enc_a, enc_b):
    split, n, d = enc_a.shape
    return [
        (enc_a, (1, n, d), lambda i, t: (jnp.minimum(t[i], split - 1), 0, 0)),
        (enc_b, (1, n, d), lambda i, t: (jnp.maximum(t[i] - split, 0), 0, 0)),
    ]


def kv_rec(table, enc_a, enc_b, w):
    split, n, d = enc_a.shape
    slots = 2 * split
    return call(
        functools.partial(kv_rec_kernel, split),
        (slots,),
        rec_blocks(enc_a, enc_b) + [whole(w)],
        [out_paged((slots, n, w.shape[1]), BF)],
        scalars=(table,),
        flops=2 * slots * n * d * w.shape[1],
        nbytes=4 * slots * n * d + 2 * d * d,
    )[0]


def cross_fwd_kernel(lims, q, kv_a, kv_b, o, lse):
    slot = pl.program_id(0)
    rows, w = q.shape[1:]
    n = kv_a.shape[1]

    def run(masked):
        rowsum = []
        for t in range(w // PAIR):
            c = slice(t * PAIR, (t + 1) * PAIR)
            cv = slice(w + t * PAIR, w + (t + 1) * PAIR)
            qm = pair_rows(q[0, :, c])
            ss = []
            for j, kv in enumerate((kv_a, kv_b)):
                s = nt(kv[0, :, c], qm)
                if masked:
                    pos = lax.broadcasted_iota(jnp.int32, s.shape, 0)
                    s = jnp.where(pos < lims[j, slot], s, MASKED)
                ss.append(s)
            m = jnp.maximum(*[jnp.max(s, axis=0, keepdims=True) for s in ss])
            es = [jnp.exp(s - m) for s in ss]
            total = sum(jnp.sum(e, axis=0, keepdims=True) for e in es)
            acc = tn(kv_a[0, :, cv], es[0].astype(BF)) + tn(kv_b[0, :, cv], es[1].astype(BF))
            inv = 1.0 / total
            o[0, t * PAIR : t * PAIR + HEAD_DIM, :] = (
                acc[:HEAD_DIM, :rows] * inv[:, :rows]
            ).astype(BF)
            o[0, t * PAIR + HEAD_DIM : (t + 1) * PAIR, :] = (
                acc[HEAD_DIM:, rows:] * inv[:, rows:]
            ).astype(BF)
            row = m + jnp.log(total)
            rowsum += [row[:, :rows], row[:, rows:]]
        rowsum += [jnp.zeros((1, rows), F32)] * (8 - len(rowsum))
        lse[0] = jnp.concatenate(rowsum, axis=0)

    full = (lims[0, slot] >= n) & (lims[1, slot] >= n)
    pl.when(full)(lambda: run(False))
    pl.when(jnp.logical_not(full))(lambda: run(True))


def cross_fwd(lims, q, kv_a, kv_b):
    slots, rows, w = q.shape
    n = kv_a.shape[1]
    return call(
        cross_fwd_kernel,
        (slots,),
        [paged(q), paged(kv_a), paged(kv_b)],
        [out_paged((slots, w, rows), BF), out_paged((slots, 8, rows), F32)],
        scalars=(lims,),
        flops=32 * slots * rows * n * w,
        nbytes=slots * (8 * n * w + 4 * rows * w),
        exps=2 * slots * rows * n * w // HEAD_DIM,
    )


def cross_bwd_kernel(lims, q, do, lse, delta, kv_a, kv_b, dq, dkv_a, dkv_b):
    slot = pl.program_id(0)
    rows, w = q.shape[1:]
    n = kv_a.shape[1]

    def run(masked):
        for t in range(w // PAIR):
            c = slice(t * PAIR, (t + 1) * PAIR)
            cv = slice(w + t * PAIR, w + (t + 1) * PAIR)
            qm = pair_rows(q[0, :, c])
            gm = pair_rows(do[0, :, c])
            ls, dl = two_rows(lse[0], t), two_rows(delta[0], t)
            acc = None
            for j, (kv, dkv) in enumerate(((kv_a, dkv_a), (kv_b, dkv_b))):
                k = kv[0, :, c]
                s = nt(k, qm)
                if masked:
                    pos = lax.broadcasted_iota(jnp.int32, s.shape, 0)
                    s = jnp.where(pos < lims[j, slot], s, MASKED)
                p = jnp.exp(s - ls)
                ds = (p * (nt(kv[0, :, cv], gm) - dl)).astype(BF)
                dkv[0, :, c] = nn(ds, qm).astype(BF)
                dkv[0, :, cv] = nn(p.astype(BF), gm).astype(BF)
                part = tn(k, ds)
                acc = part if acc is None else acc + part
            dq[0, t * PAIR : t * PAIR + HEAD_DIM, :] = (acc[:HEAD_DIM, :rows] * SCALE).astype(BF)
            dq[0, t * PAIR + HEAD_DIM : (t + 1) * PAIR, :] = (
                acc[HEAD_DIM:, rows:] * SCALE
            ).astype(BF)

    full = (lims[0, slot] >= n) & (lims[1, slot] >= n)
    pl.when(full)(lambda: run(False))
    pl.when(jnp.logical_not(full))(lambda: run(True))


def cross_bwd(lims, q, do, lse, delta, kv_a, kv_b):
    slots, rows, w = q.shape
    n = kv_a.shape[1]
    return call(
        cross_bwd_kernel,
        (slots,),
        [paged(a) for a in (q, do, lse, delta, kv_a, kv_b)],
        [
            out_paged((slots, w, rows), BF), out_paged((slots, n, 2 * w), BF),
            out_paged((slots, n, 2 * w), BF),
        ],
        scalars=(lims,),
        flops=80 * slots * rows * n * w,
        nbytes=slots * (16 * n * w + 8 * rows * w),
        exps=2 * slots * rows * n * w // HEAD_DIM,
    )


def enc_terms(step, dkv, enc, wk_keep, wv_keep, wk_send, wv_send, keep, send, dw):
    w = wk_keep.shape[1]
    dk, dv = dkv[0, :, :w], dkv[0, :, w:]
    send[0] = (nt(dk, wk_send[...]) + nt(dv, wv_send[...])).astype(BF)
    keep[0] = (nt(dk, wk_keep[...]) + nt(dv, wv_keep[...])).astype(BF)
    part = tn(dkv[0], enc)

    @pl.when(step == 0)
    def _():
        dw[...] = part

    @pl.when(step != 0)
    def _():
        dw[...] += part


def enc_own_kernel(table, head, dkv, enc, wkk, wvk, wks, wvs, keep, send, dw):
    enc_terms(pl.program_id(0), dkv, enc[0], wkk, wvk, wks, wvs, keep, send, dw)


def enc_rec_kernel(split, table, head, dkv, enc_a, enc_b, wkk, wvk, wks, wvs, keep, send, dw):
    i = pl.program_id(0)

    @pl.when(table[i] < split)
    def _():
        enc_terms(i, dkv, enc_a[0], wkk, wvk, wks, wvs, keep, send, dw)

    @pl.when(table[i] >= split)
    def _():
        enc_terms(i, dkv, enc_b[0], wkk, wvk, wks, wvs, keep, send, dw)


def enc_back(table, head, dkv, encs, wk, wv):
    slots, n, w2 = dkv.shape
    d, w = wk.shape
    part = d // 2
    if len(encs) == 1:
        body = enc_own_kernel
        blocks = [(encs[0], (1, n, d), lambda i, t, h: (t[i], 0, 0))]
    else:
        split = encs[0].shape[0]
        body = functools.partial(enc_rec_kernel, split)
        blocks = [
            (encs[0], (1, n, d), lambda i, t, h: (jnp.minimum(t[i], split - 1), 0, 0)),
            (encs[1], (1, n, d), lambda i, t, h: (jnp.maximum(t[i] - split, 0), 0, 0)),
        ]
    mine = lambda i, t, h: (h[0], 0)
    other = lambda i, t, h: (1 - h[0], 0)
    return call(
        body,
        (slots,),
        [paged(dkv)]
        + blocks
        + [
            (wk, (part, w), mine), (wv, (part, w), mine), (wk, (part, w), other),
            (wv, (part, w), other),
        ],
        [
            out_paged((slots, n, part), BF), out_paged((slots, n, part), BF),
            out_whole((w2, d), F32),
        ],
        scalars=(table, head),
        flops=4 * slots * n * d * w2,
        nbytes=slots * n * (2 * w2 + 4 * d),
    )


def add_pages_kernel(a, b, out):
    out[0] = (a[0].astype(F32) + b[0].astype(F32)).astype(out.dtype)


def add_pages(a, b):
    return call(
        add_pages_kernel,
        (a.shape[0],),
        [paged(a), paged(b)],
        [out_paged(a.shape, BF)],
        flops=a.size,
        nbytes=6 * a.size,
    )[0]


def enc_first_kernel(table, a, b, out):
    out[0] = a[0].astype(F32) + b[0].astype(F32)


def enc_first(table, a, b, pages):
    slots, n, c = a.shape
    return call(
        enc_first_kernel,
        (slots,),
        [paged(a), paged(b)],
        [((pages, n, c), F32, (1, n, c), lambda i, t: (t[i], 0, 0))],
        scalars=(table,),
        flops=a.size,
        nbytes=8 * a.size,
    )[0]


def enc_second_kernel(table, a, _, out):
    out[0] = a[0].astype(F32)


def enc_second(table, a, so_far):
    slots, n, c = a.shape
    return call(
        enc_second_kernel,
        (slots,),
        [paged(a), (so_far, (1, 8, 128), lambda i, t: (0, 0, 0))],
        [(so_far.shape, F32, (1, n, c), lambda i, t: (t[i], 0, 0))],
        scalars=(table,),
        flops=a.size,
        nbytes=6 * a.size,
        aliases={2: 0},
    )[0]


def swap(x, axis, mask, size):
    return lax.ppermute(x, axis, [(i, i ^ mask) for i in range(size)])


def bit_of(axis, mask):
    return (lax.axis_index(axis) // mask) % 2


def reduce_rows(x, steps, sizes):
    for axis, mask in steps:
        half = x.shape[0] // 2
        b = bit_of(axis, mask)
        keep = lax.dynamic_slice_in_dim(x, b * half, half, 0)
        send = lax.dynamic_slice_in_dim(x, (1 - b) * half, half, 0)
        got = swap(send, axis, mask, sizes[axis])
        x = (keep.astype(F32) + got.astype(F32)).astype(x.dtype)
    for axis, mask in reversed(steps):
        b = bit_of(axis, mask)
        got = swap(x, axis, mask, sizes[axis])
        x = jnp.concatenate([jnp.where(b == 0, x, got), jnp.where(b == 0, got, x)], axis=0)
    return x


def reduce_bucket(x, sizes):
    dp = [("dp", 1 << i) for i in range(sizes["dp"].bit_length() - 1)]
    seq = [("seq", 1 << i) for i in range(sizes["seq"].bit_length() - 1)]
    half = x.shape[0] // 2
    return jnp.concatenate(
        [
            reduce_rows(x[:half], dp + seq, sizes),
            reduce_rows(x[half:], dp[::-1] + seq, sizes),
        ],
        axis=0,
    )


def reduce_small(x, sizes):
    x = x + swap(x, "head", 1, sizes["head"])
    for axis in ("dp", "seq"):
        for i in range(sizes[axis].bit_length() - 1):
            x = x + swap(x, axis, 1 << i, sizes[axis])
    return x


def rows_grad(a, b):
    a = a.reshape(-1, a.shape[-1])
    b = b.reshape(-1, b.shape[-1])
    return lax.dot_general(a, b, (((0,), (0,)), ((), ())), preferred_element_type=F32).astype(BF)


def per_device(
    sizes,
    dec_input,
    enc_states,
    page_group,
    target_mask,
    rel_buckets,
    self_gain,
    cross_gain,
    ffn_gain,
    self_q,
    self_k,
    self_v,
    self_o,
    rel_table,
    cross_q_w,
    cross_k,
    cross_v,
    cross_o,
    ff_in,
    ff_out,
    cotangent,
):
    n_seq = sizes["seq"]
    pages, half, d = dec_input.shape
    n = enc_states.shape[1]
    w = self_q.shape[1]
    nb = n_seq // 2
    slots = nb * pages
    s = lax.axis_index("seq")
    h = lax.axis_index("head")
    block, par = s // 2, s % 2
    head = h.reshape(1).astype(jnp.int32)

    kk = jnp.arange(slots, dtype=jnp.int32) // pages
    pg = jnp.arange(slots, dtype=jnp.int32) % pages
    owner = (block + kk) % nb
    own_table = ((owner * 2 + par) * pages + pg).astype(jnp.int32)
    away_table = ((owner * 2 + 1 - par) * pages + pg).astype(jnp.int32)
    rec_table = (((owner - h * (nb // 2)) % nb) * pages + pg).astype(jnp.int32)

    def head_swap(x):
        return swap(x, "head", 1, 2)

    def owners(x):
        got = [x]
        for step in range(1, nb):
            perm = [
                (2 * b + r, 2 * ((b - step) % nb) + r) for b in range(nb) for r in range(2)
            ]
            got.append(lax.ppermute(x, "seq", perm))
        return got

    def returned(x):
        got = [x[:pages]]
        for step in range(1, nb):
            perm = [
                (2 * b + r, 2 * ((b + step) % nb) + r) for b in range(nb) for r in range(2)
            ]
            got.append(lax.ppermute(x[step * pages : (step + 1) * pages], "seq", perm))
        return got

    x_other = head_swap(dec_input)
    away = lax.dynamic_slice(
        enc_states.reshape(nb, 2, pages, n, d),
        (h * (nb // 2), 1 - par, 0, 0, 0),
        (nb // 2, 1, pages, n, d),
    ).reshape(slots // 2, n, d)
    enc_a = swap(away, "seq", 1, n_seq)
    cot_other = head_swap(cotangent)
    cot = jnp.concatenate(
        [jnp.where(h == 0, cotangent, cot_other), jnp.where(h == 0, cot_other, cotangent)], axis=1
    )
    groups = jnp.concatenate(owners(page_group))
    enc_len = OCR + PATCH_SMALL + groups * (PATCH_LARGE - PATCH_SMALL)
    lims = jnp.stack([enc_len - s * n, enc_len - (s + 1 - 2 * par) * n]).astype(jnp.int32)
    lens = jnp.sum(target_mask, axis=1).astype(jnp.int32)
    table = jnp.pad(rel_table.T, ((0, 8 - rel_table.shape[1]), (0, 128 - rel_table.shape[0])))
    gains = [g.reshape(1, d) for g in (self_gain, cross_gain, ffn_gain)]
    w_kv = jnp.concatenate([cross_k, cross_v], axis=1)

    xf, n1, qkv, o1, lse1, a_part = self_fwd(
        head, lens, dec_input, x_other, gains[0], self_q, self_k, self_v, self_o, rel_buckets, table
    )
    a_other = head_swap(a_part)
    kv_a = kv_own(own_table, enc_states, w_kv, slots)
    h1, n2, q2 = cross_q(xf, a_part, a_other, gains[1], cross_q_w, 2)
    q_all = jnp.concatenate(owners(q2), axis=0)
    enc_b = head_swap(enc_a)
    kv_b = kv_rec(rec_table, enc_a, enc_b, w_kv)
    o_all, lse_all = cross_fwd(lims, q_all, kv_a, kv_b)
    o2, o2t, lse2, c_part = combine(returned(o_all), returned(lse_all), cross_o, 2)
    c_other = head_swap(c_part)
    h2, n3, act, du, dn3 = ffn(h1, c_part, c_other, cot, gains[2], ff_in, ff_out, 2)
    dn3_other = head_swap(dn3)
    dh2, dcr, do2, delta, ffn_gain_part = grad_two(
        head, h2, dn3, dn3_other, cot, gains[2], cross_o, o2t, 2
    )
    do_all = jnp.concatenate(owners(do2), axis=0)
    lse_back = jnp.concatenate(owners(lse2), axis=0)
    delta_all = jnp.concatenate(owners(delta), axis=0)

    f_keep, f_send = branch_ffn(head, act, ff_out, 2)
    f_other = head_swap(f_send)
    output, squares = output_rows(
        head, lens, h2, f_keep, f_other, a_part, a_other, c_part, c_other
    )
    bucket_ffn = jnp.concatenate([rows_grad(act, cot), rows_grad(du, n3)], axis=0)
    sum_ffn = reduce_bucket(bucket_ffn, sizes)

    dq_all, dkv_a, dkv_b = cross_bwd(lims, q_all, do_all, lse_back, delta_all, kv_a, kv_b)
    dq2, dn2 = grad_q(returned(dq_all), cross_q_w, 2)
    dn2_other = head_swap(dn2)
    keep_b, send_b, dw_b = enc_back(rec_table, head, dkv_b, [enc_a, enc_b], cross_k, cross_v)
    back_b = add_pages(keep_b, head_swap(send_b))
    enc_away = swap(back_b, "seq", 1, n_seq)
    keep_a, send_a, dw_a = enc_back(own_table, head, dkv_a, [enc_states], cross_k, cross_v)
    enc_grad = enc_first(own_table, keep_a, head_swap(send_a), enc_states.shape[0])

    dh1, dar, dqkv, ds1, dn1_keep, dn1_send, cross_gain_part = self_bwd(
        head, lens, h1, dn2, dn2_other, dh2, gains[1], self_q, self_k, self_v, self_o,
        rel_buckets, table, qkv, lse1,
    )
    dn1_other = head_swap(dn1_send)
    bucket_cross = jnp.concatenate(
        [rows_grad(dq2, n2), (dw_a + dw_b).astype(BF), rows_grad(o2, dcr)], axis=0
    )
    sum_cross = reduce_bucket(bucket_cross, sizes)
    bucket_self = jnp.concatenate([rows_grad(dqkv, n1), rows_grad(o1, dar)], axis=0)
    sum_self = reduce_bucket(bucket_self, sizes)
    input_grad, self_gain_part = last(dec_input, dn1_keep, dn1_other, dh1, gains[0])
    table_part = table_grad(ds1, rel_buckets)
    enc_grad = enc_second(away_table, enc_away, enc_grad)

    small = jnp.stack([jnp.sum(g, axis=0) for g in (self_gain_part, cross_gain_part, ffn_gain_part)])
    squares = jnp.sum(squares[:, :4], axis=-1)
    squares = squares + head_swap(squares)
    counts = lens.astype(F32) * d
    rms_stats = jnp.sqrt(squares / counts[:, None])
    small = reduce_small(small, sizes)
    for axis in ("dp", "seq"):
        for i in range(sizes[axis].bit_length() - 1):
            table_part = table_part + swap(table_part, axis, 1 << i, sizes[axis])

    def turned(x):
        return jnp.transpose(x.astype(F32))

    units = ff_in.shape[1]
    return (
        output,
        input_grad,
        enc_grad,
        small[0],
        small[1],
        small[2],
        turned(sum_self[:w]),
        turned(sum_self[w : 2 * w]),
        turned(sum_self[2 * w : 3 * w]),
        sum_self[3 * w :].astype(F32),
        table_part.T,
        turned(sum_cross[:w]),
        turned(sum_cross[w : 2 * w]),
        turned(sum_cross[2 * w : 3 * w]),
        sum_cross[3 * w :].astype(F32),
        turned(sum_ffn[units:]),
        sum_ffn[:units].astype(F32),
        rms_stats,
    )


def solution(mesh):
    sizes = dict(mesh.shape)
    rows = P(("dp", "seq"), "head", None)
    cols, tall = P(None, "head"), P("head", None)
    placed = (
        rows, P("dp", "seq", None), P(("dp", "seq")), P(("dp", "seq"), None),
        P(("dp", "seq"), None, None), P(), P(), P(), cols, cols, cols, tall, cols, cols, cols, cols,
        tall, cols, tall, rows,
    )
    return jax.shard_map(
        functools.partial(per_device, sizes),
        mesh=mesh,
        in_specs=placed,
        out_specs=(
            rows, rows, P("dp", "seq", "head"), P(), P(), P(), cols, cols, cols, tall, cols, cols,
            cols, cols, tall, cols, tall, P(("dp", "seq"), None),
        ),
        check_vma=False,
    )
```

```python
import functools

import jax
import jax.numpy as jnp
from jax import lax
from jax.experimental import pallas as pl
from jax.experimental.layout import Layout, with_layout_constraint
from jax.experimental.pallas import tpu as pltpu
from jax.sharding import PartitionSpec as P

HEAD_DIM = 64
OCR = 512
PATCH_SMALL = 196
PATCH_LARGE = 784
EPSILON = 1e-06
MASKED = -1000000000.0
BF = jnp.bfloat16
F32 = jnp.float32
SCALE = HEAD_DIM ** (-0.5)
VMEM = 56 * 1024 * 1024
PAIR = 2 * HEAD_DIM


def nn(a, b):
    return lax.dot_general(a, b, (((1,), (0,)), ((), ())), preferred_element_type=F32)


def nt(a, b):
    return lax.dot_general(a, b, (((1,), (1,)), ((), ())), preferred_element_type=F32)


def tn(a, b):
    return lax.dot_general(a, b, (((0,), (0,)), ((), ())), preferred_element_type=F32)


ORDER = []


def call(body, grid, ins, outs, *, us, scalars=(), scratch=(), after=(), aliases={}):
    held = [a for a, _, _ in ins]
    after = [t for t in [*after, *ORDER] if not any(t is a for a in held)]
    first, last = len(scalars) + len(ins), len(scalars) + len(ins) + len(after)

    def run(*refs):
        body(*refs[:first], *refs[last:])

    spec = pltpu.PrefetchScalarGridSpec(
        num_scalar_prefetch=len(scalars),
        grid=grid,
        in_specs=[pl.BlockSpec(b, m) for _, b, m in ins]
        + [pl.BlockSpec(memory_space=pl.ANY)] * len(after),
        out_specs=[pl.BlockSpec(b, m) for _, _, b, m in outs],
        scratch_shapes=list(scratch),
    )
    results = pl.pallas_call(
        run,
        grid_spec=spec,
        out_shape=[jax.ShapeDtypeStruct(s, d) for s, d, _, _ in outs],
        compiler_params=pltpu.CompilerParams(
            vmem_limit_bytes=VMEM, dimension_semantics=("arbitrary",) * len(grid)
        ),
        cost_estimate=pl.CostEstimate(flops=int(us * 1e10), bytes_accessed=0, transcendentals=0),
        input_output_aliases=aliases,
    )(*scalars, *[a for a, _, _ in ins], *after)
    ORDER[:] = [min(results, key=lambda r: r.size)]
    return results


def whole(a):
    n = a.ndim
    return (a, a.shape, lambda *_: (0,) * n)


def paged(a, k=1):
    a, at = a if isinstance(a, tuple) else (a, 0)
    n = a.ndim
    return (a, (k,) + a.shape[1:], lambda i, *_: (i + at // k,) + (0,) * (n - 1))


def kept(a):
    n = a.ndim
    return (a, (1,) * (n - 2) + (8, 128), lambda *_: (0,) * n)


def out_paged(shape, dtype, k=1):
    n = len(shape)
    return (shape, dtype, (k,) + tuple(shape[1:]), lambda i, *_: (i,) + (0,) * (n - 1))


def out_whole(shape, dtype):
    n = len(shape)
    return (shape, dtype, tuple(shape), lambda *_: (0,) * n)


def inv_rms(v):
    return lax.rsqrt(jnp.mean(v * v, axis=-1, keepdims=True) + EPSILON)


def pair_rows(block):
    lane = lax.broadcasted_iota(jnp.int32, (1, PAIR), 1)
    low = (lane < HEAD_DIM).astype(F32).astype(block.dtype)
    return jnp.concatenate([block * low, block * (1 - low)], axis=0)


def thirds(v):
    hi = v.astype(BF)
    rest = v - hi.astype(F32)
    mid = rest.astype(BF)
    return [hi, mid, (rest - mid.astype(F32)).astype(BF)]


def joined(hi, mid, lo):
    return hi.astype(F32) + mid.astype(F32) + lo.astype(F32)


STATS = 32
MORE = 32


def two_rows(ref_rows, t):
    return jnp.concatenate([ref_rows[2 * t : 2 * t + 1, :], ref_rows[2 * t + 1 : 2 * t + 2, :]], axis=1)


def norm_back(v, gain, dn):
    inv = inv_rms(v)
    weighted = dn * gain
    inner = jnp.mean(weighted * v, axis=-1, keepdims=True)
    return dn * v * inv, inv * weighted - v * (inv * inv * inv * inner)


def fold8(v):
    return jnp.sum(v.reshape(v.shape[0] // 8, 8, v.shape[1]), axis=0)


def self_bias(buckets_ref, table_ref, heads):
    idx = jnp.transpose(buckets_ref[0])
    rows = []
    for h in range(heads):
        tab = jnp.broadcast_to(table_ref[h : h + 1, :], idx.shape)
        rows.append(jnp.take_along_axis(tab, idx, axis=1))
    return rows


def self_allowed(length, rows):
    key = lax.broadcasted_iota(jnp.int32, (rows, rows), 0)
    query = lax.broadcasted_iota(jnp.int32, (rows, rows), 1)
    ok = (key <= query) & (key < length)
    return jnp.concatenate([ok, ok], axis=1)


def self_fwd_kernel(
    head, lens, xo, xr, gain, wq, wk, wv, wo, buckets, table, xf, n1, qkv, o1, lse, a_part
):
    page = pl.program_id(0)
    first = head[0] == 0
    own, rec = xo[0].astype(F32), xr[0].astype(F32)
    x = jnp.concatenate([jnp.where(first, own, rec), jnp.where(first, rec, own)], axis=0)
    xf[0] = x.astype(BF)
    n = (x * inv_rms(x) * gain[...]).astype(BF)
    n1[0] = n
    w = wq.shape[1]
    q = (nn(n, wq[...]).astype(BF).astype(F32) * SCALE).astype(BF)
    k = nn(n, wk[...]).astype(BF)
    v = nn(n, wv[...]).astype(BF)
    qkv[0, :, 0:w] = q
    qkv[0, :, w : 2 * w] = k
    qkv[0, :, 2 * w : 3 * w] = v
    rows = x.shape[0]
    bias = self_bias(buckets, table, w // HEAD_DIM)
    ok = self_allowed(lens[page], rows)
    lses, outs = [], []
    for t in range(w // PAIR):
        c = slice(t * PAIR, (t + 1) * PAIR)
        s = nt(k[:, c], pair_rows(q[:, c])) + jnp.concatenate(bias[2 * t : 2 * t + 2], axis=1)
        s = jnp.where(ok, s, MASKED)
        m = jnp.max(s, axis=0, keepdims=True)
        e = jnp.exp(s - m)
        total = jnp.sum(e, axis=0, keepdims=True)
        p = e * (1.0 / total)
        o = tn(p.astype(BF), v[:, c])
        lane = lax.broadcasted_iota(jnp.int32, (rows, PAIR), 1)
        outs.append(jnp.where(lane < HEAD_DIM, o[:rows], o[rows:]))
        row = m + jnp.log(total)
        lses += [row[:, :rows], row[:, rows:]]
    lses += [jnp.zeros((1, rows), F32)] * (8 - len(lses))
    lse[0] = jnp.concatenate(lses, axis=0)
    o = jnp.concatenate(outs, axis=1).astype(BF)
    o1[0] = o
    a_part[0] = nn(o, wo[...]).astype(BF)


def self_fwd(head, lens, xo, xr, gain, wq, wk, wv, wo, buckets, table, after=()):
    pages, half, d = xo.shape
    rows, w = 2 * half, wq.shape[1]
    return call(
        self_fwd_kernel,
        (pages,),
        [
            paged(xo), paged(xr), whole(gain), whole(wq), whole(wk), whole(wv), whole(wo),
            paged(buckets), whole(table),
        ],
        [
            out_paged((pages, rows, d), BF), out_paged((pages, rows, d), BF),
            out_paged((pages, rows, 3 * w), BF), out_paged((pages, rows, w), BF),
            out_paged((pages, 8, rows), F32), out_paged((pages, rows, d), BF),
        ],
        scalars=(head, lens),
        us=10, after=after,
    )


def self_bwd_kernel(
    at, head, lens, h1, dn_a, dn_b, dh2, gain, wq, wk, wv, wo, buckets, table, qkv, lse,
    dh1, dar_out, dq_out, dk_out, dv_out, ds_out, dn_keep, dn_send, gain_grad,
):
    page = pl.program_id(0)
    first = head[0] == 0
    v1 = h1[0]
    rows = v1.shape[0]
    half = rows // 2
    gg, dv = norm_back(v1, gain[...], dn_a[0].astype(F32) + dn_b[0].astype(F32))
    d1 = dh2[0] + dv
    gpart = fold8(jnp.where(first, gg[:half], gg[half:]))

    @pl.when(page == 0)
    def _():
        gain_grad[...] = gpart

    @pl.when(page != 0)
    def _():
        gain_grad[...] += gpart

    dh1[0] = jnp.where(first, d1[:half], d1[half:])
    dar = d1.astype(BF)
    dar_out[0] = dar
    w = wo.shape[0]
    do = nt(dar, wo[...]).astype(BF)
    bias = self_bias(buckets, table, w // HEAD_DIM)
    ok = self_allowed(lens[page + at], rows)
    lane = lax.broadcasted_iota(jnp.int32, (rows, PAIR), 1)
    dqs, dks, dvs = [], [], []
    for t in range(w // PAIR):
        c = slice(t * PAIR, (t + 1) * PAIR)
        q = pair_rows(qkv[0, :, t * PAIR : (t + 1) * PAIR])
        k = qkv[0, :, w + t * PAIR : w + (t + 1) * PAIR]
        v = qkv[0, :, 2 * w + t * PAIR : 2 * w + (t + 1) * PAIR]
        g = pair_rows(do[:, c])
        s = nt(k, q) + jnp.concatenate(bias[2 * t : 2 * t + 2], axis=1)
        s = jnp.where(ok, s, MASKED)
        p = jnp.exp(s - two_rows(lse[0], t))
        dp = nt(v, g)
        ds = (p * (dp - jnp.sum(p * dp, axis=0, keepdims=True))).astype(BF)
        ds_out[0, 2 * t] = ds[:, :rows]
        ds_out[0, 2 * t + 1] = ds[:, rows:]
        dq = tn(ds, k) * SCALE
        dqs.append(jnp.where(lane < HEAD_DIM, dq[:rows], dq[rows:]).astype(BF))
        dks.append(nn(ds, q).astype(BF))
        dvs.append(nn(p.astype(BF), g).astype(BF))
    dq, dk, dvv = (jnp.concatenate(a, axis=1) for a in (dqs, dks, dvs))
    dq_out[0] = dq
    dk_out[0] = dk
    dv_out[0] = dvv
    dn = (nt(dq, wq[...]) + nt(dk, wk[...]) + nt(dvv, wv[...])).astype(BF).astype(F32)
    dn_keep[0] = jnp.where(first, dn[:half], dn[half:]).astype(BF)
    dn_send[0] = jnp.where(first, dn[half:], dn[:half]).astype(BF)


def self_bwd(at, head, lens, h1, dn_a, dn_b, dh2, gain, wq, wk, wv, wo, buckets, table, qkv, lse, after=()):
    pages, rows, d = dh2.shape
    w = wq.shape[1]
    heads = w // HEAD_DIM
    return call(
        functools.partial(self_bwd_kernel, at),
        (pages,),
        [
            paged((h1, at)), paged(dn_a), paged(dn_b), paged(dh2), whole(gain), whole(wq),
            whole(wk), whole(wv), whole(wo), paged((buckets, at)), whole(table), paged((qkv, at)),
            paged((lse, at)),
        ],
        [
            out_paged((pages, rows // 2, d), F32), out_paged((pages, rows, d), BF),
            out_paged((pages, rows, w), BF), out_paged((pages, rows, w), BF),
            out_paged((pages, rows, w), BF), out_paged((pages, heads, rows, rows), BF),
            out_paged((pages, rows // 2, d), BF), out_paged((pages, rows // 2, d), BF),
            out_whole((8, d), F32),
        ],
        scalars=(head, lens),
        us=2.8 * pages,
        after=after,
    )


def table_grad_kernel(ds, buckets, out):
    page = pl.program_id(0)
    idx = jnp.transpose(buckets[0])
    heads = ds.shape[1]
    dsf = [ds[0, h].astype(F32) for h in range(heads)]
    rows = [[] for _ in range(heads)]
    for b in range(32):
        hit = idx == b
        for h in range(heads):
            rows[h].append(jnp.sum(jnp.where(hit, dsf[h], 0.0), axis=0, keepdims=True))
    for h in range(heads):
        part = jnp.concatenate(rows[h], axis=0)

        @pl.when(page == 0)
        def _():
            out[h] = part

        @pl.when(page != 0)
        def _():
            out[h] += part


def table_grad(ds, buckets, at, after=()):
    pages, heads, rows, _ = ds.shape
    (out,) = call(
        table_grad_kernel,
        (pages,),
        [paged(ds), paged((buckets, at))],
        [out_whole((heads, 32, rows), F32)],
        us=9, after=after,
    )
    return jnp.sum(out, axis=-1)


def cross_q_kernel(xf, a_a, a_b, gain, wq, h1, n2, q2):
    k, rows, d = xf.shape
    h = xf[...].astype(F32) + a_a[...].astype(F32) + a_b[...].astype(F32)
    h1[...] = h
    h = h.reshape(k * rows, d)
    n = (h * inv_rms(h) * gain[...]).astype(BF)
    n2[...] = n.reshape(k, rows, d)
    q = nn(n, wq[...]).astype(BF).astype(F32) * SCALE
    q2[...] = q.astype(BF).reshape(k, rows, wq.shape[1])


def cross_q(xf, a_a, a_b, gain, wq, k, after=()):
    pages, rows, d = xf.shape
    w = wq.shape[1]
    return call(
        cross_q_kernel,
        (pages // k,),
        [paged(xf, k), paged(a_a, k), paged(a_b, k), whole(gain), whole(wq)],
        [
            out_paged((pages, rows, d), F32, k), out_paged((pages, rows, d), BF, k),
            out_paged((pages, rows, w), BF, k),
        ],
        us=5, after=after,
    )


def combine_kernel(nparts, *refs):
    os = refs[:nparts]
    wo, o2, o2t, lse, c_part = refs[nparts:]
    k, w, rows = o2t.shape
    heads = w // HEAD_DIM
    flat = []
    for i in range(k):
        terms = [o[i, w:, :].astype(F32) for o in os]
        ls = [t[:8] + t[8:16] + t[16:24] for t in terms]
        m = ls[0]
        for l in ls[1:]:
            m = jnp.maximum(m, l)
        es = [jnp.exp(l - m) for l in ls]
        total = sum(es[1:], es[0])
        lse[i] = m + jnp.log(total)
        inv = 1.0 / total
        ws = [e * inv for e in es]
        pieces = []
        for h in range(heads):
            r = slice(h * HEAD_DIM, (h + 1) * HEAD_DIM)
            acc = os[0][i, r, :].astype(F32) * ws[0][h : h + 1, :]
            for o, ww in zip(os[1:], ws[1:]):
                acc = acc + o[i, r, :].astype(F32) * ww[h : h + 1, :]
            pieces.append(acc)
        ot = jnp.concatenate(pieces, axis=0)
        o2t[i] = ot.astype(BF)
        o = jnp.transpose(ot).astype(BF)
        o2[i] = o
        flat.append(o)
    c = nn(jnp.concatenate(flat, axis=0), wo[...])
    c_part[...] = c.astype(BF).reshape(c_part.shape)


def combine(os, wo, k, after=()):
    pages, _, rows = os[0].shape
    w, d = wo.shape
    return call(
        functools.partial(combine_kernel, len(os)),
        (pages // k,),
        [paged(o, k) for o in os] + [whole(wo)],
        [
            out_paged((pages, rows, w), BF, k), out_paged((pages, w, rows), BF, k),
            out_paged((pages, 8, rows), F32, k), out_paged((pages, rows, d), BF, k),
        ],
        us=4.5,
        after=after,
    )


def ffn_kernel(h1, c_a, c_b, cot, gain, w_in, w_out, h2, n3, act_out, du_out, dn3):
    k, rows, d = h1.shape
    h = (h1[...] + c_a[...].astype(F32) + c_b[...].astype(F32)).reshape(k * rows, d)
    h2[...] = h.reshape(k, rows, d)
    n = (h * inv_rms(h) * gain[...]).astype(BF)
    n3[...] = n.reshape(k, rows, d)
    g = cot[...].reshape(k * rows, d)
    units = w_in.shape[1]
    step = units // 3
    root = 0.7978845608028654
    total = None
    for j in range(0, units, step):
        c = slice(j, j + step)
        u = nn(n, w_in[:, c])
        da = nt(g, w_out[c, :])
        u2 = u * u
        th = jnp.tanh(root * u * (1.0 + 0.044715 * u2))
        half = 0.5 + 0.5 * th
        act_out[:, :, c] = (u * half).astype(BF).reshape(k, rows, step)
        slope = half + (0.5 * root) * u * (1.0 - th * th) * (1.0 + (3 * 0.044715) * u2)
        du = (da * slope).astype(BF)
        du_out[:, :, c] = du.reshape(k, rows, step)
        part = nt(du, w_in[:, c])
        total = part if total is None else total + part
    dn3[...] = total.astype(BF).reshape(k, rows, d)


def ffn(at, h1, c_a, c_b, cot, gain, w_in, w_out, k, after=()):
    pages, rows, d = c_a.shape
    units = w_in.shape[1]
    return call(
        ffn_kernel,
        (pages // k,),
        [
            paged((h1, at), k), paged(c_a, k), paged(c_b, k), paged((cot, at), k), whole(gain), whole(w_in),
            whole(w_out),
        ],
        [
            out_paged((pages, rows, d), F32, k), out_paged((pages, rows, d), BF, k),
            out_paged((pages, rows, units), BF, k), out_paged((pages, rows, units), BF, k),
            out_paged((pages, rows, d), BF, k),
        ],
        us=12, after=after,
    )


def grad_two_kernel(head, h2, dn_a, dn_b, cot, gain, wo, o2t, lse, dh2, dcr_out, do2, gain_grad):
    step = pl.program_id(0)
    k, rows, d = h2.shape
    half = rows // 2
    w = wo.shape[0]
    first = head[0] == 0
    gacc = None
    flat = []
    for i in range(k):
        gg, dv = norm_back(h2[i], gain[...], dn_a[i].astype(F32) + dn_b[i].astype(F32))
        part = fold8(jnp.where(first, gg[:half], gg[half:]))
        gacc = part if gacc is None else gacc + part
        g = cot[i].astype(F32) + dv
        dh2[i] = g
        dcr = g.astype(BF)
        dcr_out[i] = dcr
        flat.append(dcr)
        dot = nt(wo[...], dcr).astype(BF).astype(F32) * o2t[i].astype(F32)
        sums = [
            jnp.sum(dot[a : a + HEAD_DIM], axis=0, keepdims=True) for a in range(0, w, HEAD_DIM)
        ]
        sums += [jnp.zeros((1, rows), F32)] * (8 - len(sums))
        terms = thirds(lse[i]) + thirds(jnp.concatenate(sums, axis=0))
        stats = jnp.concatenate([t.astype(F32) for t in terms], axis=0)
        per = w // rows
        lines = [
            jnp.concatenate([stats[r + p : r + p + 1] for p in range(per)], axis=1)
            for t in range(6)
            for r in range(8 * t, 8 * t + w // HEAD_DIM, per)
        ]
        lines.append(jnp.zeros((MORE - len(lines), w), F32))
        do2[i, rows:, :] = jnp.concatenate(lines, axis=0).astype(BF)
    g2 = nt(jnp.concatenate(flat, axis=0), wo[...]).astype(BF)
    do2[:, :rows, :] = g2.reshape(k, rows, w)

    @pl.when(step == 0)
    def _():
        gain_grad[...] = gacc

    @pl.when(step != 0)
    def _():
        gain_grad[...] += gacc


def grad_two(at, head, h2, dn_a, dn_b, cot, gain, wo, o2t, lse, k, after=()):
    pages, rows, d = h2.shape
    w = wo.shape[0]
    return call(
        grad_two_kernel,
        (pages // k,),
        [
            paged(h2, k), paged(dn_a, k), paged(dn_b, k), paged((cot, at), k), whole(gain), whole(wo),
            paged(o2t, k), paged(lse, k),
        ],
        [
            out_paged((pages, rows, d), F32, k), out_paged((pages, rows, d), BF, k),
            out_paged((pages, rows + MORE, w), BF, k), out_whole((8, d), F32),
        ],
        scalars=(head,),
        us=5.6, after=after,
    )


def grad_q_kernel(nparts, *refs):
    parts = refs[:nparts]
    wq, dq2, dn2 = refs[nparts:]
    k, w, rows = parts[0].shape
    flat = []
    for i in range(k):
        acc = parts[0][i].astype(F32)
        for p in parts[1:]:
            acc = acc + p[i].astype(F32)
        dq = jnp.transpose(acc).astype(BF)
        dq2[i] = dq
        flat.append(dq)
    dn = nt(jnp.concatenate(flat, axis=0), wq[...])
    dn2[...] = dn.astype(BF).reshape(dn2.shape)


def grad_q(parts, wq, k, after=()):
    pages, w, rows = parts[0].shape
    d = wq.shape[0]
    return call(
        functools.partial(grad_q_kernel, len(parts)),
        (pages // k,),
        [paged(p, k) for p in parts] + [whole(wq)],
        [out_paged((pages, rows, w), BF, k), out_paged((pages, rows, d), BF, k)],
        us=4, after=after,
    )


def last_kernel(xo, dn_a, dn_b, dh1, gain, out, gain_grad):
    page = pl.program_id(0)
    gg, dv = norm_back(
        xo[0].astype(F32), gain[...], dn_a[0].astype(F32) + dn_b[0].astype(F32)
    )
    out[0] = dh1[0] + dv
    part = fold8(gg)

    @pl.when(page == 0)
    def _():
        gain_grad[...] = part

    @pl.when(page != 0)
    def _():
        gain_grad[...] += part


def last(at, xo, dn_a, dn_b, dh1, gain, after=()):
    pages, half, d = dh1.shape
    return call(
        last_kernel,
        (pages,),
        [paged((xo, at)), paged(dn_a), paged(dn_b), paged(dh1), whole(gain)],
        [out_paged((pages, half, d), F32), out_whole((8, d), F32)],
        us=0.9 * pages,
        after=after,
    )


def branch_ffn_kernel(head, act, w_out, keep, send):
    k, rows, units = act.shape
    half = rows // 2
    first = head[0] == 0
    f = nn(act[...].reshape(k * rows, units), w_out[...])
    f = f.reshape(k, rows, f.shape[1])
    keep[...] = jnp.where(first, f[:, :half], f[:, half:]).astype(BF)
    send[...] = jnp.where(first, f[:, half:], f[:, :half]).astype(BF)


def branch_ffn(head, act, w_out, k, after=()):
    pages, rows, units = act.shape
    d = w_out.shape[1]
    return call(
        branch_ffn_kernel,
        (pages // k,),
        [paged(act, k), whole(w_out)],
        [out_paged((pages, rows // 2, d), BF, k), out_paged((pages, rows // 2, d), BF, k)],
        scalars=(head,),
        us=6.8, after=after,
    )


def output_kernel(at, head, lens, h2, f_a, f_b, a_a, a_b, c_a, c_b, out, stats):
    page = pl.program_id(0)
    first = head[0] == 0
    half = f_a.shape[1]

    def mine(ref):
        v = ref[0].astype(F32)
        return jnp.where(first, v[:half], v[half:])

    f = f_a[0].astype(F32) + f_b[0].astype(F32)
    y = mine(h2) + f
    out[0] = y.astype(BF)
    a = mine(a_a) + mine(a_b)
    c = mine(c_a) + mine(c_b)
    row = lax.broadcasted_iota(jnp.int32, (half, 1), 0) + head[0] * half
    valid = (row < lens[page + at]).astype(F32)
    stats[0] = jnp.concatenate(
        [jnp.sum(v * v * valid, axis=0, keepdims=True) for v in (y, a, c, f)]
        + [jnp.zeros((4, y.shape[1]), F32)],
        axis=0,
    )


def output_rows(at, head, lens, h2, f_a, f_b, a_a, a_b, c_a, c_b, after=()):
    pages, rows, d = h2.shape
    return call(
        functools.partial(output_kernel, at),
        (pages,),
        [paged(a) for a in (h2, f_a, f_b, (a_a, at), (a_b, at), c_a, c_b)],
        [out_paged((pages, rows // 2, d), BF), out_paged((pages, 8, d), F32)],
        scalars=(head, lens),
        us=7.4, after=after,
    )


def gate(x):
    return pl.pallas_call(
        lambda *refs: None,
        out_shape=jax.ShapeDtypeStruct(x.shape, x.dtype),
        in_specs=[pl.BlockSpec(memory_space=pl.ANY)] * (1 + len(ORDER)),
        out_specs=pl.BlockSpec(memory_space=pl.ANY),
        input_output_aliases={0: 0},
        cost_estimate=pl.CostEstimate(flops=0, bytes_accessed=0, transcendentals=0),
    )(x, *ORDER)


def kv_kernel(copied, src, dst, enc, w, *refs):
    if copied:
        kv, copy = refs[-2:]
        copy[...] = enc[...]
    else:
        kv = refs[-1]
    for i in range(enc.shape[0]):
        kv[i] = nn(enc[i], w[...]).astype(BF)


def kv_project(src, dst, enc, w, slots, k, copied=False, prev=None, after=()):
    n, d = enc.shape[1:]
    ins = [(enc, (k, n, d), lambda i, a, b: (a[i], 0, 0)), whole(w)]
    if prev is not None:
        ins += [kept(p) for p in prev]
    widths = [w.shape[1]] + [d] * copied
    return call(
        functools.partial(kv_kernel, copied),
        (src.shape[0],),
        ins,
        [((slots, n, c), BF, (k, n, c), lambda i, a, b: (b[i], 0, 0)) for c in widths],
        scalars=(src, dst),
        us=0.9 * k * src.shape[0],
        after=after,
        aliases={} if prev is None else {4 + i: i for i in range(len(prev))},
    )


def cross_fwd_kernel(lims, q, kv_a, kv_b, o):
    slot = pl.program_id(0)
    rows, w = q.shape[1:]
    n = kv_a.shape[1]

    def run(masked):
        rowsum = []
        for t in range(w // PAIR):
            c = slice(t * PAIR, (t + 1) * PAIR)
            cv = slice(w + t * PAIR, w + (t + 1) * PAIR)
            qm = pair_rows(q[0, :, c])
            ss = []
            for j, kv in enumerate((kv_a, kv_b)):
                s = nt(kv[0, :, c], qm)
                if masked:
                    pos = lax.broadcasted_iota(jnp.int32, s.shape, 0)
                    s = jnp.where(pos < lims[j, slot], s, MASKED)
                ss.append(s)
            m = jnp.maximum(*[jnp.max(s, axis=0, keepdims=True) for s in ss])
            es = [jnp.exp(s - m) for s in ss]
            total = sum(jnp.sum(e, axis=0, keepdims=True) for e in es)
            acc = tn(kv_a[0, :, cv], es[0].astype(BF)) + tn(kv_b[0, :, cv], es[1].astype(BF))
            inv = 1.0 / total
            o[0, t * PAIR : t * PAIR + HEAD_DIM, :] = (
                acc[:HEAD_DIM, :rows] * inv[:, :rows]
            ).astype(BF)
            o[0, t * PAIR + HEAD_DIM : (t + 1) * PAIR, :] = (
                acc[HEAD_DIM:, rows:] * inv[:, rows:]
            ).astype(BF)
            row = m + jnp.log(total)
            rowsum += [row[:, :rows], row[:, rows:]]
        rowsum += [jnp.zeros((1, rows), F32)] * (8 - len(rowsum))
        terms = thirds(jnp.concatenate(rowsum, axis=0)) + [jnp.zeros((STATS - 24, rows), BF)]
        o[0, w:, :] = jnp.concatenate([t.astype(F32) for t in terms], axis=0).astype(BF)

    full = (lims[0, slot] >= n) & (lims[1, slot] >= n)
    pl.when(full)(lambda: run(False))
    pl.when(jnp.logical_not(full))(lambda: run(True))


def cross_fwd(lims, q, kv_a, kv_b, at, pages, after=()):
    rows, w = q[0].shape[1:]
    return call(
        cross_fwd_kernel,
        (pages,),
        [paged(q), paged((kv_a, at)), paged((kv_b, at))],
        [out_paged((pages, w + STATS, rows), BF)],
        scalars=(lims,),
        us=1.6 * pages,
        after=after,
    )[0]


def cross_bwd_kernel(lims, q, do, kv_a, kv_b, *refs):
    dq, dkv_a, dkv_b = refs[-3:]
    slot = pl.program_id(0)
    rows, w = q.shape[1:]
    n = kv_a.shape[1]
    per = w // rows
    lines = w // HEAD_DIM // per
    stats = do[0, rows:, :].astype(F32)

    def line(first, head):
        at = [first + t * lines + head // per for t in range(3)]
        c = slice(head % per * rows, (head % per + 1) * rows)
        return sum(stats[a : a + 1, c] for a in at)

    def both(first, t):
        return jnp.concatenate([line(first, 2 * t), line(first, 2 * t + 1)], axis=1)

    def run(masked):
        for t in range(w // PAIR):
            c = slice(t * PAIR, (t + 1) * PAIR)
            cv = slice(w + t * PAIR, w + (t + 1) * PAIR)
            qm = pair_rows(q[0, :, c])
            gm = pair_rows(do[0, :rows, c])
            ls, dl = both(0, t), both(3 * lines, t)
            acc = None
            for j, (kv, dkv) in enumerate(((kv_a, dkv_a), (kv_b, dkv_b))):
                k = kv[0, :, c]
                s = nt(k, qm)
                if masked:
                    pos = lax.broadcasted_iota(jnp.int32, s.shape, 0)
                    s = jnp.where(pos < lims[j, slot], s, MASKED)
                p = jnp.exp(s - ls)
                ds = (p * (nt(kv[0, :, cv], gm) - dl)).astype(BF)
                dkv[0, :, c] = nn(ds, qm).astype(BF)
                dkv[0, :, cv] = nn(p.astype(BF), gm).astype(BF)
                part = tn(k, ds)
                acc = part if acc is None else acc + part
            dq[0, t * PAIR : t * PAIR + HEAD_DIM, :] = (acc[:HEAD_DIM, :rows] * SCALE).astype(BF)
            dq[0, t * PAIR + HEAD_DIM : (t + 1) * PAIR, :] = (
                acc[HEAD_DIM:, rows:] * SCALE
            ).astype(BF)

    full = (lims[0, slot] >= n) & (lims[1, slot] >= n)
    pl.when(full)(lambda: run(False))
    pl.when(jnp.logical_not(full))(lambda: run(True))


def cross_bwd(lims, q, do, kv_a, kv_b, at, prev=None, after=()):
    pages, _, w = do.shape
    rows = q[0].shape[1]
    n = kv_a.shape[1]
    ins = [paged(a) for a in (q, do, (kv_a, at), (kv_b, at))]
    if prev is not None:
        ins += [kept(p) for p in prev]

    def out(v):
        return (v.shape, BF, (1,) + v.shape[1:], lambda i, *_: (i + at, 0, 0))

    return call(
        cross_bwd_kernel,
        (pages,),
        ins,
        [out_paged((pages, w, rows), BF), out(kv_a), out(kv_b)],
        scalars=(lims,),
        us=2.4 * pages,
        after=after,
        aliases={} if prev is None else {5: 1, 6: 2},
    )


def enc_back_kernel(src, head, dkv, enc, w, prev, keep, send, dw):
    low = head[0] == 0
    part = keep.shape[-1]

    @pl.when(pl.program_id(0) == 0)
    def _():
        dw[...] = prev[...]

    for j in range(dkv.shape[0]):
        term = nt(dkv[j], w[...])
        lo, hi = term[:, :part], term[:, part:]
        keep[j] = jnp.where(low, lo, hi).astype(BF)
        send[j] = jnp.where(low, hi, lo).astype(BF)
        dw[...] += tn(enc[j], dkv[j])


def enc_back(src, head, dkv, enc, w, prev, k, after=()):
    slots, n, w2 = dkv.shape
    d = w.shape[0]
    part = d // 2
    return call(
        enc_back_kernel,
        (slots // k,),
        [paged(dkv, k), (enc, (k, n, d), lambda i, t, h: (t[i], 0, 0)), whole(w), whole(prev)],
        [
            out_paged((slots, n, part), BF, k), out_paged((slots, n, part), BF, k),
            out_whole((d, w2), F32),
        ],
        scalars=(src, head),
        us=1.7 * slots,
        after=after,
    )


def add_pages_kernel(a, b, out):
    out[...] = (a[...].astype(F32) + b[...].astype(F32)).astype(BF)


def add_pages(at, pages, a, b, after=()):
    return call(
        add_pages_kernel,
        (pages,),
        [paged((a, at)), paged((b, at))],
        [out_paged((pages,) + a.shape[1:], BF)],
        us=0.7 * pages,
        after=after,
    )[0]


def swap(x, axis, mask, size):
    return lax.ppermute(x, axis, [(i, i ^ mask) for i in range(size)])


def pick(bit, a, b):
    return jnp.where(bit == 0, b, a), jnp.where(bit == 0, a, b)


def rows_of(refs):
    return jnp.concatenate([r[...] for r in refs], axis=0) if len(refs) > 1 else refs[0][...]


def grads_wide_kernel(nc, bits, *refs):
    act, n3, du = (refs[j * nc : (j + 1) * nc] for j in range(3))
    cot, send_a, keep_a, send_b, keep_b = refs[3 * nc :]
    i = pl.program_id(0)
    for lo, out in ((0, send_a), (2, keep_a)):

        @pl.when((i >= lo) & (i < lo + 2))
        def _():
            out[...] = tn(rows_of(act), cot[...]).astype(BF)

    for lo, out in ((4, send_b), (6, keep_b)):

        @pl.when((i >= lo) & (i < lo + 2))
        def _():
            out[...] = tn(rows_of(n3), rows_of(du)).astype(BF)


def flat_rows(v):
    return v.reshape(-1, v.shape[-1])


def grads_wide(bits, act, cot, n3, du, after=()):
    act, n3, du = ([flat_rows(v) for v in c] for c in (act, n3, du))
    cot = flat_rows(cot)
    rows, units, d = act[0].shape[0], act[0].shape[1], cot.shape[1]
    blk = units // 4

    def quarter_a(i, t):
        j = jnp.minimum(i, 3)
        side = jnp.where(j < 2, 1 - t[0], t[0])
        return (0, 2 * side + j % 2)

    def side_b(i, t):
        return (0, jnp.where(jnp.maximum(i, 4) < 6, 1 - t[1], t[1]))

    def out(lo):
        return ((2 * blk, d), BF, (blk, d), lambda i, t: (jnp.clip(i - lo, 0, 1), 0))

    return call(
        functools.partial(grads_wide_kernel, len(act)),
        (8,),
        [(v, (rows, blk), quarter_a) for v in act]
        + [(v, (rows, d // 2), lambda i, t: (0, jnp.maximum(i, 4) % 2)) for v in n3]
        + [(v, (rows, units // 2), side_b) for v in du]
        + [whole(cot)],
        [out(0), out(2), out(4), out(6)],
        scalars=(bits,),
        us=10,
        after=after,
    )


def grads_self_kernel(nc, bits, n, o, *refs):
    dq, dk, dv, g = (rows_of(refs[j * nc : (j + 1) * nc]) for j in range(4))
    send_a, keep_a, send_b, keep_b = refs[4 * nc :]
    d = n.shape[1]
    turned = jnp.transpose(n[...])
    send_a[...], keep_a[...] = pick(bits[0], nn(turned, dq).astype(BF), nn(turned, dk).astype(BF))
    ot = tn(o[...], g).astype(BF)
    ot = jnp.concatenate([ot[:, : d // 2], ot[:, d // 2 :]], axis=0)
    send_b[...], keep_b[...] = pick(bits[1], nn(turned, dv).astype(BF), ot)


def grads_cross_kernel(nc, bits, n, dw, *refs):
    dq, o, g = (rows_of(refs[j * nc : (j + 1) * nc]) for j in range(3))
    send_a, keep_a, send_b, keep_b = refs[3 * nc :]
    d = n.shape[1]
    w = dq.shape[1]
    send_a[...], keep_a[...] = pick(bits[0], tn(n[...], dq).astype(BF), dw[:, :w].astype(BF))
    ot = tn(o, g).astype(BF)
    ot = jnp.concatenate([ot[:, : d // 2], ot[:, d // 2 :]], axis=0)
    send_b[...], keep_b[...] = pick(bits[1], dw[:, w:].astype(BF), ot)


def grads_tall(kernel, bits, arrays, chunked, d, w, us, after=()):
    flat = [flat_rows(v) for v in arrays] + [flat_rows(v) for c in chunked for v in c]
    return call(
        functools.partial(kernel, len(chunked[0])),
        (1,),
        [whole(v) for v in flat],
        [out_whole((d, w), BF)] * 4,
        scalars=(bits,),
        us=us,
        after=after,
    )


def sum_one_kernel(bits, keep_a, got_a, keep_b, got_b, send_a, next_a, send_b, next_b):
    blk = send_a.shape[0]
    for keep, got, send, nxt, bit in (
        (keep_a, got_a, send_a, next_a, bits[1]), (keep_b, got_b, send_b, next_b, bits[0])
    ):
        lo = keep[:blk].astype(F32) + got[:blk].astype(F32)
        hi = keep[blk:].astype(F32) + got[blk:].astype(F32)
        s, k = pick(bit, lo, hi)
        send[...] = s.astype(BF)
        nxt[...] = k.astype(BF)


def sum_two_kernel(nz, place, keep_a, got_a, keep_b, got_b, *rest):
    outs, (sum_a, sum_b) = rest[:nz], rest[nz:]
    part = keep_a.shape[0] // nz
    sum_a[...] = keep_a[...].astype(F32) + got_a[...].astype(F32)
    sum_b[...] = keep_b[...].astype(F32) + got_b[...].astype(F32)
    for k in range(nz):
        z = lax.rem(place[0] + k, nz)
        at = pl.ds(pl.multiple_of(z * part, part), part)
        outs[k][:part] = sum_a[at, :].astype(BF)
        outs[k][part:] = sum_b[at, :].astype(BF)


def sum_three_kernel(*refs):
    acc = refs[0][...].astype(F32)
    for r in refs[1:-1]:
        acc = acc + r[...].astype(F32)
    refs[-1][...] = acc.astype(BF)


def join_kernel(nz, place, *refs):
    pieces, (out_a, out_b, all_a, all_b) = refs[:nz], refs[nz:]
    part = pieces[0].shape[0] // 2
    for k in range(nz):
        z = lax.rem(place[0] + k, nz)
        at = pl.ds(pl.multiple_of(z * part, part), part)
        all_a[at, :] = pieces[k][:part].astype(F32)
        all_b[at, :] = pieces[k][part:].astype(F32)
    out_a[...] = all_a[...].astype(BF)
    out_b[...] = all_b[...].astype(BF)


def reduce_bucket(parts, bits, place, nz):
    send_a, keep_a, send_b, keep_b = parts
    blk, c = send_a.shape[0] // 2, send_a.shape[1]
    piece = (2 * blk // nz, c)
    fast = c / 384

    def x(v):
        return swap(v, "dp", 1, 4)

    def y(v):
        return swap(v, "dp", 2, 4)

    def shift(v, k):
        return lax.ppermute(v, "seq", [((i + k) % nz, i) for i in range(nz)])

    got_a, got_b = x(send_a), y(send_b)
    yield
    send_a, keep_a, send_b, keep_b = call(
        sum_one_kernel, (1,), [whole(v) for v in (keep_a, got_a, keep_b, got_b)],
        [out_whole((blk, c), BF)] * 4, scalars=(bits,), us=2 * fast,
    )
    got_a, got_b = y(send_a), x(send_b)
    yield
    outs = call(
        functools.partial(sum_two_kernel, nz), (1,),
        [whole(v) for v in (keep_a, got_a, keep_b, got_b)], [out_whole(piece, BF)] * nz,
        scalars=(place,), scratch=[pltpu.VMEM((blk, c), F32)] * 2, us=1.5 * fast,
    )
    got = [shift(outs[k], -k) for k in range(1, nz)]
    yield
    (mine,) = call(
        sum_three_kernel, (1,), [whole(v) for v in [outs[0]] + got], [out_whole(piece, BF)],
        us=1.5,
    )
    pieces = [mine] + [shift(mine, k) for k in range(1, nz)]
    yield
    a0, b0 = call(
        functools.partial(join_kernel, nz), (1,), [whole(v) for v in pieces],
        [out_whole((blk, c), BF)] * 2, scalars=(place,),
        scratch=[pltpu.VMEM((blk, c), F32)] * 2, us=1.5 * fast,
    )
    a1, b1 = y(a0), x(b0)
    a2, b2 = x(a0), y(b0)
    a3, b3 = x(a1), y(b1)
    yield [a0, a1, a2, a3, b0, b1, b2, b3]


def final_kernel(outs, bits, *refs):
    pieces, results = refs[:8], refs[8:]
    t = pl.program_id(0)
    for half, (hi, lo) in enumerate(((bits[0], bits[1]), (bits[1], bits[0]))):
        rel = (t // 2 + hi) % 2 * 2 + (t % 2 + lo) % 2
        for j in range(4):
            for r, (at, first, count) in zip(results, outs):
                if at != half:
                    continue

                @pl.when((rel == j) & (t >= first) & (t < first + count))
                def _():
                    r[...] = pieces[4 * half + j][...].astype(F32)


def final(pieces, bits, outs, us, after=()):
    blk, c = pieces[0].shape

    def index(first, count, where):
        return lambda t, *_: where(jnp.clip(t - first, 0, count - 1))

    return call(
        functools.partial(final_kernel, [(o[1], o[2], o[3]) for o in outs]),
        (4,),
        [whole(p) for p in pieces],
        [(o[0], F32, (blk, c), index(o[2], o[3], o[4])) for o in outs],
        scalars=(bits,),
        us=us,
        after=after,
    )


def per_device(
    sizes,
    dec_input,
    enc_states,
    page_group,
    target_mask,
    rel_buckets,
    self_gain,
    cross_gain,
    ffn_gain,
    self_q,
    self_k,
    self_v,
    self_o,
    rel_table,
    cross_q_w,
    cross_k,
    cross_v,
    cross_o,
    ff_in,
    ff_out,
    cotangent,
):
    n_seq = sizes["seq"]
    pages, half, d = dec_input.shape
    n = enc_states.shape[1]
    w = self_q.shape[1]
    nb = n_seq // 2
    slots = nb * pages
    k = 3
    chunks = pages // k
    ORDER.clear()
    s = lax.axis_index("seq")
    h = lax.axis_index("head")
    dp = lax.axis_index("dp")
    block, par = s // 2, s % 2
    head = h.reshape(1).astype(jnp.int32)
    bits = jnp.stack([dp % 2, dp // 2]).astype(jnp.int32)
    place = s.reshape(1).astype(jnp.int32)

    kk = jnp.arange(nb * chunks, dtype=jnp.int32) // chunks
    cc = jnp.arange(nb * chunks, dtype=jnp.int32) % chunks
    ident = jnp.arange(nb * chunks, dtype=jnp.int32)
    own_groups = ((((block + kk) % nb) * 2 + par) * chunks + cc).astype(jnp.int32)
    jl = jnp.arange(nb, dtype=jnp.int32)
    arrived = ((jl + h * (nb // 2) - block) % nb * chunks).astype(jnp.int32)

    def head_swap(x):
        return swap(x, "head", 1, 2)

    def rolled(x, step):
        perm = [(2 * b + r, 2 * ((b - step) % nb) + r) for b in range(nb) for r in range(2)]
        return lax.ppermute(x, "seq", perm) if step % nb else x

    def owners(x):
        return [rolled(x, step) for step in range(nb)]

    others = list(range(1, nb))
    both = range(chunks)

    x_other = head_swap(dec_input)
    away = lax.dynamic_slice(
        enc_states.reshape(nb, 2, pages, n, d),
        (h * (nb // 2), 1 - par, 0, 0, 0),
        (nb // 2, 1, pages, n, d),
    ).reshape(nb // 2, pages, n, d)
    away = [away[:, c * k : (c + 1) * k].reshape(nb // 2 * k, n, d) for c in both]
    enc_in = [swap(away[0], "seq", 1, n_seq)]
    cot_other = head_swap(cotangent)
    cot = jnp.concatenate(
        [jnp.where(h == 0, cotangent, cot_other), jnp.where(h == 0, cot_other, cotangent)], axis=1
    )
    enc_len = [
        OCR + PATCH_SMALL + g * (PATCH_LARGE - PATCH_SMALL) for g in owners(page_group)
    ]
    lims = [
        jnp.stack([e - s * n, e - (s + 1 - 2 * par) * n]).astype(jnp.int32) for e in enc_len
    ]
    lens = jnp.sum(target_mask, axis=1).astype(jnp.int32)
    table = jnp.pad(rel_table.T, ((0, 8 - rel_table.shape[1]), (0, 128 - rel_table.shape[0])))
    gains = [g.reshape(1, d) for g in (self_gain, cross_gain, ffn_gain)]
    w_kv = jnp.concatenate([cross_k, cross_v], axis=1)

    xf, n1, qkv, o1, lse1, a_part = self_fwd(
        head, lens, dec_input, x_other, gains[0], self_q, self_k, self_v, self_o, rel_buckets, table,
        after=(away[0], *lims[1:]),
    )
    a_other = head_swap(a_part)
    h1, n2, q2 = cross_q(xf, a_part, a_other, gains[1], cross_q_w, k)
    qs = owners(q2)
    for c in both[1:]:
        enc_in.append(swap(gate(away[c]), "seq", 1, n_seq))
    (kv_a,) = kv_project(own_groups, ident, enc_states, w_kv, slots, k)
    os = [[None] * chunks for _ in range(nb)]
    rec = None

    def attend(j, c):
        o = cross_fwd(
            lims[j][:, c * k : (c + 1) * k], (qs[j], c * k), kv_a, kv_b, j * pages + c * k, k
        )
        os[j][c] = rolled(o, -j)

    for c in both:
        direct = gate(enc_in[c])
        for late, part in enumerate((direct, head_swap(direct))):
            rec = kv_project(
                ident[: nb // 2], arrived[late * (nb // 2) : (late + 1) * (nb // 2)] + c, part,
                w_kv, slots, k, copied=True, prev=rec,
            )
        kv_b, enc_rec = rec
        attend(0, c)
        if c:
            for e in range(c - 1, chunks if c == chunks - 1 else c):
                for j in others:
                    attend(j, e)

    o2, o2t, lse2, c_part, c_other = ([None] * chunks for _ in range(5))
    h2, n3, act, du, dn3, dn3_other = ([None] * chunks for _ in range(6))
    dh2, dcr, gain3, dos = ([None] * chunks for _ in range(4))
    dqs = [[None] * chunks for _ in range(nb)]
    dkv = None

    def mix(c):
        o2[c], o2t[c], lse2[c], c_part[c] = combine(
            [v[c] for v in os], cross_o, k
        )
        c_other[c] = head_swap(c_part[c])

    def feed(c):
        h2[c], n3[c], act[c], du[c], dn3[c] = ffn(
            c * k, h1, c_part[c], c_other[c], cot, gains[2], ff_in, ff_out, k
        )
        dn3_other[c] = head_swap(dn3[c])

    def turn(c):
        dh2[c], dcr[c], do2, gain3[c] = grad_two(
            c * k, head, h2[c], dn3[c], dn3_other[c], cot, gains[2], cross_o, o2t[c], lse2[c], k
        )
        dos[c] = owners(do2)

    def back(j, c):
        nonlocal dkv
        dqs[j][c], *dkv = cross_bwd(
            lims[j][:, c * k : (c + 1) * k], (qs[j], c * k), dos[c][j], kv_a, kv_b,
            j * pages + c * k, prev=dkv,
        )
        dqs[j][c] = rolled(dqs[j][c], -j)

    mix(0)
    feed(0)
    for c in both[1:]:
        mix(c)
        turn(c - 1)
        feed(c)
        back(0, c - 1)
    turn(chunks - 1)
    grads_ffn = reduce_bucket(grads_wide(bits, act, cot, n3, du), bits, place, n_seq)
    next(grads_ffn)
    for c in both[:-1]:
        for j in others:
            back(j, c)
    for j in [0] + others:
        back(j, chunks - 1)
    next(grads_ffn)

    keep_b, send_b, dw = enc_back(
        ident, head, dkv[1], enc_rec, w_kv, jnp.zeros((d, 2 * w), F32), k
    )
    send_b = head_swap(send_b)
    dq2, dn2, dn2_other = ([None] * chunks for _ in range(3))
    for c in both:
        dq2[c], dn2[c] = grad_q([v[c] for v in dqs], cross_q_w, k)
        dn2_other[c] = head_swap(dn2[c])
        if c == 0:
            next(grads_ffn)
    quarter = slots // 4
    enc_away = []

    def send_away(*parts):
        for i in parts:
            enc_away.append(
                swap(add_pages(i * quarter, quarter, keep_b, send_b), "seq", 1, n_seq)
            )

    backs = []
    dn1_other = []
    for c in both:
        backs.append(
            self_bwd(
                c * k, head, lens, h1, dn2[c], dn2_other[c], dh2[c], gains[1], self_q, self_k,
                self_v, self_o, rel_buckets, table, qkv, lse1,
            )
        )
        dn1_other.append(head_swap(backs[c][7]))
        if c == 0:
            send_away(0)
    dh1, dar, dq1, dk1, dv1, ds1, dn1, _, gain2 = zip(*backs)
    grads_self = reduce_bucket(
        grads_tall(
            grads_self_kernel, bits, [n1, o1], [dq1, dk1, dv1, dar], d, w, 7
        ),
        bits, place, n_seq,
    )
    next(grads_self)
    next(grads_ffn)
    send_away(1)
    keep_a, send_a, dw = enc_back(own_groups, head, dkv[0], enc_states, w_kv, dw, k)
    send_a = head_swap(send_a)
    next(grads_self)
    grads_cross = reduce_bucket(
        grads_tall(grads_cross_kernel, bits, [n2, dw], [dq2, o2, dcr], d, w, 6),
        bits, place, n_seq,
    )
    next(grads_cross)
    sums_ffn = next(grads_ffn)
    next(grads_self)
    lasts = [last(c * k, dec_input, dn1[c], dn1_other[c], dh1[c], gains[0]) for c in both]
    next(grads_cross)
    send_away(2)
    next(grads_self)
    branches = [branch_ffn(head, act[c], ff_out, k) for c in both]
    f_other = [head_swap(f[1]) for f in branches]
    next(grads_cross)
    sums_self = next(grads_self)
    send_away(3)
    tables = [table_grad(ds1[c], rel_buckets, c * k) for c in both]
    next(grads_cross)
    outputs = [
        output_rows(
            c * k, head, lens, h2[c], branches[c][0], f_other[c], a_part, a_other, c_part[c],
            c_other[c],
        )
        for c in both
    ]
    sums_cross = next(grads_cross)

    units = ff_in.shape[1]
    row, col = (lambda v: (v, 0)), (lambda v: (0, v))
    ff_out_grad, ff_in_grad = final(
        sums_ffn, bits,
        [((units, d), 0, 0, 4, row), ((d, units), 1, 0, 4, lambda v: (v % 2, v // 2))], 6,
    )
    four = [
        ((d, w), 0, 0, 2, row), ((d, w), 0, 2, 2, row), ((d, w), 1, 0, 2, row), ((w, d), 1, 2, 2, col)
    ]
    sq, sk, sv, so = final(sums_self, bits, four, 4)

    back_a = (keep_a.astype(F32) + send_a.astype(F32)).astype(BF)
    enc_away = jnp.concatenate(enc_away, axis=0)
    pieces = []
    for j in range(nb):
        at = (j - block) % nb * pages
        mine, theirs = (
            lax.dynamic_slice_in_dim(v, at, pages, 0) for v in (back_a, enc_away)
        )
        pieces += [jnp.where(par == 0, mine, theirs), jnp.where(par == 0, theirs, mine)]
    enc_t = jnp.transpose(jnp.concatenate(pieces, axis=0), (1, 0, 2)).astype(F32)
    enc_grad = jnp.transpose(with_layout_constraint(enc_t, Layout((0, 1, 2))), (1, 0, 2))
    cq, ck, cv, co = final(sums_cross, bits, four, 4)

    output = jnp.concatenate([o[0] for o in outputs], axis=0)
    input_grad = jnp.concatenate([o[0] for o in lasts], axis=0)
    squares = jnp.sum(jnp.concatenate([o[1] for o in outputs], axis=0)[:, :4], axis=-1)
    squares = squares + head_swap(squares)
    counts = lens.astype(F32) * d
    rms_stats = jnp.sqrt(squares / counts[:, None])
    small = jnp.stack(
        [jnp.sum(sum(g), axis=0) for g in ([o[1] for o in lasts], gain2, gain3)]
    )
    small = small + head_swap(small)
    table_part = sum(tables)
    line = jnp.pad(table_part.reshape(1, -1), ((0, 0), (0, d - table_part.size)))
    small = jnp.concatenate([small, line], axis=0)
    for axis in ("dp", "seq"):
        for i in range(sizes[axis].bit_length() - 1):
            small = small + swap(small, axis, 1 << i, sizes[axis])
    table_sum = small[3, : table_part.size].reshape(table_part.shape)

    return (
        output, input_grad, enc_grad, small[0], small[1], small[2], sq, sk, sv, so, table_sum.T,
        cq, ck, cv, co, ff_in_grad, ff_out_grad, rms_stats,
    )


def solution(mesh):
    sizes = dict(mesh.shape)
    rows = P(("dp", "seq"), "head", None)
    cols, tall = P(None, "head"), P("head", None)
    placed = (
        rows, P("dp", "seq", None), P(("dp", "seq")), P(("dp", "seq"), None),
        P(("dp", "seq"), None, None), P(), P(), P(), cols, cols, cols, tall, cols, cols, cols, cols,
        tall, cols, tall, rows,
    )
    return jax.shard_map(
        functools.partial(per_device, sizes),
        mesh=mesh,
        in_specs=placed,
        out_specs=(
            rows, rows, P("dp", "seq", "head"), P(), P(), P(), cols, cols, cols, tall, cols, cols,
            cols, cols, tall, cols, tall, P(("dp", "seq"), None),
        ),
        check_vma=False,
    )
```

```python
import functools

import jax
import jax.numpy as jnp
from jax import lax
from jax.experimental import pallas as pl
from jax.experimental.layout import Layout, with_layout_constraint
from jax.experimental.pallas import tpu as pltpu
from jax.sharding import PartitionSpec as P

HEAD_DIM = 64
OCR = 512
PATCH_SMALL = 196
PATCH_LARGE = 784
EPSILON = 1e-06
MASKED = -1000000000.0
BF = jnp.bfloat16
F32 = jnp.float32
SCALE = HEAD_DIM ** (-0.5)
VMEM = 56 * 1024 * 1024
PAIR = 2 * HEAD_DIM


def nn(a, b):
    return lax.dot_general(a, b, (((1,), (0,)), ((), ())), preferred_element_type=F32)


def nt(a, b):
    return lax.dot_general(a, b, (((1,), (1,)), ((), ())), preferred_element_type=F32)


def tn(a, b):
    return lax.dot_general(a, b, (((0,), (0,)), ((), ())), preferred_element_type=F32)


ORDER = []


def call(body, grid, ins, outs, *, us, scalars=(), scratch=(), after=(), aliases={}):
    held = [a for a, _, _ in ins]
    after = [t for t in [*after, *ORDER] if not any(t is a for a in held)]
    first, last = len(scalars) + len(ins), len(scalars) + len(ins) + len(after)

    def run(*refs):
        body(*refs[:first], *refs[last:])

    spec = pltpu.PrefetchScalarGridSpec(
        num_scalar_prefetch=len(scalars),
        grid=grid,
        in_specs=[pl.BlockSpec(b, m) for _, b, m in ins]
        + [pl.BlockSpec(memory_space=pl.ANY)] * len(after),
        out_specs=[pl.BlockSpec(b, m) for _, _, b, m in outs],
        scratch_shapes=list(scratch),
    )
    results = pl.pallas_call(
        run,
        grid_spec=spec,
        out_shape=[jax.ShapeDtypeStruct(s, d) for s, d, _, _ in outs],
        compiler_params=pltpu.CompilerParams(
            vmem_limit_bytes=VMEM, dimension_semantics=("arbitrary",) * len(grid)
        ),
        cost_estimate=pl.CostEstimate(flops=int(us * 1e10), bytes_accessed=0, transcendentals=0),
        input_output_aliases=aliases,
    )(*scalars, *[a for a, _, _ in ins], *after)
    ORDER[:] = [min(results, key=lambda r: r.size)]
    return results


def whole(a):
    n = a.ndim
    return (a, a.shape, lambda *_: (0,) * n)


def paged(a, k=1):
    a, at = a if isinstance(a, tuple) else (a, 0)
    n = a.ndim
    return (a, (k,) + a.shape[1:], lambda i, *_: (i + at // k,) + (0,) * (n - 1))


def kept(a):
    n = a.ndim
    return (a, (1,) * (n - 2) + (8, 128), lambda *_: (0,) * n)


def out_paged(shape, dtype, k=1):
    n = len(shape)
    return (shape, dtype, (k,) + tuple(shape[1:]), lambda i, *_: (i,) + (0,) * (n - 1))


def out_whole(shape, dtype):
    n = len(shape)
    return (shape, dtype, tuple(shape), lambda *_: (0,) * n)


def inv_rms(v):
    return lax.rsqrt(jnp.mean(v * v, axis=-1, keepdims=True) + EPSILON)


def pair_rows(block):
    lane = lax.broadcasted_iota(jnp.int32, (1, PAIR), 1)
    low = (lane < HEAD_DIM).astype(F32).astype(block.dtype)
    return jnp.concatenate([block * low, block * (1 - low)], axis=0)


def thirds(v):
    hi = v.astype(BF)
    rest = v - hi.astype(F32)
    mid = rest.astype(BF)
    return [hi, mid, (rest - mid.astype(F32)).astype(BF)]


def joined(hi, mid, lo):
    return hi.astype(F32) + mid.astype(F32) + lo.astype(F32)


STATS = 32
MORE = 32


def two_rows(ref_rows, t):
    return jnp.concatenate([ref_rows[2 * t : 2 * t + 1, :], ref_rows[2 * t + 1 : 2 * t + 2, :]], axis=1)


def norm_back(v, gain, dn):
    inv = inv_rms(v)
    weighted = dn * gain
    inner = jnp.mean(weighted * v, axis=-1, keepdims=True)
    return dn * v * inv, inv * weighted - v * (inv * inv * inv * inner)


def fold8(v):
    return jnp.sum(v.reshape(v.shape[0] // 8, 8, v.shape[1]), axis=0)


def self_bias(buckets_ref, table_ref, heads):
    idx = jnp.transpose(buckets_ref[0])
    rows = []
    for h in range(heads):
        tab = jnp.broadcast_to(table_ref[h : h + 1, :], idx.shape)
        rows.append(jnp.take_along_axis(tab, idx, axis=1))
    return rows


def self_allowed(length, rows):
    key = lax.broadcasted_iota(jnp.int32, (rows, rows), 0)
    query = lax.broadcasted_iota(jnp.int32, (rows, rows), 1)
    ok = (key <= query) & (key < length)
    return jnp.concatenate([ok, ok], axis=1)


def self_fwd_kernel(
    head, lens, xo, xr, gain, wq, wk, wv, wo, buckets, table, xf, n1, qkv, o1, lse, a_part
):
    page = pl.program_id(0)
    first = head[0] == 0
    own, rec = xo[0].astype(F32), xr[0].astype(F32)
    x = jnp.concatenate([jnp.where(first, own, rec), jnp.where(first, rec, own)], axis=0)
    xf[0] = x.astype(BF)
    n = (x * inv_rms(x) * gain[0:1]).astype(BF)
    n1[0] = n
    w = wq.shape[1]
    q = (nn(n, wq[...]).astype(BF).astype(F32) * SCALE).astype(BF)
    k = nn(n, wk[...]).astype(BF)
    v = nn(n, wv[...]).astype(BF)
    qkv[0, :, 0:w] = q
    qkv[0, :, w : 2 * w] = k
    qkv[0, :, 2 * w : 3 * w] = v
    rows = x.shape[0]
    bias = self_bias(buckets, table, w // HEAD_DIM)
    ok = self_allowed(lens[page], rows)
    lses, outs = [], []
    for t in range(w // PAIR):
        c = slice(t * PAIR, (t + 1) * PAIR)
        s = nt(k[:, c], pair_rows(q[:, c])) + jnp.concatenate(bias[2 * t : 2 * t + 2], axis=1)
        s = jnp.where(ok, s, MASKED)
        m = jnp.max(s, axis=0, keepdims=True)
        e = jnp.exp(s - m)
        total = jnp.sum(e, axis=0, keepdims=True)
        p = e * (1.0 / total)
        o = tn(p.astype(BF), v[:, c])
        lane = lax.broadcasted_iota(jnp.int32, (rows, PAIR), 1)
        outs.append(jnp.where(lane < HEAD_DIM, o[:rows], o[rows:]))
        row = m + jnp.log(total)
        lses += [row[:, :rows], row[:, rows:]]
    lses += [jnp.zeros((1, rows), F32)] * (8 - len(lses))
    lse[0] = jnp.concatenate(lses, axis=0)
    o = jnp.concatenate(outs, axis=1).astype(BF)
    o1[0] = o
    a_part[0] = nn(o, wo[...]).astype(BF)


def self_fwd(head, lens, xo, xr, gain, wq, wk, wv, wo, buckets, table, after=()):
    pages, half, d = xo.shape
    rows, w = 2 * half, wq.shape[1]
    return call(
        self_fwd_kernel,
        (pages,),
        [
            paged(xo), paged(xr), whole(gain), whole(wq), whole(wk), whole(wv), whole(wo),
            paged(buckets), whole(table),
        ],
        [
            out_paged((pages, rows, d), BF), out_paged((pages, rows, d), BF),
            out_paged((pages, rows, 3 * w), BF), out_paged((pages, rows, w), BF),
            out_paged((pages, 8, rows), F32), out_paged((pages, rows, d), BF),
        ],
        scalars=(head, lens),
        us=10, after=after,
    )


def self_bwd_kernel(
    at, head, lens, h1, dn_a, dn_b, dh2, gain, wq, wk, wv, wo, buckets, table, qkv, lse,
    dh1, dar_out, dq_out, dk_out, dv_out, ds_out, dn_keep, dn_send, gain_grad,
):
    page = pl.program_id(0)
    first = head[0] == 0
    v1 = h1[0]
    rows = v1.shape[0]
    half = rows // 2
    gg, dv = norm_back(v1, gain[1:2], dn_a[0].astype(F32) + dn_b[0].astype(F32))
    d1 = dh2[0] + dv
    gpart = fold8(jnp.where(first, gg[:half], gg[half:]))

    @pl.when(page == 0)
    def _():
        gain_grad[...] = gpart

    @pl.when(page != 0)
    def _():
        gain_grad[...] += gpart

    dh1[0] = jnp.where(first, d1[:half], d1[half:])
    dar = d1.astype(BF)
    dar_out[0] = dar
    w = wo.shape[0]
    do = nt(dar, wo[...]).astype(BF)
    bias = self_bias(buckets, table, w // HEAD_DIM)
    ok = self_allowed(lens[page + at], rows)
    lane = lax.broadcasted_iota(jnp.int32, (rows, PAIR), 1)
    dqs, dks, dvs = [], [], []
    for t in range(w // PAIR):
        c = slice(t * PAIR, (t + 1) * PAIR)
        q = pair_rows(qkv[0, :, t * PAIR : (t + 1) * PAIR])
        k = qkv[0, :, w + t * PAIR : w + (t + 1) * PAIR]
        v = qkv[0, :, 2 * w + t * PAIR : 2 * w + (t + 1) * PAIR]
        g = pair_rows(do[:, c])
        s = nt(k, q) + jnp.concatenate(bias[2 * t : 2 * t + 2], axis=1)
        s = jnp.where(ok, s, MASKED)
        p = jnp.exp(s - two_rows(lse[0], t))
        dp = nt(v, g)
        ds = (p * (dp - jnp.sum(p * dp, axis=0, keepdims=True))).astype(BF)
        ds_out[0, 2 * t] = ds[:, :rows]
        ds_out[0, 2 * t + 1] = ds[:, rows:]
        dq = tn(ds, k) * SCALE
        dqs.append(jnp.where(lane < HEAD_DIM, dq[:rows], dq[rows:]).astype(BF))
        dks.append(nn(ds, q).astype(BF))
        dvs.append(nn(p.astype(BF), g).astype(BF))
    dq, dk, dvv = (jnp.concatenate(a, axis=1) for a in (dqs, dks, dvs))
    dq_out[0] = dq
    dk_out[0] = dk
    dv_out[0] = dvv
    dn = (nt(dq, wq[...]) + nt(dk, wk[...]) + nt(dvv, wv[...])).astype(BF).astype(F32)
    dn_keep[0] = jnp.where(first, dn[:half], dn[half:]).astype(BF)
    dn_send[0] = jnp.where(first, dn[half:], dn[:half]).astype(BF)


def self_bwd(at, head, lens, h1, dn_a, dn_b, dh2, gain, wq, wk, wv, wo, buckets, table, qkv, lse, after=()):
    pages, rows, d = dh2.shape
    w = wq.shape[1]
    heads = w // HEAD_DIM
    return call(
        functools.partial(self_bwd_kernel, at),
        (pages,),
        [
            paged((h1, at)), paged(dn_a), paged(dn_b), paged(dh2), whole(gain), whole(wq),
            whole(wk), whole(wv), whole(wo), paged((buckets, at)), whole(table), paged((qkv, at)),
            paged((lse, at)),
        ],
        [
            out_paged((pages, rows // 2, d), F32), out_paged((pages, rows, d), BF),
            out_paged((pages, rows, w), BF), out_paged((pages, rows, w), BF),
            out_paged((pages, rows, w), BF), out_paged((pages, heads, rows, rows), BF),
            out_paged((pages, rows // 2, d), BF), out_paged((pages, rows // 2, d), BF),
            out_whole((8, d), F32),
        ],
        scalars=(head, lens),
        us=2.8 * pages,
        after=after,
    )


def table_grad_kernel(ds, buckets, out):
    page = pl.program_id(0)
    idx = jnp.transpose(buckets[0])
    heads = ds.shape[1]
    dsf = [ds[0, h].astype(F32) for h in range(heads)]
    rows = [[] for _ in range(heads)]
    for b in range(32):
        hit = idx == b
        for h in range(heads):
            rows[h].append(jnp.sum(jnp.where(hit, dsf[h], 0.0), axis=0, keepdims=True))
    for h in range(heads):
        part = jnp.concatenate(rows[h], axis=0)

        @pl.when(page == 0)
        def _():
            out[h] = part

        @pl.when(page != 0)
        def _():
            out[h] += part


def table_grad(ds, buckets, at, after=()):
    pages, heads, rows, _ = ds.shape
    (out,) = call(
        table_grad_kernel,
        (pages,),
        [paged(ds), paged((buckets, at))],
        [out_whole((heads, 32, rows), F32)],
        us=9, after=after,
    )
    return jnp.sum(out, axis=-1)


def cross_q_kernel(xf, a_a, a_b, gain, wq, h1, n2, q2, zero):
    zero[...] = jnp.zeros_like(zero)
    k, rows, d = xf.shape
    h = xf[...].astype(F32) + a_a[...].astype(F32) + a_b[...].astype(F32)
    h1[...] = h
    h = h.reshape(k * rows, d)
    n = (h * inv_rms(h) * gain[1:2]).astype(BF)
    n2[...] = n.reshape(k, rows, d)
    q = nn(n, wq[...]).astype(BF).astype(F32) * SCALE
    q2[...] = q.astype(BF).reshape(k, rows, wq.shape[1])


def cross_q(xf, a_a, a_b, gain, wq, k, after=()):
    pages, rows, d = xf.shape
    w = wq.shape[1]
    return call(
        cross_q_kernel,
        (pages // k,),
        [paged(xf, k), paged(a_a, k), paged(a_b, k), whole(gain), whole(wq)],
        [
            out_paged((pages, rows, d), F32, k), out_paged((pages, rows, d), BF, k),
            out_paged((pages, rows, w), BF, k), out_whole((8, 128), jnp.int32),
        ],
        us=4, after=after,
    )


def combine_kernel(nparts, *refs):
    os = refs[:nparts]
    wo, o2, o2t, lse, c_part = refs[nparts:]
    k, w, rows = o2t.shape
    heads = w // HEAD_DIM
    flat = []
    for i in range(k):
        terms = [o[i, w:, :].astype(F32) for o in os]
        ls = [t[:8] + t[8:16] + t[16:24] for t in terms]
        m = ls[0]
        for l in ls[1:]:
            m = jnp.maximum(m, l)
        es = [jnp.exp(l - m) for l in ls]
        total = sum(es[1:], es[0])
        lse[i] = m + jnp.log(total)
        inv = 1.0 / total
        ws = [e * inv for e in es]
        pieces = []
        for h in range(heads):
            r = slice(h * HEAD_DIM, (h + 1) * HEAD_DIM)
            acc = os[0][i, r, :].astype(F32) * ws[0][h : h + 1, :]
            for o, ww in zip(os[1:], ws[1:]):
                acc = acc + o[i, r, :].astype(F32) * ww[h : h + 1, :]
            pieces.append(acc)
        ot = jnp.concatenate(pieces, axis=0)
        o2t[i] = ot.astype(BF)
        o = jnp.transpose(ot).astype(BF)
        o2[i] = o
        flat.append(o)
    c = nn(jnp.concatenate(flat, axis=0), wo[...])
    c_part[...] = c.astype(BF).reshape(c_part.shape)


def combine(os, wo, k, after=()):
    pages, _, rows = os[0].shape
    w, d = wo.shape
    return call(
        functools.partial(combine_kernel, len(os)),
        (pages // k,),
        [paged(o, k) for o in os] + [whole(wo)],
        [
            out_paged((pages, rows, w), BF, k), out_paged((pages, w, rows), BF, k),
            out_paged((pages, 8, rows), F32, k), out_paged((pages, rows, d), BF, k),
        ],
        us=2.7,
        after=after,
    )


def ffn_kernel(h1, c_a, c_b, cot, gain, w_in, w_out, h2, n3, act_out, du_out, dn3):
    k, rows, d = h1.shape
    h = (h1[...] + c_a[...].astype(F32) + c_b[...].astype(F32)).reshape(k * rows, d)
    h2[...] = h.reshape(k, rows, d)
    n = (h * inv_rms(h) * gain[2:3]).astype(BF)
    n3[...] = n.reshape(k, rows, d)
    g = cot[...].reshape(k * rows, d)
    units = w_in.shape[1]
    step = units // 3
    root = 0.7978845608028654
    total = None
    for j in range(0, units, step):
        c = slice(j, j + step)
        u = nn(n, w_in[:, c])
        da = nt(g, w_out[c, :])
        u2 = u * u
        th = jnp.tanh(root * u * (1.0 + 0.044715 * u2))
        half = 0.5 + 0.5 * th
        act_out[:, :, c] = (u * half).astype(BF).reshape(k, rows, step)
        slope = half + (0.5 * root) * u * (1.0 - th * th) * (1.0 + (3 * 0.044715) * u2)
        du = (da * slope).astype(BF)
        du_out[:, :, c] = du.reshape(k, rows, step)
        part = nt(du, w_in[:, c])
        total = part if total is None else total + part
    dn3[...] = total.astype(BF).reshape(k, rows, d)


def ffn(at, h1, c_a, c_b, cot, gain, w_in, w_out, k, after=()):
    pages, rows, d = c_a.shape
    units = w_in.shape[1]
    return call(
        ffn_kernel,
        (pages // k,),
        [
            paged((h1, at), k), paged(c_a, k), paged(c_b, k), paged((cot, at), k), whole(gain), whole(w_in),
            whole(w_out),
        ],
        [
            out_paged((pages, rows, d), F32, k), out_paged((pages, rows, d), BF, k),
            out_paged((pages, rows, units), BF, k), out_paged((pages, rows, units), BF, k),
            out_paged((pages, rows, d), BF, k),
        ],
        us=12, after=after,
    )


def grad_two_kernel(head, h2, dn_a, dn_b, cot, gain, wo, o2t, lse, dh2, dcr_out, do2, gain_grad):
    step = pl.program_id(0)
    k, rows, d = h2.shape
    half = rows // 2
    w = wo.shape[0]
    first = head[0] == 0
    gacc = None
    flat = []
    for i in range(k):
        gg, dv = norm_back(h2[i], gain[2:3], dn_a[i].astype(F32) + dn_b[i].astype(F32))
        part = fold8(jnp.where(first, gg[:half], gg[half:]))
        gacc = part if gacc is None else gacc + part
        g = cot[i].astype(F32) + dv
        dh2[i] = g
        dcr = g.astype(BF)
        dcr_out[i] = dcr
        flat.append(dcr)
        dot = nt(wo[...], dcr).astype(BF).astype(F32) * o2t[i].astype(F32)
        sums = [
            jnp.sum(dot[a : a + HEAD_DIM], axis=0, keepdims=True) for a in range(0, w, HEAD_DIM)
        ]
        sums += [jnp.zeros((1, rows), F32)] * (8 - len(sums))
        terms = thirds(lse[i]) + thirds(jnp.concatenate(sums, axis=0))
        stats = jnp.concatenate([t.astype(F32) for t in terms], axis=0)
        per = w // rows
        lines = [
            jnp.concatenate([stats[r + p : r + p + 1] for p in range(per)], axis=1)
            for t in range(6)
            for r in range(8 * t, 8 * t + w // HEAD_DIM, per)
        ]
        lines.append(jnp.zeros((MORE - len(lines), w), F32))
        do2[i, rows:, :] = jnp.concatenate(lines, axis=0).astype(BF)
    g2 = nt(jnp.concatenate(flat, axis=0), wo[...]).astype(BF)
    do2[:, :rows, :] = g2.reshape(k, rows, w)

    @pl.when(step == 0)
    def _():
        gain_grad[...] = gacc

    @pl.when(step != 0)
    def _():
        gain_grad[...] += gacc


def grad_two(at, head, h2, dn_a, dn_b, cot, gain, wo, o2t, lse, k, after=()):
    pages, rows, d = h2.shape
    w = wo.shape[0]
    return call(
        grad_two_kernel,
        (pages // k,),
        [
            paged(h2, k), paged(dn_a, k), paged(dn_b, k), paged((cot, at), k), whole(gain), whole(wo),
            paged(o2t, k), paged(lse, k),
        ],
        [
            out_paged((pages, rows, d), F32, k), out_paged((pages, rows, d), BF, k),
            out_paged((pages, rows + MORE, w), BF, k), out_whole((8, d), F32),
        ],
        scalars=(head,),
        us=5.6, after=after,
    )


def grad_q_kernel(nparts, *refs):
    parts = refs[:nparts]
    wq, dq2, dn2 = refs[nparts:]
    k, w, rows = parts[0].shape
    flat = []
    for i in range(k):
        acc = parts[0][i].astype(F32)
        for p in parts[1:]:
            acc = acc + p[i].astype(F32)
        dq = jnp.transpose(acc).astype(BF)
        dq2[i] = dq
        flat.append(dq)
    dn = nt(jnp.concatenate(flat, axis=0), wq[...])
    dn2[...] = dn.astype(BF).reshape(dn2.shape)


def grad_q(parts, wq, k, after=()):
    pages, w, rows = parts[0].shape
    d = wq.shape[0]
    return call(
        functools.partial(grad_q_kernel, len(parts)),
        (pages // k,),
        [paged(p, k) for p in parts] + [whole(wq)],
        [out_paged((pages, rows, w), BF, k), out_paged((pages, rows, d), BF, k)],
        us=4, after=after,
    )


def last_kernel(xo, dn_a, dn_b, dh1, gain, *refs):
    out, gain_grad = refs[-2:]
    acc = None
    for i in range(dh1.shape[0]):
        gg, dv = norm_back(
            xo[i].astype(F32), gain[0:1], dn_a[i].astype(F32) + dn_b[i].astype(F32)
        )
        out[i] = dh1[i] + dv
        part = fold8(gg)
        acc = part if acc is None else acc + part
    gain_grad[...] = acc


def last(at, xo, dn_a, dn_b, dh1, gain, prev=None, after=()):
    pages, half, d = dh1.shape
    return call(
        last_kernel,
        (1,),
        [paged((xo, at), pages), paged(dn_a, pages), paged(dn_b, pages), paged(dh1, pages), whole(gain)]
        + ([] if prev is None else [kept(prev)]),
        [
            (xo.shape, F32, (pages, half, d), lambda i, *_: (at // pages, 0, 0)),
            out_whole((8, d), F32),
        ],
        us=3,
        after=after,
        aliases={} if prev is None else {5: 0},
    )


def branch_ffn_kernel(nc, head, *refs):
    acts, (w_out, keep, send) = refs[:nc], refs[nc:]
    first = head[0] == 0
    for c, act in enumerate(acts):

        @pl.when(pl.program_id(0) == c)
        def _():
            k, rows, units = act.shape
            half = rows // 2
            f = nn(act[...].reshape(k * rows, units), w_out[...])
            f = f.reshape(k, rows, f.shape[1])
            keep[...] = jnp.where(first, f[:, :half], f[:, half:]).astype(BF)
            send[...] = jnp.where(first, f[:, half:], f[:, :half]).astype(BF)


def branch_ffn(head, acts, w_out, after=()):
    k, rows, units = acts[0].shape
    d = w_out.shape[1]
    pages = k * len(acts)
    return call(
        functools.partial(branch_ffn_kernel, len(acts)),
        (len(acts),),
        [whole(a) for a in acts] + [whole(w_out)],
        [out_paged((pages, rows // 2, d), BF, k), out_paged((pages, rows // 2, d), BF, k)],
        scalars=(head,),
        us=7,
        after=after,
    )


def output_kernel(at, head, lens, h2, f_a, f_b, a_a, a_b, c_a, c_b, *refs):
    out, stats = refs[-2:]
    page = pl.program_id(0)
    first = head[0] == 0
    half = f_a.shape[1]

    def mine(ref):
        v = ref[0].astype(F32)
        return jnp.where(first, v[:half], v[half:])

    f = f_a[0].astype(F32) + f_b[0].astype(F32)
    y = mine(h2) + f
    out[0] = y.astype(BF)
    a = mine(a_a) + mine(a_b)
    c = mine(c_a) + mine(c_b)
    row = lax.broadcasted_iota(jnp.int32, (half, 1), 0) + head[0] * half
    valid = (row < lens[page + at]).astype(F32)
    stats[0] = jnp.concatenate(
        [jnp.sum(v * v * valid, axis=0, keepdims=True) for v in (y, a, c, f)]
        + [jnp.zeros((4, y.shape[1]), F32)],
        axis=0,
    )


def output_rows(at, head, lens, h2, f_a, f_b, a_a, a_b, c_a, c_b, prev=None, after=()):
    pages, rows, d = h2.shape
    return call(
        functools.partial(output_kernel, at),
        (pages,),
        [paged(a) for a in (h2, (f_a, at), (f_b, at), (a_a, at), (a_b, at), c_a, c_b)]
        + ([] if prev is None else [kept(prev)]),
        [
            (
                (a_a.shape[0], rows // 2, d), BF, (1, rows // 2, d),
                lambda i, *_: (i + at, 0, 0),
            ),
            out_paged((pages, 8, d), F32),
        ],
        scalars=(head, lens),
        us=1.5 * pages,
        after=after,
        aliases={} if prev is None else {9: 0},
    )


def gate(x):
    return pl.pallas_call(
        lambda *refs: None,
        out_shape=jax.ShapeDtypeStruct(x.shape, x.dtype),
        in_specs=[pl.BlockSpec(memory_space=pl.ANY)] * (1 + len(ORDER)),
        out_specs=pl.BlockSpec(memory_space=pl.ANY),
        input_output_aliases={0: 0},
        cost_estimate=pl.CostEstimate(flops=0, bytes_accessed=0, transcendentals=0),
    )(x, *ORDER)


def kv_kernel(copied, pos, enc, w, *refs):
    if copied:
        kv, copy = refs[-2:]
        copy[...] = enc[...]
    else:
        kv = refs[-1]
    for i in range(enc.shape[0]):
        kv[i] = nn(enc[i], w[...]).astype(BF)


def kv_project(pos, enc, w, slots, k, where, copied=False, prev=None, after=()):
    n, d = enc.shape[1:]
    ins = [paged(enc, k), whole(w)]
    if prev is not None:
        ins += [kept(p) for p in prev]
    widths = [w.shape[1]] + [d] * copied
    return call(
        functools.partial(kv_kernel, copied),
        (enc.shape[0] // k,),
        ins,
        [((slots, n, c), BF, (k, n, c), lambda i, p: (where(i, p), 0, 0)) for c in widths],
        scalars=(pos,),
        us=0.9 * enc.shape[0],
        after=after,
        aliases={} if prev is None else {3 + i: i for i in range(len(prev))},
    )


def limits(pos, group, n):
    length = OCR + PATCH_SMALL + group * (PATCH_LARGE - PATCH_SMALL)
    return length - pos[1] * n, length - (pos[1] + 1 - 2 * pos[6]) * n


def cross_fwd_kernel(at, pos, group, q, kv_a, kv_b, o):
    rows, w = q.shape[1:]
    n = kv_a.shape[1]
    lims = limits(pos, group[pl.program_id(0) + at], n)

    def run(masked):
        rowsum = []
        for t in range(w // PAIR):
            c = slice(t * PAIR, (t + 1) * PAIR)
            cv = slice(w + t * PAIR, w + (t + 1) * PAIR)
            qm = pair_rows(q[0, :, c])
            ss = []
            for j, kv in enumerate((kv_a, kv_b)):
                s = nt(kv[0, :, c], qm)
                if masked:
                    pos = lax.broadcasted_iota(jnp.int32, s.shape, 0)
                    s = jnp.where(pos < lims[j], s, MASKED)
                ss.append(s)
            m = jnp.maximum(*[jnp.max(s, axis=0, keepdims=True) for s in ss])
            es = [jnp.exp(s - m) for s in ss]
            total = sum(jnp.sum(e, axis=0, keepdims=True) for e in es)
            acc = tn(kv_a[0, :, cv], es[0].astype(BF)) + tn(kv_b[0, :, cv], es[1].astype(BF))
            inv = 1.0 / total
            o[0, t * PAIR : t * PAIR + HEAD_DIM, :] = (
                acc[:HEAD_DIM, :rows] * inv[:, :rows]
            ).astype(BF)
            o[0, t * PAIR + HEAD_DIM : (t + 1) * PAIR, :] = (
                acc[HEAD_DIM:, rows:] * inv[:, rows:]
            ).astype(BF)
            row = m + jnp.log(total)
            rowsum += [row[:, :rows], row[:, rows:]]
        rowsum += [jnp.zeros((1, rows), F32)] * (8 - len(rowsum))
        terms = thirds(jnp.concatenate(rowsum, axis=0)) + [jnp.zeros((STATS - 24, rows), BF)]
        o[0, w:, :] = jnp.concatenate([t.astype(F32) for t in terms], axis=0).astype(BF)

    full = (lims[0] >= n) & (lims[1] >= n)
    pl.when(full)(lambda: run(False))
    pl.when(jnp.logical_not(full))(lambda: run(True))


def cross_fwd(pos, group, q, kv_a, kv_b, at, pages, after=()):
    rows, w = q[0].shape[1:]
    return call(
        functools.partial(cross_fwd_kernel, q[1]),
        (pages,),
        [paged(q), paged((kv_a, at)), paged((kv_b, at))],
        [out_paged((pages, w + STATS, rows), BF)],
        scalars=(pos, group),
        us=1.6 * pages,
        after=after,
    )[0]


def cross_bwd_kernel(at, pos, group, q, do, kv_a, kv_b, *refs):
    dq, dkv_a, dkv_b = refs[-3:]
    rows, w = q.shape[1:]
    n = kv_a.shape[1]
    lims = limits(pos, group[pl.program_id(0) + at], n)
    per = w // rows
    lines = w // HEAD_DIM // per
    stats = do[0, rows:, :].astype(F32)

    def line(first, head):
        at = [first + t * lines + head // per for t in range(3)]
        c = slice(head % per * rows, (head % per + 1) * rows)
        return sum(stats[a : a + 1, c] for a in at)

    def both(first, t):
        return jnp.concatenate([line(first, 2 * t), line(first, 2 * t + 1)], axis=1)

    def run(masked):
        for t in range(w // PAIR):
            c = slice(t * PAIR, (t + 1) * PAIR)
            cv = slice(w + t * PAIR, w + (t + 1) * PAIR)
            qm = pair_rows(q[0, :, c])
            gm = pair_rows(do[0, :rows, c])
            ls, dl = both(0, t), both(3 * lines, t)
            acc = None
            for j, (kv, dkv) in enumerate(((kv_a, dkv_a), (kv_b, dkv_b))):
                k = kv[0, :, c]
                s = nt(k, qm)
                if masked:
                    pos = lax.broadcasted_iota(jnp.int32, s.shape, 0)
                    s = jnp.where(pos < lims[j], s, MASKED)
                p = jnp.exp(s - ls)
                ds = (p * (nt(kv[0, :, cv], gm) - dl)).astype(BF)
                dkv[0, :, c] = nn(ds, qm).astype(BF)
                dkv[0, :, cv] = nn(p.astype(BF), gm).astype(BF)
                part = tn(k, ds)
                acc = part if acc is None else acc + part
            dq[0, t * PAIR : t * PAIR + HEAD_DIM, :] = (acc[:HEAD_DIM, :rows] * SCALE).astype(BF)
            dq[0, t * PAIR + HEAD_DIM : (t + 1) * PAIR, :] = (
                acc[HEAD_DIM:, rows:] * SCALE
            ).astype(BF)

    full = (lims[0] >= n) & (lims[1] >= n)
    pl.when(full)(lambda: run(False))
    pl.when(jnp.logical_not(full))(lambda: run(True))


def cross_bwd(pos, group, q, do, kv_a, kv_b, at, prev=None, after=()):
    pages, _, w = do.shape
    rows = q[0].shape[1]
    n = kv_a.shape[1]
    ins = [paged(a) for a in (q, do, (kv_a, at), (kv_b, at))]
    if prev is not None:
        ins += [kept(p) for p in prev]

    def out(v):
        return (v.shape, BF, (1,) + v.shape[1:], lambda i, *_: (i + at, 0, 0))

    return call(
        functools.partial(cross_bwd_kernel, q[1]),
        (pages,),
        ins,
        [out_paged((pages, w, rows), BF), out(kv_a), out(kv_b)],
        scalars=(pos, group),
        us=2.4 * pages,
        after=after,
        aliases={} if prev is None else {6: 1, 7: 2},
    )


def enc_back_kernel(head, dkv, enc, w, prev, keep, send, dw):
    low = head[0] == 0
    part = keep.shape[-1]

    @pl.when(pl.program_id(0) == 0)
    def _():
        dw[...] = prev[...]

    for j in range(dkv.shape[0]):
        term = nt(dkv[j], w[...])
        lo, hi = term[:, :part], term[:, part:]
        keep[j] = jnp.where(low, lo, hi).astype(BF)
        send[j] = jnp.where(low, hi, lo).astype(BF)
        dw[...] += tn(enc[j], dkv[j])


def enc_back(head, dkv, enc, w, prev, k, after=()):
    slots, n, w2 = dkv.shape
    d = w.shape[0]
    part = d // 2
    return call(
        enc_back_kernel,
        (slots // k,),
        [paged(dkv, k), paged(enc, k), whole(w), whole(prev)],
        [
            out_paged((slots, n, part), BF, k), out_paged((slots, n, part), BF, k),
            out_whole((d, w2), F32),
        ],
        scalars=(head,),
        us=1.7 * slots,
        after=after,
    )


def add_pages_kernel(a, b, out):
    out[...] = (a[...].astype(F32) + b[...].astype(F32)).astype(BF)


def add_pages(at, pages, a, b, k, after=()):
    return call(
        add_pages_kernel,
        (pages // k,),
        [paged((a, at), k), paged((b, at), k)],
        [out_paged((pages,) + a.shape[1:], BF, k)],
        us=0.7 * pages,
        after=after,
    )[0]


def swap(x, axis, mask, size):
    return lax.ppermute(x, axis, [(i, i ^ mask) for i in range(size)])


def pick(bit, a, b):
    return jnp.where(bit == 0, b, a), jnp.where(bit == 0, a, b)


def rows_of(refs):
    return jnp.concatenate([r[...] for r in refs], axis=0) if len(refs) > 1 else refs[0][...]


def grads_wide_kernel(nc, bits, *refs):
    act, n3, du = (refs[j * nc : (j + 1) * nc] for j in range(3))
    cot, send_a, keep_a, send_b, keep_b = refs[3 * nc :]
    i = pl.program_id(0)
    for lo, out in ((0, send_a), (2, keep_a)):

        @pl.when((i >= lo) & (i < lo + 2))
        def _():
            out[...] = tn(rows_of(act), cot[...]).astype(BF)

    for lo, out in ((4, send_b), (6, keep_b)):

        @pl.when((i >= lo) & (i < lo + 2))
        def _():
            out[...] = tn(rows_of(n3), rows_of(du)).astype(BF)


def flat_rows(v):
    return v.reshape(-1, v.shape[-1])


def grads_wide(bits, act, cot, n3, du, after=()):
    act, n3, du = ([flat_rows(v) for v in c] for c in (act, n3, du))
    cot = flat_rows(cot)
    rows, units, d = act[0].shape[0], act[0].shape[1], cot.shape[1]
    blk = units // 4

    def quarter_a(i, t):
        j = jnp.minimum(i, 3)
        side = jnp.where(j < 2, 1 - t[2], t[2])
        return (0, 2 * side + j % 2)

    def side_b(i, t):
        return (0, jnp.where(jnp.maximum(i, 4) < 6, 1 - t[3], t[3]))

    def out(lo):
        return ((2 * blk, d), BF, (blk, d), lambda i, t: (jnp.clip(i - lo, 0, 1), 0))

    return call(
        functools.partial(grads_wide_kernel, len(act)),
        (8,),
        [(v, (rows, blk), quarter_a) for v in act]
        + [(v, (rows, d // 2), lambda i, t: (0, jnp.maximum(i, 4) % 2)) for v in n3]
        + [(v, (rows, units // 2), side_b) for v in du]
        + [whole(cot)],
        [out(0), out(2), out(4), out(6)],
        scalars=(bits,),
        us=10,
        after=after,
    )


def stacked(v):
    c = v.shape[1] // 2
    return jnp.concatenate([v[:, :c], v[:, c:]], axis=0)


def grads_self_kernel(nc, bits, n, o, *refs):
    dq, dk, dv, g = (rows_of(refs[j * nc : (j + 1) * nc]) for j in range(4))
    send_a, keep_a, send_b, keep_b = refs[-4:]
    turned = jnp.transpose(n[...])
    send_a[...], keep_a[...] = pick(bits[2], nn(turned, dq).astype(BF), nn(turned, dk).astype(BF))
    ot = stacked(tn(o[...], g).astype(BF))
    send_b[...], keep_b[...] = pick(bits[3], nn(turned, dv).astype(BF), ot)


def grads_cross_kernel(nc, bits, n, dw, *refs):
    dq, o, g = (rows_of(refs[j * nc : (j + 1) * nc]) for j in range(3))
    send_a, keep_a, send_b, keep_b = refs[-4:]
    w = dq.shape[1]
    send_a[...], keep_a[...] = pick(bits[2], tn(n[...], dq).astype(BF), dw[:, :w].astype(BF))
    ot = stacked(tn(o, g).astype(BF))
    send_b[...], keep_b[...] = pick(bits[3], dw[:, w:].astype(BF), ot)


def grads_tall(kernel, bits, arrays, chunked, d, w, us, after=()):
    flat = [flat_rows(v) for v in arrays] + [flat_rows(v) for c in chunked for v in c]
    return call(
        functools.partial(kernel, len(chunked[0])),
        (1,),
        [whole(v) for v in flat],
        [out_whole((d, w), BF)] * 4,
        scalars=(bits,),
        us=us,
        after=after,
    )


def sum_one_kernel(bits, keep_a, got_a, keep_b, got_b, send_a, next_a, send_b, next_b):
    blk = send_a.shape[0]
    for keep, got, send, nxt, bit in (
        (keep_a, got_a, send_a, next_a, bits[3]), (keep_b, got_b, send_b, next_b, bits[2])
    ):
        lo = keep[:blk].astype(F32) + got[:blk].astype(F32)
        hi = keep[blk:].astype(F32) + got[blk:].astype(F32)
        s, k = pick(bit, lo, hi)
        send[...] = s.astype(BF)
        nxt[...] = k.astype(BF)


def sum_two_kernel(keep_a, got_a, keep_b, got_b, out):
    nz, part = out.shape[0], out.shape[1] // 2
    sides = ((0, keep_a, got_a), (part, keep_b, got_b))
    for first, keep, got in sides:
        total = keep[...].astype(F32) + got[...].astype(F32)
        for z in range(nz):
            out[z, first : first + part] = total[z * part : (z + 1) * part].astype(BF)


def sum_three_kernel(got, out):
    nz = got.shape[0]
    total = sum(got[z].astype(F32) for z in range(nz)).astype(BF)
    for z in range(nz):
        out[z] = total


def join_kernel(got, out_a, out_b):
    nz, part = got.shape[0], got.shape[1] // 2
    for first, out in ((0, out_a), (part, out_b)):
        out[...] = jnp.concatenate(
            [got[z, first : first + part].astype(F32) for z in range(nz)], axis=0
        ).astype(BF)


def reduce_bucket(parts, bits, nz):
    send_a, keep_a, send_b, keep_b = parts
    blk, c = send_a.shape[0] // 2, send_a.shape[1]
    piece = (nz, 2 * blk // nz, c)
    fast = c / 384

    def x(v):
        return swap(v, "dp", 1, 4)

    def y(v):
        return swap(v, "dp", 2, 4)

    def over_seq(v):
        return lax.all_to_all(v, "seq", 0, 0, tiled=True)

    got_a, got_b = x(send_a), y(send_b)
    yield
    send_a, keep_a, send_b, keep_b = call(
        sum_one_kernel, (1,), [whole(v) for v in (keep_a, got_a, keep_b, got_b)],
        [out_whole((blk, c), BF)] * 4, scalars=(bits,), us=2 * fast,
    )
    got_a, got_b = y(send_a), x(send_b)
    yield
    (out,) = call(
        sum_two_kernel, (1,), [whole(v) for v in (keep_a, got_a, keep_b, got_b)],
        [out_whole(piece, BF)], us=1.5 * fast,
    )
    got = over_seq(out)
    yield
    (out,) = call(sum_three_kernel, (1,), [whole(got)], [out_whole(piece, BF)], us=1.5)
    got = over_seq(out)
    yield
    a0, b0 = call(join_kernel, (1,), [whole(got)], [out_whole((blk, c), BF)] * 2, us=1.5 * fast)
    a1, b1 = y(a0), x(b0)
    a2, b2 = x(a0), y(b0)
    yield [a0, a1, a2, x(a1), b0, b1, b2, y(b1)]


def final_kernel(outs, pos, *refs):
    pieces, results = refs[:8], refs[8:]
    t = pl.program_id(0)
    for half, (hi, lo) in enumerate(((pos[2], pos[3]), (pos[3], pos[2]))):
        rel = (t // 2 + hi) % 2 * 2 + (t % 2 + lo) % 2
        for j in range(4):
            for r, (at, first, count) in zip(results, outs):
                if at != half:
                    continue

                @pl.when((rel == j) & (t >= first) & (t < first + count))
                def _():
                    r[...] = pieces[4 * half + j][...].astype(F32)


def final(pieces, pos, outs, us, after=()):
    blk, c = pieces[0].shape

    def index(first, count, where):
        return lambda t, *_: where(jnp.clip(t - first, 0, count - 1))

    return call(
        functools.partial(final_kernel, [(o[1], o[2], o[3]) for o in outs]),
        (4,),
        [whole(p) for p in pieces],
        [(o[0], F32, (blk, c), index(o[2], o[3], o[4])) for o in outs],
        scalars=(pos,),
        us=us,
        after=after,
    )


def add_kernel(a, b, out):
    out[...] = a[...] + b[...]


def add_small(a, b):
    return call(add_kernel, (1,), [whole(a), whole(b)], [out_whole(a.shape, F32)], us=1)[0]


def place_kernel(pos, a, b, out):
    out[...] = (a[...].astype(F32) + b[...].astype(F32)).astype(BF)


def keep_kernel(pos, a, prev, out):
    out[...] = a[...]


def place_sum(pos, a, b, pages, k, where):
    n, c = a.shape[1:]
    return call(
        place_kernel,
        (a.shape[0] // k,),
        [paged(a, k), paged(b, k)],
        [((pages, n, c), BF, (k, n, c), lambda i, p: (where(i, p), 0, 0))],
        scalars=(pos,),
        us=1.2 * a.shape[0] // k,
    )[0]


def place_more(pos, a, so_far, k, where):
    n, c = a.shape[1:]
    return call(
        keep_kernel,
        (a.shape[0] // k,),
        [paged(a, k), kept(so_far)],
        [(so_far.shape, BF, (k, n, c), lambda i, p: (where(i, p), 0, 0))],
        scalars=(pos,),
        us=1.5 * a.shape[0] // k,
        aliases={2: 0},
    )[0]


def per_device(
    sizes,
    dec_input,
    enc_states,
    page_group,
    target_mask,
    rel_buckets,
    self_gain,
    cross_gain,
    ffn_gain,
    self_q,
    self_k,
    self_v,
    self_o,
    rel_table,
    cross_q_w,
    cross_k,
    cross_v,
    cross_o,
    ff_in,
    ff_out,
    cotangent,
):
    n_seq = sizes["seq"]
    pages, half, d = dec_input.shape
    n = enc_states.shape[1]
    w = self_q.shape[1]
    nb = n_seq // 2
    slots = nb * pages
    k = 3
    chunks = pages // k
    ORDER.clear()
    s = lax.axis_index("seq")
    h = lax.axis_index("head")
    dp = lax.axis_index("dp")
    block, par = s // 2, s % 2
    pos = jnp.stack(
        [v.astype(jnp.int32) for v in (h, s, dp % 2, dp // 2, dp, block, par)]
    )
    head = bits = pos

    def arrived(late, c):
        return lambda i, p: (
            (i // k + late * (nb // 2) + p[0] * (nb // 2) + nb - p[5]) % nb * pages + c * k + i % k
        )

    def out_group(first, other):
        def where(i, p):
            kk, c = (i + first) // chunks, (i + first) % chunks
            side = 1 - p[6] if other else p[6]
            return ((p[5] + kk) % nb * 2 + side) * chunks + c

        return where

    def head_swap(x):
        return swap(x, "head", 1, 2)

    def rolled(x, step):
        perm = [(2 * b + r, 2 * ((b - step) % nb) + r) for b in range(nb) for r in range(2)]
        return lax.ppermute(x, "seq", perm) if step % nb else x

    def owners(x):
        return [rolled(x, step) for step in range(nb)]

    others = list(range(1, nb))
    both = range(chunks)

    x_other = head_swap(dec_input)
    enc_t = jnp.transpose(enc_states, (1, 0, 2))

    def some_pages(at):
        return jnp.transpose(lax.dynamic_slice_in_dim(enc_t, at, pages, 1), (1, 0, 2))

    away = [some_pages(((h * (nb // 2) + i) * 2 + 1 - par) * pages) for i in range(nb // 2)]
    away = [
        jnp.concatenate([v[c * k : (c + 1) * k] for v in away], axis=0) for c in both
    ]
    enc_in = [swap(v, "seq", 1, n_seq) for v in away]
    cot_other = head_swap(cotangent)
    cot = jnp.concatenate(
        [jnp.where(h == 0, cotangent, cot_other), jnp.where(h == 0, cot_other, cotangent)], axis=1
    )
    page_groups = owners(page_group)
    lens = jnp.sum(target_mask, axis=1).astype(jnp.int32)
    table = jnp.pad(rel_table.T, ((0, 8 - rel_table.shape[1]), (0, 128 - rel_table.shape[0])))
    gains = jnp.stack([self_gain, cross_gain, ffn_gain])
    w_kv = jnp.concatenate([cross_k, cross_v], axis=1)

    xf, n1, qkv, o1, lse1, a_part = self_fwd(
        head, lens, dec_input, x_other, gains, self_q, self_k, self_v, self_o, rel_buckets, table,
        after=(*away, *page_groups[1:], cot_other),
    )
    a_other = head_swap(a_part)
    h1, n2, q2, zero = cross_q(xf, a_part, a_other, gains, cross_q_w, k)
    qs = owners(q2)
    direct = gate(enc_in[0])
    arriving = [[direct, head_swap(direct)]]
    enc_own = jnp.concatenate(
        [some_pages((((block + i) % nb) * 2 + par) * pages + zero[0, 0]) for i in range(nb)], axis=0
    )
    (kv_a,) = kv_project(pos, enc_own, w_kv, slots, k, lambda i, p: i)
    os = [[None] * chunks for _ in range(nb)]
    rec = None

    def attend(j, c):
        o = cross_fwd(
            pos, page_groups[j], (qs[j], c * k), kv_a, kv_b, j * pages + c * k, k
        )
        os[j][c] = rolled(o, -j)

    for c in both:
        if c:
            direct = gate(enc_in[c])
            arriving.append([direct, head_swap(direct)])
        for late, part in enumerate(arriving[c]):
            rec = kv_project(
                pos, part, w_kv, slots, 1, arrived(late, c), copied=True, prev=rec
            )
        kv_b, enc_rec = rec
        if c == chunks - 1:
            for e in range(max(c - 1, 0), chunks):
                for j in others:
                    attend(j, e)
        elif c:
            for j in others:
                attend(j, c - 1)
        attend(0, c)

    o2, o2t, lse2, c_part, c_other = ([None] * chunks for _ in range(5))
    h2, n3, act, du, dn3, dn3_other = ([None] * chunks for _ in range(6))
    dh2, dcr, gain3, dos = ([None] * chunks for _ in range(4))
    dqs = [[None] * chunks for _ in range(nb)]
    dkv = None

    def mix(c):
        o2[c], o2t[c], lse2[c], c_part[c] = combine(
            [v[c] for v in os], cross_o, k
        )
        c_other[c] = head_swap(c_part[c])

    def feed(c):
        h2[c], n3[c], act[c], du[c], dn3[c] = ffn(
            c * k, h1, c_part[c], c_other[c], cot, gains, ff_in, ff_out, k
        )
        dn3_other[c] = head_swap(dn3[c])

    def turn(c):
        dh2[c], dcr[c], do2, gain3[c] = grad_two(
            c * k, head, h2[c], dn3[c], dn3_other[c], cot, gains, cross_o, o2t[c], lse2[c], k
        )
        dos[c] = owners(do2)

    def back(j, c):
        nonlocal dkv
        dqs[j][c], *dkv = cross_bwd(
            pos, page_groups[j], (qs[j], c * k), dos[c][j], kv_a, kv_b,
            j * pages + c * k, prev=dkv,
        )
        dqs[j][c] = rolled(dqs[j][c], -j)

    mix(0)
    feed(0)
    for c in both[1:]:
        mix(c)
        turn(c - 1)
        feed(c)
        if c == chunks - 1:
            grads_ffn = reduce_bucket(grads_wide(bits, act, cot, n3, du), bits, n_seq)
            next(grads_ffn)
            turn(c)
        back(0, c - 1)
    for c in both[:-1]:
        for j in others:
            back(j, c)
    for j in [0] + others:
        if j == nb - 1:
            next(grads_ffn)
        back(j, chunks - 1)

    keep_b, send_b, dw = enc_back(
        head, dkv[1], enc_rec, w_kv, jnp.zeros((d, 2 * w), F32), k
    )
    send_b = head_swap(send_b)
    dq2, dn2, dn2_other = ([None] * chunks for _ in range(3))
    for c in both:
        dq2[c], dn2[c] = grad_q([v[c] for v in dqs], cross_q_w, k)
        dn2_other[c] = head_swap(dn2[c])
        if c == chunks - 1:
            next(grads_ffn)
    quarter = slots // 4
    spans = [(0, 2 * quarter), (2 * quarter, quarter), (3 * quarter, quarter)]
    enc_away = []

    def send_away():
        at, count = spans[len(enc_away)]
        enc_away.append(
            swap(add_pages(at, count, keep_b, send_b, k), "seq", 1, n_seq)
        )

    keep_a, send_a, dw = enc_back(head, dkv[0], enc_own, w_kv, dw, k, after=(send_b,))
    send_away()
    send_a = head_swap(send_a)
    grads_cross = reduce_bucket(
        grads_tall(grads_cross_kernel, bits, [n2, dw], [dq2, o2, dcr], d, w, 6), bits, n_seq
    )
    next(grads_cross)
    next(grads_ffn)
    backs = []
    dn1_other = []
    for c in both:
        backs.append(
            self_bwd(
                c * k, head, lens, h1, dn2[c], dn2_other[c], dh2[c], gains, self_q, self_k,
                self_v, self_o, rel_buckets, table, qkv, lse1,
            )
        )
        dn1_other.append(head_swap(backs[c][7]))
        if c == 0:
            next(grads_cross)
    dh1, dar, dq1, dk1, dv1, ds1, dn1, _, gain2 = zip(*backs)
    next(grads_cross)
    send_away()
    grads_self = reduce_bucket(
        grads_tall(
            grads_self_kernel, bits, [n1, o1], [dq1, dk1, dv1, dar], d, w, 7,
            after=(*dn1_other[:1], send_a),
        ),
        bits, n_seq,
    )
    next(grads_self)
    f_keep, f_send = branch_ffn(head, act, ff_out, after=dn1_other)
    f_other = head_swap(f_send)
    enc_out = place_sum(pos, keep_a, send_a, 2 * slots, k, out_group(0, False))
    enc_out = place_more(pos, enc_away[0], enc_out, k, out_group(0, True))
    next(grads_self)
    sums_ffn = next(grads_ffn)
    input_grad, gain1 = None, []
    for c in both:
        input_grad, g = last(
            c * k, dec_input, dn1[c], dn1_other[c], dh1[c], gains, prev=input_grad
        )
        gain1.append(g)
    next(grads_self)
    next(grads_cross)
    tables = [table_grad(ds1[c], rel_buckets, c * k) for c in both]
    enc_out = place_more(pos, enc_away[1], enc_out, k, out_group(spans[1][0] // k, True))
    next(grads_self)
    send_away()
    output, squares = None, []
    for c in both:
        output, sq = output_rows(
            c * k, head, lens, h2[c], f_keep, f_other, a_part, a_other, c_part[c],
            c_other[c], prev=output,
        )
        squares.append(sq)
    units = ff_in.shape[1]
    row, col = (lambda v: (v, 0)), (lambda v: (0, v))
    ff_out_grad, ff_in_grad = final(
        sums_ffn, pos,
        [((units, d), 0, 0, 4, row), ((d, units), 1, 0, 4, lambda v: (v % 2, v // 2))], 6,
    )
    sums_cross = next(grads_cross)
    sums_self = next(grads_self)

    squares = jnp.sum(jnp.concatenate(squares, axis=0)[:, :4], axis=-1)

    def line(v):
        return jnp.pad(v.reshape(1, -1), ((0, 0), (0, d - v.size)))

    small = jnp.concatenate(
        [jnp.sum(sum(g), axis=0)[None] for g in (gain1, gain2, gain3)] + [line(squares)], axis=0
    )
    small_other = head_swap(small)
    small = add_small(small, small_other)
    rms_stats = jnp.sqrt(small[3, : pages * 4].reshape(pages, 4) / (lens.astype(F32) * d)[:, None])
    table_part = sum(tables)
    small = jnp.concatenate([small[:3], line(table_part)], axis=0)
    steps = [(axis, 1 << i) for axis in ("dp", "seq") for i in range(sizes[axis].bit_length() - 1)]
    four = [
        ((d, w), 0, 0, 2, row), ((d, w), 0, 2, 2, row), ((d, w), 1, 0, 2, row), ((w, d), 1, 2, 2, col)
    ]
    for step, (axis, mask) in enumerate(steps):
        other = swap(small, axis, mask, sizes[axis])
        if step == 1:
            enc_out = place_more(
                pos, enc_away[2], enc_out, k, out_group(spans[2][0] // k, True)
            )
        if step == 2:
            cq, ck, cv, co = final(sums_cross, pos, four, 5)
        small = add_small(small, other)
    table_sum = small[3, : table_part.size].reshape(table_part.shape)
    enc_grad = with_layout_constraint(
        jnp.transpose(enc_out, (1, 0, 2)).astype(F32), Layout((0, 1, 2))
    )
    enc_grad = jnp.transpose(enc_grad, (1, 0, 2))
    sq, sk, sv, so = final(sums_self, pos, four, 5)

    return (
        output, input_grad, enc_grad, small[0], small[1], small[2], sq, sk, sv, so, table_sum.T,
        cq, ck, cv, co, ff_in_grad, ff_out_grad, rms_stats,
    )


def solution(mesh):
    sizes = dict(mesh.shape)
    rows = P(("dp", "seq"), "head", None)
    cols, tall = P(None, "head"), P("head", None)
    placed = (
        rows, P("dp", "seq", None), P(("dp", "seq")), P(("dp", "seq"), None),
        P(("dp", "seq"), None, None), P(), P(), P(), cols, cols, cols, tall, cols, cols, cols, cols,
        tall, cols, tall, rows,
    )
    return jax.shard_map(
        functools.partial(per_device, sizes),
        mesh=mesh,
        in_specs=placed,
        out_specs=(
            rows, rows, P("dp", "seq", "head"), P(), P(), P(), cols, cols, cols, tall, cols, cols,
            cols, cols, tall, cols, tall, P(("dp", "seq"), None),
        ),
        check_vma=False,
    )
```

```python
import functools
import math

import jax
import jax.numpy as jnp
from jax import lax
from jax.experimental import pallas as pl
from jax.experimental.layout import Layout, with_layout_constraint
from jax.experimental.pallas import tpu as pltpu
from jax.sharding import PartitionSpec as P

HEAD_DIM = 64
OCR = 512
PATCH_SMALL = 196
PATCH_LARGE = 784
EPSILON = 1e-06
MASKED = -1000000000.0
BF = jnp.bfloat16
F32 = jnp.float32
SCALE = HEAD_DIM ** (-0.5)
ROOM = 14 * 1024 * 1024
PAIR = 2 * HEAD_DIM


def nn(a, b):
    return lax.dot_general(a, b, (((1,), (0,)), ((), ())), preferred_element_type=F32)


def nt(a, b):
    return lax.dot_general(a, b, (((1,), (1,)), ((), ())), preferred_element_type=F32)


def tn(a, b):
    return lax.dot_general(a, b, (((0,), (0,)), ((), ())), preferred_element_type=F32)


ORDER = []


def call(body, grid, ins, outs, *, us, scalars=(), scratch=(), after=(), aliases={}):
    held = [a for a, _, _ in ins]
    after = [t for t in [*after, *ORDER] if not any(t is a for a in held)]
    first, last = len(scalars) + len(ins), len(scalars) + len(ins) + len(after)

    def run(*refs):
        body(*refs[:first], *refs[last:])

    spec = pltpu.PrefetchScalarGridSpec(
        num_scalar_prefetch=len(scalars),
        grid=grid,
        in_specs=[pl.BlockSpec(b, m) for _, b, m in ins]
        + [pl.BlockSpec(memory_space=pl.ANY)] * len(after),
        out_specs=[pl.BlockSpec(b, m) for _, _, b, m in outs],
        scratch_shapes=list(scratch),
    )
    blocks = [(b, a.dtype) for a, b, _ in ins] + [(b, t) for _, t, b, _ in outs]
    held = sum(2 * math.prod(b) * jnp.dtype(t).itemsize for b, t in blocks)
    held += sum(math.prod(v.shape) * jnp.dtype(v.dtype).itemsize for v in scratch)
    results = pl.pallas_call(
        run,
        grid_spec=spec,
        out_shape=[jax.ShapeDtypeStruct(s, d) for s, d, _, _ in outs],
        compiler_params=pltpu.CompilerParams(
            vmem_limit_bytes=max(held + ROOM, 46 * 1024 * 1024), dimension_semantics=("arbitrary",) * len(grid)
        ),
        cost_estimate=pl.CostEstimate(flops=int(us * 1e10), bytes_accessed=0, transcendentals=0),
        input_output_aliases=aliases,
    )(*scalars, *[a for a, _, _ in ins], *after)
    ORDER[:] = [min(results, key=lambda r: r.size)]
    return results


def whole(a):
    n = a.ndim
    return (a, a.shape, lambda *_: (0,) * n)


def paged(a, k=1):
    a, at = a if isinstance(a, tuple) else (a, 0)
    n = a.ndim
    return (a, (k,) + a.shape[1:], lambda i, *_: (i + at // k,) + (0,) * (n - 1))


def kept(a):
    n = a.ndim
    return (a, (1,) * (n - 2) + (8, 128), lambda *_: (0,) * n)


def out_paged(shape, dtype, k=1):
    n = len(shape)
    return (shape, dtype, (k,) + tuple(shape[1:]), lambda i, *_: (i,) + (0,) * (n - 1))


def out_whole(shape, dtype):
    n = len(shape)
    return (shape, dtype, tuple(shape), lambda *_: (0,) * n)


def inv_rms(v):
    return lax.rsqrt(jnp.mean(v * v, axis=-1, keepdims=True) + EPSILON)


def pair_rows(block):
    lane = lax.broadcasted_iota(jnp.int32, (1, PAIR), 1)
    low = (lane < HEAD_DIM).astype(F32).astype(block.dtype)
    return jnp.concatenate([block * low, block * (1 - low)], axis=0)


def thirds(v):
    hi = v.astype(BF)
    rest = v - hi.astype(F32)
    mid = rest.astype(BF)
    return [hi, mid, (rest - mid.astype(F32)).astype(BF)]


def joined(hi, mid, lo):
    return hi.astype(F32) + mid.astype(F32) + lo.astype(F32)


STATS = 32
MORE = 32


def two_rows(ref_rows, t):
    return jnp.concatenate([ref_rows[2 * t : 2 * t + 1, :], ref_rows[2 * t + 1 : 2 * t + 2, :]], axis=1)


def norm_back(v, gain, dn):
    inv = inv_rms(v)
    weighted = dn * gain
    inner = jnp.mean(weighted * v, axis=-1, keepdims=True)
    return dn * v * inv, inv * weighted - v * (inv * inv * inv * inner)


def fold8(v):
    return jnp.sum(v.reshape(v.shape[0] // 8, 8, v.shape[1]), axis=0)


def self_bias(buckets_ref, table_ref, heads):
    idx = jnp.transpose(buckets_ref[0])
    rows = []
    for h in range(heads):
        tab = jnp.broadcast_to(table_ref[h : h + 1, :], idx.shape)
        rows.append(jnp.take_along_axis(tab, idx, axis=1))
    return rows


def self_allowed(length, rows):
    key = lax.broadcasted_iota(jnp.int32, (rows, rows), 0)
    query = lax.broadcasted_iota(jnp.int32, (rows, rows), 1)
    ok = (key <= query) & (key < length)
    return jnp.concatenate([ok, ok], axis=1)


def self_fwd_kernel(
    head, lens, xo, xr, gain, wq, wk, wv, wo, buckets, table, xf, n1, qkv, o1, lse, a_part
):
    page = pl.program_id(0)
    first = head[0] == 0
    own, rec = xo[0].astype(F32), xr[0].astype(F32)
    x = jnp.concatenate([jnp.where(first, own, rec), jnp.where(first, rec, own)], axis=0)
    xf[0] = x.astype(BF)
    n = (x * inv_rms(x) * gain[0:1]).astype(BF)
    n1[0] = n
    w = wq.shape[1]
    q = (nn(n, wq[...]).astype(BF).astype(F32) * SCALE).astype(BF)
    k = nn(n, wk[...]).astype(BF)
    v = nn(n, wv[...]).astype(BF)
    qkv[0, :, 0:w] = q
    qkv[0, :, w : 2 * w] = k
    qkv[0, :, 2 * w : 3 * w] = v
    rows = x.shape[0]
    bias = self_bias(buckets, table, w // HEAD_DIM)
    ok = self_allowed(lens[page], rows)
    lses, outs = [], []
    for t in range(w // PAIR):
        c = slice(t * PAIR, (t + 1) * PAIR)
        s = nt(k[:, c], pair_rows(q[:, c])) + jnp.concatenate(bias[2 * t : 2 * t + 2], axis=1)
        s = jnp.where(ok, s, MASKED)
        m = jnp.max(s, axis=0, keepdims=True)
        e = jnp.exp(s - m)
        total = jnp.sum(e, axis=0, keepdims=True)
        p = e * (1.0 / total)
        o = tn(p.astype(BF), v[:, c])
        lane = lax.broadcasted_iota(jnp.int32, (rows, PAIR), 1)
        outs.append(jnp.where(lane < HEAD_DIM, o[:rows], o[rows:]))
        row = m + jnp.log(total)
        lses += [row[:, :rows], row[:, rows:]]
    lses += [jnp.zeros((1, rows), F32)] * (8 - len(lses))
    lse[0] = jnp.concatenate(lses, axis=0)
    o = jnp.concatenate(outs, axis=1).astype(BF)
    o1[0] = o
    a_part[0] = nn(o, wo[...]).astype(BF)


def self_fwd(head, lens, xo, xr, gain, wq, wk, wv, wo, buckets, table, after=()):
    pages, half, d = xo.shape
    rows, w = 2 * half, wq.shape[1]
    return call(
        self_fwd_kernel,
        (pages,),
        [
            paged(xo), paged(xr), whole(gain), whole(wq), whole(wk), whole(wv), whole(wo),
            paged(buckets), whole(table),
        ],
        [
            out_paged((pages, rows, d), BF), out_paged((pages, rows, d), BF),
            out_paged((pages, rows, 3 * w), BF), out_paged((pages, rows, w), BF),
            out_paged((pages, 8, rows), F32), out_paged((pages, rows, d), BF),
        ],
        scalars=(head, lens),
        us=10, after=after,
    )


def self_bwd_kernel(
    at, head, lens, h1, dn_a, dn_b, dh2, gain, wq, wk, wv, wo, buckets, table, qkv, lse,
    dh1, dar_out, dq_out, dk_out, dv_out, ds_out, dn_keep, dn_send, gain_grad,
):
    page = pl.program_id(0)
    first = head[0] == 0
    v1 = h1[0]
    rows = v1.shape[0]
    half = rows // 2
    gg, dv = norm_back(v1, gain[1:2], dn_a[0].astype(F32) + dn_b[0].astype(F32))
    d1 = dh2[0] + dv
    gpart = fold8(jnp.where(first, gg[:half], gg[half:]))

    @pl.when(page == 0)
    def _():
        gain_grad[...] = gpart

    @pl.when(page != 0)
    def _():
        gain_grad[...] += gpart

    dh1[0] = jnp.where(first, d1[:half], d1[half:])
    dar = d1.astype(BF)
    dar_out[0] = dar
    w = wo.shape[0]
    do = nt(dar, wo[...]).astype(BF)
    bias = self_bias(buckets, table, w // HEAD_DIM)
    ok = self_allowed(lens[page + at], rows)
    lane = lax.broadcasted_iota(jnp.int32, (rows, PAIR), 1)
    dqs, dks, dvs = [], [], []
    for t in range(w // PAIR):
        c = slice(t * PAIR, (t + 1) * PAIR)
        q = pair_rows(qkv[0, :, t * PAIR : (t + 1) * PAIR])
        k = qkv[0, :, w + t * PAIR : w + (t + 1) * PAIR]
        v = qkv[0, :, 2 * w + t * PAIR : 2 * w + (t + 1) * PAIR]
        g = pair_rows(do[:, c])
        s = nt(k, q) + jnp.concatenate(bias[2 * t : 2 * t + 2], axis=1)
        s = jnp.where(ok, s, MASKED)
        p = jnp.exp(s - two_rows(lse[0], t))
        dp = nt(v, g)
        ds = (p * (dp - jnp.sum(p * dp, axis=0, keepdims=True))).astype(BF)
        ds_out[0, 2 * t] = ds[:, :rows]
        ds_out[0, 2 * t + 1] = ds[:, rows:]
        dq = tn(ds, k) * SCALE
        dqs.append(jnp.where(lane < HEAD_DIM, dq[:rows], dq[rows:]).astype(BF))
        dks.append(nn(ds, q).astype(BF))
        dvs.append(nn(p.astype(BF), g).astype(BF))
    dq, dk, dvv = (jnp.concatenate(a, axis=1) for a in (dqs, dks, dvs))
    dq_out[0] = dq
    dk_out[0] = dk
    dv_out[0] = dvv
    dn = (nt(dq, wq[...]) + nt(dk, wk[...]) + nt(dvv, wv[...])).astype(BF).astype(F32)
    dn_keep[0] = jnp.where(first, dn[:half], dn[half:]).astype(BF)
    dn_send[0] = jnp.where(first, dn[half:], dn[:half]).astype(BF)


def self_bwd(at, head, lens, h1, dn_a, dn_b, dh2, gain, wq, wk, wv, wo, buckets, table, qkv, lse, after=()):
    pages, rows, d = dh2.shape
    w = wq.shape[1]
    heads = w // HEAD_DIM
    return call(
        functools.partial(self_bwd_kernel, at),
        (pages,),
        [
            paged((h1, at)), paged(dn_a), paged(dn_b), paged(dh2), whole(gain), whole(wq),
            whole(wk), whole(wv), whole(wo), paged((buckets, at)), whole(table), paged((qkv, at)),
            paged((lse, at)),
        ],
        [
            out_paged((pages, rows // 2, d), F32), out_paged((pages, rows, d), BF),
            out_paged((pages, rows, w), BF), out_paged((pages, rows, w), BF),
            out_paged((pages, rows, w), BF), out_paged((pages, heads, rows, rows), BF),
            out_paged((pages, rows // 2, d), BF), out_paged((pages, rows // 2, d), BF),
            out_whole((8, d), F32),
        ],
        scalars=(head, lens),
        us=2.8 * pages,
        after=after,
    )


def table_grad_kernel(ds, buckets, out):
    page = pl.program_id(0)
    idx = jnp.transpose(buckets[0])
    heads = ds.shape[1]
    dsf = [ds[0, h].astype(F32) for h in range(heads)]
    rows = [[] for _ in range(heads)]
    for b in range(32):
        hit = idx == b
        for h in range(heads):
            rows[h].append(jnp.sum(jnp.where(hit, dsf[h], 0.0), axis=0, keepdims=True))
    for h in range(heads):
        part = jnp.concatenate(rows[h], axis=0)

        @pl.when(page == 0)
        def _():
            out[h] = part

        @pl.when(page != 0)
        def _():
            out[h] += part


def table_grad(ds, buckets, at, after=()):
    pages, heads, rows, _ = ds.shape
    (out,) = call(
        table_grad_kernel,
        (pages,),
        [paged(ds), paged((buckets, at))],
        [out_whole((heads, 32, rows), F32)],
        us=9, after=after,
    )
    return jnp.sum(out, axis=-1)


def cross_q_kernel(xf, a_a, a_b, gain, wq, h1, n2, q2, zero):
    zero[...] = jnp.zeros_like(zero)
    k, rows, d = xf.shape
    h = xf[...].astype(F32) + a_a[...].astype(F32) + a_b[...].astype(F32)
    h1[...] = h
    h = h.reshape(k * rows, d)
    n = (h * inv_rms(h) * gain[1:2]).astype(BF)
    n2[...] = n.reshape(k, rows, d)
    q = nn(n, wq[...]).astype(BF).astype(F32) * SCALE
    q2[...] = q.astype(BF).reshape(k, rows, wq.shape[1])


def cross_q(xf, a_a, a_b, gain, wq, k, after=()):
    pages, rows, d = xf.shape
    w = wq.shape[1]
    return call(
        cross_q_kernel,
        (pages // k,),
        [paged(xf, k), paged(a_a, k), paged(a_b, k), whole(gain), whole(wq)],
        [
            out_paged((pages, rows, d), F32, k), out_paged((pages, rows, d), BF, k),
            out_paged((pages, rows, w), BF, k), out_whole((8, 128), jnp.int32),
        ],
        us=4, after=after,
    )


def combine_kernel(nparts, *refs):
    os = refs[:nparts]
    wo, o2, o2t, lse, c_part = refs[nparts:]
    k, w, rows = o2t.shape
    heads = w // HEAD_DIM
    flat = []
    for i in range(k):
        terms = [o[i, w:, :].astype(F32) for o in os]
        ls = [t[:8] + t[8:16] + t[16:24] for t in terms]
        m = ls[0]
        for l in ls[1:]:
            m = jnp.maximum(m, l)
        es = [jnp.exp(l - m) for l in ls]
        total = sum(es[1:], es[0])
        lse[i] = m + jnp.log(total)
        inv = 1.0 / total
        ws = [e * inv for e in es]
        pieces = []
        for h in range(heads):
            r = slice(h * HEAD_DIM, (h + 1) * HEAD_DIM)
            acc = os[0][i, r, :].astype(F32) * ws[0][h : h + 1, :]
            for o, ww in zip(os[1:], ws[1:]):
                acc = acc + o[i, r, :].astype(F32) * ww[h : h + 1, :]
            pieces.append(acc)
        ot = jnp.concatenate(pieces, axis=0)
        o2t[i] = ot.astype(BF)
        o = jnp.transpose(ot).astype(BF)
        o2[i] = o
        flat.append(o)
    c = nn(jnp.concatenate(flat, axis=0), wo[...])
    c_part[...] = c.astype(BF).reshape(c_part.shape)


def combine(os, wo, k, after=()):
    pages, _, rows = os[0].shape
    w, d = wo.shape
    return call(
        functools.partial(combine_kernel, len(os)),
        (pages // k,),
        [paged(o, k) for o in os] + [whole(wo)],
        [
            out_paged((pages, rows, w), BF, k), out_paged((pages, w, rows), BF, k),
            out_paged((pages, 8, rows), F32, k), out_paged((pages, rows, d), BF, k),
        ],
        us=2.7,
        after=after,
    )


def ffn_kernel(h1, c_a, c_b, cot, gain, w_in, w_out, h2, n3, act_out, du_out, dn3):
    k, rows, d = h1.shape
    h = (h1[...] + c_a[...].astype(F32) + c_b[...].astype(F32)).reshape(k * rows, d)
    h2[...] = h.reshape(k, rows, d)
    n = (h * inv_rms(h) * gain[2:3]).astype(BF)
    n3[...] = n.reshape(k, rows, d)
    g = cot[...].reshape(k * rows, d)
    units = w_in.shape[1]
    step = units // 3
    root = 0.7978845608028654
    total = None
    for j in range(0, units, step):
        c = slice(j, j + step)
        u = nn(n, w_in[:, c])
        da = nt(g, w_out[c, :])
        u2 = u * u
        th = jnp.tanh(root * u * (1.0 + 0.044715 * u2))
        half = 0.5 + 0.5 * th
        act_out[:, :, c] = (u * half).astype(BF).reshape(k, rows, step)
        slope = half + (0.5 * root) * u * (1.0 - th * th) * (1.0 + (3 * 0.044715) * u2)
        du = (da * slope).astype(BF)
        du_out[:, :, c] = du.reshape(k, rows, step)
        part = nt(du, w_in[:, c])
        total = part if total is None else total + part
    dn3[...] = total.astype(BF).reshape(k, rows, d)


def ffn(at, h1, c_a, c_b, cot, gain, w_in, w_out, k, after=()):
    pages, rows, d = c_a.shape
    units = w_in.shape[1]
    return call(
        ffn_kernel,
        (pages // k,),
        [
            paged((h1, at), k), paged(c_a, k), paged(c_b, k), paged((cot, at), k), whole(gain), whole(w_in),
            whole(w_out),
        ],
        [
            out_paged((pages, rows, d), F32, k), out_paged((pages, rows, d), BF, k),
            out_paged((pages, rows, units), BF, k), out_paged((pages, rows, units), BF, k),
            out_paged((pages, rows, d), BF, k),
        ],
        us=12, after=after,
    )


def grad_two_kernel(head, h2, dn_a, dn_b, cot, gain, wo, o2t, lse, dh2, dcr_out, do2, gain_grad):
    step = pl.program_id(0)
    k, rows, d = h2.shape
    half = rows // 2
    w = wo.shape[0]
    first = head[0] == 0
    gacc = None
    flat = []
    for i in range(k):
        gg, dv = norm_back(h2[i], gain[2:3], dn_a[i].astype(F32) + dn_b[i].astype(F32))
        part = fold8(jnp.where(first, gg[:half], gg[half:]))
        gacc = part if gacc is None else gacc + part
        g = cot[i].astype(F32) + dv
        dh2[i] = g
        dcr = g.astype(BF)
        dcr_out[i] = dcr
        flat.append(dcr)
        dot = nt(wo[...], dcr).astype(BF).astype(F32) * o2t[i].astype(F32)
        sums = [
            jnp.sum(dot[a : a + HEAD_DIM], axis=0, keepdims=True) for a in range(0, w, HEAD_DIM)
        ]
        sums += [jnp.zeros((1, rows), F32)] * (8 - len(sums))
        terms = thirds(lse[i]) + thirds(jnp.concatenate(sums, axis=0))
        stats = jnp.concatenate([t.astype(F32) for t in terms], axis=0)
        per = w // rows
        lines = [
            jnp.concatenate([stats[r + p : r + p + 1] for p in range(per)], axis=1)
            for t in range(6)
            for r in range(8 * t, 8 * t + w // HEAD_DIM, per)
        ]
        lines.append(jnp.zeros((MORE - len(lines), w), F32))
        do2[i, rows:, :] = jnp.concatenate(lines, axis=0).astype(BF)
    g2 = nt(jnp.concatenate(flat, axis=0), wo[...]).astype(BF)
    do2[:, :rows, :] = g2.reshape(k, rows, w)

    @pl.when(step == 0)
    def _():
        gain_grad[...] = gacc

    @pl.when(step != 0)
    def _():
        gain_grad[...] += gacc


def grad_two(at, head, h2, dn_a, dn_b, cot, gain, wo, o2t, lse, k, after=()):
    pages, rows, d = h2.shape
    w = wo.shape[0]
    return call(
        grad_two_kernel,
        (pages // k,),
        [
            paged(h2, k), paged(dn_a, k), paged(dn_b, k), paged((cot, at), k), whole(gain), whole(wo),
            paged(o2t, k), paged(lse, k),
        ],
        [
            out_paged((pages, rows, d), F32, k), out_paged((pages, rows, d), BF, k),
            out_paged((pages, rows + MORE, w), BF, k), out_whole((8, d), F32),
        ],
        scalars=(head,),
        us=5.6, after=after,
    )


def grad_q_kernel(nparts, *refs):
    parts = refs[:nparts]
    wq, dq2, dn2 = refs[nparts:]
    k, w, rows = parts[0].shape
    flat = []
    for i in range(k):
        acc = parts[0][i].astype(F32)
        for p in parts[1:]:
            acc = acc + p[i].astype(F32)
        dq = jnp.transpose(acc).astype(BF)
        dq2[i] = dq
        flat.append(dq)
    dn = nt(jnp.concatenate(flat, axis=0), wq[...])
    dn2[...] = dn.astype(BF).reshape(dn2.shape)


def grad_q(parts, wq, k, after=()):
    pages, w, rows = parts[0].shape
    d = wq.shape[0]
    return call(
        functools.partial(grad_q_kernel, len(parts)),
        (pages // k,),
        [paged(p, k) for p in parts] + [whole(wq)],
        [out_paged((pages, rows, w), BF, k), out_paged((pages, rows, d), BF, k)],
        us=4, after=after,
    )


def last_kernel(xo, dn_a, dn_b, dh1, gain, *refs):
    out, gain_grad = refs[-2:]
    acc = None
    for i in range(dh1.shape[0]):
        gg, dv = norm_back(
            xo[i].astype(F32), gain[0:1], dn_a[i].astype(F32) + dn_b[i].astype(F32)
        )
        out[i] = dh1[i] + dv
        part = fold8(gg)
        acc = part if acc is None else acc + part
    gain_grad[...] = acc


def last(at, xo, dn_a, dn_b, dh1, gain, prev=None, after=()):
    pages, half, d = dh1.shape
    return call(
        last_kernel,
        (1,),
        [paged((xo, at), pages), paged(dn_a, pages), paged(dn_b, pages), paged(dh1, pages), whole(gain)]
        + ([] if prev is None else [kept(prev)]),
        [
            (xo.shape, F32, (pages, half, d), lambda i, *_: (at // pages, 0, 0)),
            out_whole((8, d), F32),
        ],
        us=3,
        after=after,
        aliases={} if prev is None else {5: 0},
    )


def branch_ffn_kernel(nc, head, *refs):
    acts, (w_out, keep, send) = refs[:nc], refs[nc:]
    first = head[0] == 0
    for c, act in enumerate(acts):

        @pl.when(pl.program_id(0) == c)
        def _():
            k, rows, units = act.shape
            half = rows // 2
            f = nn(act[...].reshape(k * rows, units), w_out[...])
            f = f.reshape(k, rows, f.shape[1])
            keep[...] = jnp.where(first, f[:, :half], f[:, half:]).astype(BF)
            send[...] = jnp.where(first, f[:, half:], f[:, :half]).astype(BF)


def branch_ffn(head, acts, w_out, after=()):
    k, rows, units = acts[0].shape
    d = w_out.shape[1]
    pages = k * len(acts)
    return call(
        functools.partial(branch_ffn_kernel, len(acts)),
        (len(acts),),
        [whole(a) for a in acts] + [whole(w_out)],
        [out_paged((pages, rows // 2, d), BF, k), out_paged((pages, rows // 2, d), BF, k)],
        scalars=(head,),
        us=7,
        after=after,
    )


def output_kernel(at, head, lens, h2, f_a, f_b, a_a, a_b, c_a, c_b, *refs):
    out, stats = refs[-2:]
    half = f_a.shape[1]
    for i in range(f_a.shape[0]):
        f, a, c = (
            u[i].astype(F32) + v[i].astype(F32) for u, v in ((f_a, f_b), (a_a, a_b), (c_a, c_b))
        )
        y = h2[i] + f
        out[i] = y.astype(BF)
        row = lax.broadcasted_iota(jnp.int32, (half, 1), 0) + head[0] * half
        valid = (row < lens[at + i]).astype(F32)
        stats[i] = jnp.concatenate(
            [jnp.sum(v * v * valid, axis=0, keepdims=True) for v in (y, a, c, f)]
            + [jnp.zeros((4, y.shape[1]), F32)],
            axis=0,
        )


def output_rows(at, head, lens, h2, f_a, f_b, a_a, a_b, c_a, c_b, prev=None, after=()):
    pages, rows, d = h2.shape
    half = rows // 2

    def mine(a, first):
        return (a, (pages, half, d), lambda i, p, n: (first // pages, p[0], 0))

    return call(
        functools.partial(output_kernel, at),
        (1,),
        [
            mine(h2, 0), paged((f_a, at), pages), paged((f_b, at), pages), mine(a_a, at),
            mine(a_b, at), mine(c_a, 0), mine(c_b, 0),
        ]
        + ([] if prev is None else [kept(prev)]),
        [
            ((a_a.shape[0], half, d), BF, (pages, half, d), lambda i, *_: (at // pages, 0, 0)),
            out_paged((pages, 8, d), F32, pages),
        ],
        scalars=(head, lens),
        us=3,
        after=after,
        aliases={} if prev is None else {9: 0},
    )


def gate(x):
    return pl.pallas_call(
        lambda *refs: None,
        out_shape=jax.ShapeDtypeStruct(x.shape, x.dtype),
        in_specs=[pl.BlockSpec(memory_space=pl.ANY)] * (1 + len(ORDER)),
        out_specs=pl.BlockSpec(memory_space=pl.ANY),
        input_output_aliases={0: 0},
        cost_estimate=pl.CostEstimate(flops=0, bytes_accessed=0, transcendentals=0),
    )(x, *ORDER)


def kv_kernel(copied, pos, enc, w, *refs):
    if copied:
        kv, copy = refs[-2:]
        copy[...] = enc[...]
    else:
        kv = refs[-1]
    for i in range(enc.shape[0]):
        kv[i] = nn(enc[i], w[...]).astype(BF)


def kv_project(pos, enc, w, slots, k, where, copied=False, prev=None, after=()):
    n, d = enc.shape[1:]
    ins = [paged(enc, k), whole(w)]
    if prev is not None:
        ins += [kept(p) for p in prev]
    widths = [w.shape[1]] + [d] * copied
    return call(
        functools.partial(kv_kernel, copied),
        (enc.shape[0] // k,),
        ins,
        [((slots, n, c), BF, (k, n, c), lambda i, p: (where(i, p), 0, 0)) for c in widths],
        scalars=(pos,),
        us=0.9 * enc.shape[0],
        after=after,
        aliases={} if prev is None else {3 + i: i for i in range(len(prev))},
    )


def limits(pos, group, n):
    length = OCR + PATCH_SMALL + group * (PATCH_LARGE - PATCH_SMALL)
    return length - pos[1] * n, length - (pos[1] + 1 - 2 * pos[6]) * n


def cross_fwd_kernel(at, pos, group, q, kv_a, kv_b, o):
    rows, w = q.shape[1:]
    n = kv_a.shape[1]
    lims = limits(pos, group[pl.program_id(0) + at], n)

    def run(masked):
        rowsum = []
        for t in range(w // PAIR):
            c = slice(t * PAIR, (t + 1) * PAIR)
            cv = slice(w + t * PAIR, w + (t + 1) * PAIR)
            qm = pair_rows(q[0, :, c])
            ss = []
            for j, kv in enumerate((kv_a, kv_b)):
                s = nt(kv[0, :, c], qm)
                if masked:
                    pos = lax.broadcasted_iota(jnp.int32, s.shape, 0)
                    s = jnp.where(pos < lims[j], s, MASKED)
                ss.append(s)
            m = jnp.maximum(*[jnp.max(s, axis=0, keepdims=True) for s in ss])
            es = [jnp.exp(s - m) for s in ss]
            total = sum(jnp.sum(e, axis=0, keepdims=True) for e in es)
            acc = tn(kv_a[0, :, cv], es[0].astype(BF)) + tn(kv_b[0, :, cv], es[1].astype(BF))
            inv = 1.0 / total
            o[0, t * PAIR : t * PAIR + HEAD_DIM, :] = (
                acc[:HEAD_DIM, :rows] * inv[:, :rows]
            ).astype(BF)
            o[0, t * PAIR + HEAD_DIM : (t + 1) * PAIR, :] = (
                acc[HEAD_DIM:, rows:] * inv[:, rows:]
            ).astype(BF)
            row = m + jnp.log(total)
            rowsum += [row[:, :rows], row[:, rows:]]
        rowsum += [jnp.zeros((1, rows), F32)] * (8 - len(rowsum))
        terms = thirds(jnp.concatenate(rowsum, axis=0)) + [jnp.zeros((STATS - 24, rows), BF)]
        o[0, w:, :] = jnp.concatenate([t.astype(F32) for t in terms], axis=0).astype(BF)

    full = (lims[0] >= n) & (lims[1] >= n)
    pl.when(full)(lambda: run(False))
    pl.when(jnp.logical_not(full))(lambda: run(True))


def cross_fwd(pos, group, q, kv_a, kv_b, at, pages, after=()):
    rows, w = q[0].shape[1:]
    return call(
        functools.partial(cross_fwd_kernel, q[1]),
        (pages,),
        [paged(q), paged((kv_a, at)), paged((kv_b, at))],
        [out_paged((pages, w + STATS, rows), BF)],
        scalars=(pos, group),
        us=1.6 * pages,
        after=after,
    )[0]


def cross_bwd_kernel(at, pos, group, q, do, kv_a, kv_b, *refs):
    dq, dkv_a, dkv_b = refs[-3:]
    rows, w = q.shape[1:]
    n = kv_a.shape[1]
    lims = limits(pos, group[pl.program_id(0) + at], n)
    per = w // rows
    lines = w // HEAD_DIM // per
    stats = do[0, rows:, :].astype(F32)

    def line(first, head):
        at = [first + t * lines + head // per for t in range(3)]
        c = slice(head % per * rows, (head % per + 1) * rows)
        return sum(stats[a : a + 1, c] for a in at)

    def both(first, t):
        return jnp.concatenate([line(first, 2 * t), line(first, 2 * t + 1)], axis=1)

    def run(masked):
        for t in range(w // PAIR):
            c = slice(t * PAIR, (t + 1) * PAIR)
            cv = slice(w + t * PAIR, w + (t + 1) * PAIR)
            qm = pair_rows(q[0, :, c])
            gm = pair_rows(do[0, :rows, c])
            ls, dl = both(0, t), both(3 * lines, t)
            acc = None
            for j, (kv, dkv) in enumerate(((kv_a, dkv_a), (kv_b, dkv_b))):
                k = kv[0, :, c]
                s = nt(k, qm)
                if masked:
                    pos = lax.broadcasted_iota(jnp.int32, s.shape, 0)
                    s = jnp.where(pos < lims[j], s, MASKED)
                p = jnp.exp(s - ls)
                ds = (p * (nt(kv[0, :, cv], gm) - dl)).astype(BF)
                dkv[0, :, c] = nn(ds, qm).astype(BF)
                dkv[0, :, cv] = nn(p.astype(BF), gm).astype(BF)
                part = tn(k, ds)
                acc = part if acc is None else acc + part
            dq[0, t * PAIR : t * PAIR + HEAD_DIM, :] = (acc[:HEAD_DIM, :rows] * SCALE).astype(BF)
            dq[0, t * PAIR + HEAD_DIM : (t + 1) * PAIR, :] = (
                acc[HEAD_DIM:, rows:] * SCALE
            ).astype(BF)

    full = (lims[0] >= n) & (lims[1] >= n)
    pl.when(full)(lambda: run(False))
    pl.when(jnp.logical_not(full))(lambda: run(True))


def cross_bwd(pos, group, q, do, kv_a, kv_b, at, prev=None, after=()):
    pages, _, w = do.shape
    rows = q[0].shape[1]
    n = kv_a.shape[1]
    ins = [paged(a) for a in (q, do, (kv_a, at), (kv_b, at))]
    if prev is not None:
        ins += [kept(p) for p in prev]

    def out(v):
        return (v.shape, BF, (1,) + v.shape[1:], lambda i, *_: (i + at, 0, 0))

    return call(
        functools.partial(cross_bwd_kernel, q[1]),
        (pages,),
        ins,
        [out_paged((pages, w, rows), BF), out(kv_a), out(kv_b)],
        scalars=(pos, group),
        us=2.4 * pages,
        after=after,
        aliases={} if prev is None else {6: 1, 7: 2},
    )


def enc_back_kernel(head, dkv, enc, w, prev, keep, send, dw):
    low = head[0] == 0
    part = keep.shape[-1]

    @pl.when(pl.program_id(0) == 0)
    def _():
        dw[...] = prev[...]

    for j in range(dkv.shape[0]):
        term = nt(dkv[j], w[...])
        lo, hi = term[:, :part], term[:, part:]
        keep[j] = jnp.where(low, lo, hi).astype(BF)
        send[j] = jnp.where(low, hi, lo).astype(BF)
        dw[...] += tn(enc[j], dkv[j])


def enc_back(head, dkv, enc, w, prev, k, after=()):
    slots, n, w2 = dkv.shape
    d = w.shape[0]
    part = d // 2
    return call(
        enc_back_kernel,
        (slots // k,),
        [paged(dkv, k), paged(enc, k), whole(w), whole(prev)],
        [
            out_paged((slots, n, part), BF, k), out_paged((slots, n, part), BF, k),
            out_whole((d, w2), F32),
        ],
        scalars=(head,),
        us=1.7 * slots,
        after=after,
    )


def add_pages_kernel(a, b, out):
    out[...] = (a[...].astype(F32) + b[...].astype(F32)).astype(BF)


def add_pages(at, pages, a, b, k, after=()):
    return call(
        add_pages_kernel,
        (pages // k,),
        [paged((a, at), k), paged((b, at), k)],
        [out_paged((pages,) + a.shape[1:], BF, k)],
        us=0.7 * pages,
        after=after,
    )[0]


def swap(x, axis, mask, size):
    return lax.ppermute(x, axis, [(i, i ^ mask) for i in range(size)])


def pick(bit, a, b):
    return jnp.where(bit == 0, b, a), jnp.where(bit == 0, a, b)


def rows_of(refs):
    return jnp.concatenate([r[...] for r in refs], axis=0) if len(refs) > 1 else refs[0][...]


def grads_wide_kernel(nc, bits, *refs):
    act, n3, du = (refs[j * nc : (j + 1) * nc] for j in range(3))
    cot, send_a, keep_a, send_b, keep_b = refs[3 * nc :]
    i = pl.program_id(0)
    for lo, out in ((0, send_a), (2, keep_a)):

        @pl.when((i >= lo) & (i < lo + 2))
        def _():
            out[...] = tn(rows_of(act), cot[...]).astype(BF)

    for lo, out in ((4, send_b), (6, keep_b)):

        @pl.when((i >= lo) & (i < lo + 2))
        def _():
            out[...] = tn(rows_of(n3), rows_of(du)).astype(BF)


def flat_rows(v):
    return v.reshape(-1, v.shape[-1])


def grads_wide(bits, act, cot, n3, du, after=()):
    act, n3, du = ([flat_rows(v) for v in c] for c in (act, n3, du))
    cot = flat_rows(cot)
    rows, units, d = act[0].shape[0], act[0].shape[1], cot.shape[1]
    blk = units // 4

    def quarter_a(i, t):
        j = jnp.minimum(i, 3)
        side = jnp.where(j < 2, 1 - t[2], t[2])
        return (0, 2 * side + j % 2)

    def side_b(i, t):
        return (0, jnp.where(jnp.maximum(i, 4) < 6, 1 - t[3], t[3]))

    def out(lo):
        return ((2 * blk, d), BF, (blk, d), lambda i, t: (jnp.clip(i - lo, 0, 1), 0))

    return call(
        functools.partial(grads_wide_kernel, len(act)),
        (8,),
        [(v, (rows, blk), quarter_a) for v in act]
        + [(v, (rows, d // 2), lambda i, t: (0, jnp.maximum(i, 4) % 2)) for v in n3]
        + [(v, (rows, units // 2), side_b) for v in du]
        + [whole(cot)],
        [out(0), out(2), out(4), out(6)],
        scalars=(bits,),
        us=10,
        after=after,
    )


def stacked(v):
    c = v.shape[1] // 2
    return jnp.concatenate([v[:, :c], v[:, c:]], axis=0)


def grads_self_kernel(nc, bits, n, o, *refs):
    dq, dk, dv, g = (rows_of(refs[j * nc : (j + 1) * nc]) for j in range(4))
    send_a, keep_a, send_b, keep_b = refs[-4:]
    turned = jnp.transpose(n[...])
    send_a[...], keep_a[...] = pick(bits[2], nn(turned, dq).astype(BF), nn(turned, dk).astype(BF))
    ot = stacked(tn(o[...], g).astype(BF))
    send_b[...], keep_b[...] = pick(bits[3], nn(turned, dv).astype(BF), ot)


def grads_cross_kernel(nc, bits, n, dw, *refs):
    dq, o, g = (rows_of(refs[j * nc : (j + 1) * nc]) for j in range(3))
    send_a, keep_a, send_b, keep_b = refs[-4:]
    w = dq.shape[1]
    send_a[...], keep_a[...] = pick(bits[2], tn(n[...], dq).astype(BF), dw[:, :w].astype(BF))
    ot = stacked(tn(o, g).astype(BF))
    send_b[...], keep_b[...] = pick(bits[3], dw[:, w:].astype(BF), ot)


def grads_tall(kernel, bits, arrays, chunked, d, w, us, after=()):
    flat = [flat_rows(v) for v in arrays] + [flat_rows(v) for c in chunked for v in c]
    return call(
        functools.partial(kernel, len(chunked[0])),
        (1,),
        [whole(v) for v in flat],
        [out_whole((d, w), BF)] * 4,
        scalars=(bits,),
        us=us,
        after=after,
    )


def sum_one_kernel(bits, keep_a, got_a, keep_b, got_b, send_a, next_a, send_b, next_b):
    blk = send_a.shape[0]
    for keep, got, send, nxt, bit in (
        (keep_a, got_a, send_a, next_a, bits[3]), (keep_b, got_b, send_b, next_b, bits[2])
    ):
        lo = keep[:blk].astype(F32) + got[:blk].astype(F32)
        hi = keep[blk:].astype(F32) + got[blk:].astype(F32)
        s, k = pick(bit, lo, hi)
        send[...] = s.astype(BF)
        nxt[...] = k.astype(BF)


def sum_two_kernel(keep_a, got_a, keep_b, got_b, out):
    nz, part = out.shape[0], out.shape[1] // 2
    sides = ((0, keep_a, got_a), (part, keep_b, got_b))
    for first, keep, got in sides:
        total = keep[...].astype(F32) + got[...].astype(F32)
        for z in range(nz):
            out[z, first : first + part] = total[z * part : (z + 1) * part].astype(BF)


def sum_three_kernel(got, out):
    nz = got.shape[0]
    total = sum(got[z].astype(F32) for z in range(nz)).astype(BF)
    for z in range(nz):
        out[z] = total


def join_kernel(got, out_a, out_b):
    nz, part = got.shape[0], got.shape[1] // 2
    for first, out in ((0, out_a), (part, out_b)):
        out[...] = jnp.concatenate(
            [got[z, first : first + part].astype(F32) for z in range(nz)], axis=0
        ).astype(BF)


def reduce_bucket(parts, bits, nz):
    send_a, keep_a, send_b, keep_b = parts
    blk, c = send_a.shape[0] // 2, send_a.shape[1]
    piece = (nz, 2 * blk // nz, c)
    fast = c / 384

    def x(v):
        return swap(v, "dp", 1, 4)

    def y(v):
        return swap(v, "dp", 2, 4)

    def over_seq(v):
        return lax.all_to_all(v, "seq", 0, 0, tiled=True)

    got_a, got_b = x(send_a), y(send_b)
    yield
    send_a, keep_a, send_b, keep_b = call(
        sum_one_kernel, (1,), [whole(v) for v in (keep_a, got_a, keep_b, got_b)],
        [out_whole((blk, c), BF)] * 4, scalars=(bits,), us=2 * fast,
    )
    got_a, got_b = y(send_a), x(send_b)
    yield
    (out,) = call(
        sum_two_kernel, (1,), [whole(v) for v in (keep_a, got_a, keep_b, got_b)],
        [out_whole(piece, BF)], us=1.5 * fast,
    )
    got = over_seq(out)
    yield
    (out,) = call(sum_three_kernel, (1,), [whole(got)], [out_whole(piece, BF)], us=1.5)
    got = over_seq(out)
    yield
    a0, b0 = call(join_kernel, (1,), [whole(got)], [out_whole((blk, c), BF)] * 2, us=1.5 * fast)
    a1, b1 = y(a0), x(b0)
    a2, b2 = x(a0), y(b0)
    yield [a0, a1, a2, x(a1), b0, b1, b2, y(b1)]


def final_kernel(outs, pos, *refs):
    pieces, results = refs[:8], refs[8:]
    t = pl.program_id(0)
    for half, (hi, lo) in enumerate(((pos[2], pos[3]), (pos[3], pos[2]))):
        rel = (t // 2 + hi) % 2 * 2 + (t % 2 + lo) % 2
        for j in range(4):
            for r, (at, first, count) in zip(results, outs):
                if at != half:
                    continue

                @pl.when((rel == j) & (t >= first) & (t < first + count))
                def _():
                    r[...] = pieces[4 * half + j][...].astype(F32)


def final(pieces, pos, outs, us, after=()):
    blk, c = pieces[0].shape

    def index(first, count, where):
        return lambda t, *_: where(jnp.clip(t - first, 0, count - 1))

    return call(
        functools.partial(final_kernel, [(o[1], o[2], o[3]) for o in outs]),
        (4,),
        [whole(p) for p in pieces],
        [(o[0], F32, (blk, c), index(o[2], o[3], o[4])) for o in outs],
        scalars=(pos,),
        us=us,
        after=after,
    )


def add_kernel(a, b, out):
    out[...] = a[...] + b[...]


def add_small(a, b):
    return call(add_kernel, (1,), [whole(a), whole(b)], [out_whole(a.shape, F32)], us=1)[0]


def place_kernel(pos, a, b, out):
    out[...] = (a[...].astype(F32) + b[...].astype(F32)).astype(BF)


def keep_kernel(pos, a, prev, out):
    out[...] = a[...]


def place_sum(pos, a, b, pages, k, where):
    n, c = a.shape[1:]
    return call(
        place_kernel,
        (a.shape[0] // k,),
        [paged(a, k), paged(b, k)],
        [((pages, n, c), BF, (k, n, c), lambda i, p: (where(i, p), 0, 0))],
        scalars=(pos,),
        us=1.2 * a.shape[0] // k,
    )[0]


def place_more(pos, a, so_far, k, where):
    n, c = a.shape[1:]
    return call(
        keep_kernel,
        (a.shape[0] // k,),
        [paged(a, k), kept(so_far)],
        [(so_far.shape, BF, (k, n, c), lambda i, p: (where(i, p), 0, 0))],
        scalars=(pos,),
        us=1.5 * a.shape[0] // k,
        aliases={2: 0},
    )[0]


def per_device(
    sizes,
    dec_input,
    enc_states,
    page_group,
    target_mask,
    rel_buckets,
    self_gain,
    cross_gain,
    ffn_gain,
    self_q,
    self_k,
    self_v,
    self_o,
    rel_table,
    cross_q_w,
    cross_k,
    cross_v,
    cross_o,
    ff_in,
    ff_out,
    cotangent,
):
    n_seq = sizes["seq"]
    pages, half, d = dec_input.shape
    n = enc_states.shape[1]
    w = self_q.shape[1]
    nb = n_seq // 2
    slots = nb * pages
    k = 3
    chunks = pages // k
    ORDER.clear()
    s = lax.axis_index("seq")
    h = lax.axis_index("head")
    dp = lax.axis_index("dp")
    block, par = s // 2, s % 2
    pos = jnp.stack(
        [v.astype(jnp.int32) for v in (h, s, dp % 2, dp // 2, dp, block, par)]
    )
    head = bits = pos

    def arrived(late, c):
        return lambda i, p: (
            (i // k + late * (nb // 2) + p[0] * (nb // 2) + nb - p[5]) % nb * pages + c * k + i % k
        )

    def out_group(first, other):
        def where(i, p):
            kk, c = (i + first) // chunks, (i + first) % chunks
            side = 1 - p[6] if other else p[6]
            return ((p[5] + kk) % nb * 2 + side) * chunks + c

        return where

    def head_swap(x):
        return swap(x, "head", 1, 2)

    def rolled(x, step):
        perm = [(2 * b + r, 2 * ((b - step) % nb) + r) for b in range(nb) for r in range(2)]
        return lax.ppermute(x, "seq", perm) if step % nb else x

    def owners(x):
        return [rolled(x, step) for step in range(nb)]

    others = list(range(1, nb))
    both = range(chunks)

    x_other = head_swap(dec_input)
    enc_t = jnp.transpose(enc_states, (1, 0, 2))

    def some_pages(at):
        return jnp.transpose(lax.dynamic_slice_in_dim(enc_t, at, pages, 1), (1, 0, 2))

    away = [some_pages(((h * (nb // 2) + i) * 2 + 1 - par) * pages) for i in range(nb // 2)]
    away = [
        jnp.concatenate([v[c * k : (c + 1) * k] for v in away], axis=0) for c in both
    ]
    enc_in = [swap(v, "seq", 1, n_seq) for v in away]
    cot_other = head_swap(cotangent)
    cot = jnp.concatenate(
        [jnp.where(h == 0, cotangent, cot_other), jnp.where(h == 0, cot_other, cotangent)], axis=1
    )
    page_groups = owners(page_group)
    lens = jnp.sum(target_mask, axis=1).astype(jnp.int32)
    table = jnp.pad(rel_table.T, ((0, 8 - rel_table.shape[1]), (0, 128 - rel_table.shape[0])))
    gains = jnp.stack([self_gain, cross_gain, ffn_gain])
    w_kv = jnp.concatenate([cross_k, cross_v], axis=1)

    xf, n1, qkv, o1, lse1, a_part = self_fwd(
        head, lens, dec_input, x_other, gains, self_q, self_k, self_v, self_o, rel_buckets, table,
        after=(*away, *page_groups[1:], cot_other),
    )
    a_other = head_swap(a_part)
    h1, n2, q2, zero = cross_q(xf, a_part, a_other, gains, cross_q_w, k)
    qs = owners(q2)
    direct = gate(enc_in[0])
    arriving = [[direct, head_swap(direct)]]
    enc_own = jnp.concatenate(
        [some_pages((((block + i) % nb) * 2 + par) * pages + zero[0, 0]) for i in range(nb)], axis=0
    )
    (kv_a,) = kv_project(pos, enc_own, w_kv, slots, k, lambda i, p: i)
    os = [[None] * chunks for _ in range(nb)]
    rec = None

    def attend(j, c):
        o = cross_fwd(
            pos, page_groups[j], (qs[j], c * k), kv_a, kv_b, j * pages + c * k, k
        )
        os[j][c] = rolled(o, -j)

    for c in both:
        if c:
            direct = gate(enc_in[c])
            arriving.append([direct, head_swap(direct)])
        for late, part in enumerate(arriving[c]):
            rec = kv_project(
                pos, part, w_kv, slots, 1, arrived(late, c), copied=True, prev=rec
            )
        kv_b, enc_rec = rec
        if c == chunks - 1:
            for e in range(max(c - 1, 0), chunks):
                for j in others:
                    attend(j, e)
        elif c:
            for j in others:
                attend(j, c - 1)
        attend(0, c)

    o2, o2t, lse2, c_part, c_other = ([None] * chunks for _ in range(5))
    h2, n3, act, du, dn3, dn3_other = ([None] * chunks for _ in range(6))
    dh2, dcr, gain3, dos = ([None] * chunks for _ in range(4))
    dqs = [[None] * chunks for _ in range(nb)]
    dkv = None

    def mix(c):
        o2[c], o2t[c], lse2[c], c_part[c] = combine(
            [v[c] for v in os], cross_o, k
        )
        c_other[c] = head_swap(c_part[c])

    def feed(c):
        h2[c], n3[c], act[c], du[c], dn3[c] = ffn(
            c * k, h1, c_part[c], c_other[c], cot, gains, ff_in, ff_out, k
        )
        dn3_other[c] = head_swap(dn3[c])

    def turn(c):
        dh2[c], dcr[c], do2, gain3[c] = grad_two(
            c * k, head, h2[c], dn3[c], dn3_other[c], cot, gains, cross_o, o2t[c], lse2[c], k
        )
        dos[c] = owners(do2)

    def back(j, c):
        nonlocal dkv
        dqs[j][c], *dkv = cross_bwd(
            pos, page_groups[j], (qs[j], c * k), dos[c][j], kv_a, kv_b,
            j * pages + c * k, prev=dkv,
        )
        dqs[j][c] = rolled(dqs[j][c], -j)

    mix(0)
    feed(0)
    for c in both[1:]:
        mix(c)
        turn(c - 1)
        feed(c)
        if c == chunks - 1:
            grads_ffn = reduce_bucket(grads_wide(bits, act, cot, n3, du), bits, n_seq)
            next(grads_ffn)
            turn(c)
        back(0, c - 1)
    for c in both[:-1]:
        for j in others:
            back(j, c)
    for j in [0] + others:
        if j == nb - 1:
            next(grads_ffn)
        back(j, chunks - 1)

    keep_b, send_b, dw = enc_back(
        head, dkv[1], enc_rec, w_kv, jnp.zeros((d, 2 * w), F32), k
    )
    send_b = head_swap(send_b)
    dq2, dn2, dn2_other = ([None] * chunks for _ in range(3))
    for c in both:
        dq2[c], dn2[c] = grad_q([v[c] for v in dqs], cross_q_w, k)
        dn2_other[c] = head_swap(dn2[c])
        if c == chunks - 1:
            next(grads_ffn)
    quarter = slots // 4
    spans = [(0, 2 * quarter), (2 * quarter, quarter), (3 * quarter, quarter)]
    enc_away = []

    def send_away():
        at, count = spans[len(enc_away)]
        enc_away.append(
            swap(add_pages(at, count, keep_b, send_b, k), "seq", 1, n_seq)
        )

    keep_a, send_a, dw = enc_back(head, dkv[0], enc_own, w_kv, dw, k, after=(send_b,))
    send_away()
    send_a = head_swap(send_a)
    grads_cross = reduce_bucket(
        grads_tall(grads_cross_kernel, bits, [n2, dw], [dq2, o2, dcr], d, w, 6), bits, n_seq
    )
    next(grads_cross)
    next(grads_ffn)
    backs = []
    dn1_other = []
    for c in both:
        backs.append(
            self_bwd(
                c * k, head, lens, h1, dn2[c], dn2_other[c], dh2[c], gains, self_q, self_k,
                self_v, self_o, rel_buckets, table, qkv, lse1,
            )
        )
        dn1_other.append(head_swap(backs[c][7]))
        if c == 0:
            next(grads_cross)
    dh1, dar, dq1, dk1, dv1, ds1, dn1, _, gain2 = zip(*backs)
    next(grads_cross)
    send_away()
    grads_self = reduce_bucket(
        grads_tall(
            grads_self_kernel, bits, [n1, o1], [dq1, dk1, dv1, dar], d, w, 7,
            after=(*dn1_other[:1], send_a),
        ),
        bits, n_seq,
    )
    next(grads_self)
    f_keep, f_send = branch_ffn(head, act, ff_out, after=dn1_other)
    f_other = head_swap(f_send)
    enc_out = place_sum(pos, keep_a, send_a, 2 * slots, k, out_group(0, False))
    enc_out = place_more(pos, enc_away[0], enc_out, k, out_group(0, True))
    next(grads_self)
    sums_ffn = next(grads_ffn)
    input_grad, gain1 = None, []
    for c in both:
        input_grad, g = last(
            c * k, dec_input, dn1[c], dn1_other[c], dh1[c], gains, prev=input_grad
        )
        gain1.append(g)
    next(grads_self)
    next(grads_cross)
    tables = [table_grad(ds1[c], rel_buckets, c * k) for c in both]
    enc_out = place_more(pos, enc_away[1], enc_out, k, out_group(spans[1][0] // k, True))
    next(grads_self)
    send_away()
    output, squares = None, []
    for c in both:
        output, sq = output_rows(
            c * k, head, lens, h2[c], f_keep, f_other, a_part, a_other, c_part[c],
            c_other[c], prev=output,
        )
        squares.append(sq)
    units = ff_in.shape[1]
    row, col = (lambda v: (v, 0)), (lambda v: (0, v))
    ff_out_grad, ff_in_grad = final(
        sums_ffn, pos,
        [((units, d), 0, 0, 4, row), ((d, units), 1, 0, 4, lambda v: (v % 2, v // 2))], 6,
    )
    sums_cross = next(grads_cross)
    sums_self = next(grads_self)

    squares = jnp.sum(jnp.concatenate(squares, axis=0)[:, :4], axis=-1)

    def line(v):
        return jnp.pad(v.reshape(1, -1), ((0, 0), (0, d - v.size)))

    small = jnp.concatenate(
        [jnp.sum(sum(g), axis=0)[None] for g in (gain1, gain2, gain3)] + [line(squares)], axis=0
    )
    small_other = head_swap(small)
    small = add_small(small, small_other)
    rms_stats = jnp.sqrt(small[3, : pages * 4].reshape(pages, 4) / (lens.astype(F32) * d)[:, None])
    table_part = sum(tables)
    small = jnp.concatenate([small[:3], line(table_part)], axis=0)
    steps = [(axis, 1 << i) for axis in ("dp", "seq") for i in range(sizes[axis].bit_length() - 1)]
    four = [
        ((d, w), 0, 0, 2, row), ((d, w), 0, 2, 2, row), ((d, w), 1, 0, 2, row), ((w, d), 1, 2, 2, col)
    ]
    for step, (axis, mask) in enumerate(steps):
        other = swap(small, axis, mask, sizes[axis])
        if step == 1:
            enc_out = place_more(
                pos, enc_away[2], enc_out, k, out_group(spans[2][0] // k, True)
            )
        if step == 2:
            cq, ck, cv, co = final(sums_cross, pos, four, 5)
        small = add_small(small, other)
    table_sum = small[3, : table_part.size].reshape(table_part.shape)
    enc_grad = with_layout_constraint(
        jnp.transpose(enc_out, (1, 0, 2)).astype(F32), Layout((0, 1, 2))
    )
    enc_grad = jnp.transpose(enc_grad, (1, 0, 2))
    sq, sk, sv, so = final(sums_self, pos, four, 5)

    return (
        output, input_grad, enc_grad, small[0], small[1], small[2], sq, sk, sv, so, table_sum.T,
        cq, ck, cv, co, ff_in_grad, ff_out_grad, rms_stats,
    )


def solution(mesh):
    sizes = dict(mesh.shape)
    rows = P(("dp", "seq"), "head", None)
    cols, tall = P(None, "head"), P("head", None)
    placed = (
        rows, P("dp", "seq", None), P(("dp", "seq")), P(("dp", "seq"), None),
        P(("dp", "seq"), None, None), P(), P(), P(), cols, cols, cols, tall, cols, cols, cols, cols,
        tall, cols, tall, rows,
    )
    return jax.shard_map(
        functools.partial(per_device, sizes),
        mesh=mesh,
        in_specs=placed,
        out_specs=(
            rows, rows, P("dp", "seq", "head"), P(), P(), P(), cols, cols, cols, tall, cols, cols,
            cols, cols, tall, cols, tall, P(("dp", "seq"), None),
        ),
        check_vma=False,
    )
```
